32 devices in a mesh: grp: 2 (over core), tok: 8 (over z, y), head: 2 (over x).
Axes of the slice: x: 2, y: 2, z: 4, core: 2. Of those that a mesh axis runs over, the one named last changes fastest.
Arguments:
- hidden_in: bfloat16 [2, 1024, 2560], P('grp', 'tok', 'head'), may hold values from -6 to 6
- attn_gain: bfloat16 [2560], replicated, may hold values from 0.5 to 1.5
- w_query: bfloat16 [2560, 2560], P('grp', 'head'), may hold values from -0.125 to 0.125
- key_projection_weight: bfloat16 [2560, 512], P('grp', 'head'), may hold values from -0.25 to 0.25
- value_projection_weight: bfloat16 [2560, 512], P('grp', 'head'), may hold values from -0.125 to 0.125
- w_out: bfloat16 [2560, 2560], P('grp', 'head'), may hold values from -0.125 to 0.125
- prefix_keys: bfloat16 [2, 512, 4, 128], P('grp', 'tok', 'head'), may hold values from -91 to 91
- cached_prefix_values: bfloat16 [2, 512, 4, 128], P('grp', 'tok', 'head'), may hold values from -6 to 6
- request_lengths: int32 [2, 16], P('grp'), may hold values from 1 to 256, 1024 in all within a row
- moe_gain: bfloat16 [2560], replicated, may hold values from 0.5 to 1.5
- expert_ids: int32 [2, 1024, 6], P('grp', 'tok'), may hold values from 0 to 15, all different within a row; in each aligned block of 128 rows (0 to 127, 128 to 255, ..., all dimensions but the last counted through in order) at most 64 rows name the same one
- route_weights: float32 [2, 1024, 6], P('grp', 'tok'), may hold values from 0.05 to 0.3
- w_gate: bfloat16 [16, 2560, 1536], P(('grp', 'tok'), None, 'head'), may hold values from -0.125 to 0.125
- w_up: bfloat16 [16, 2560, 1536], P(('grp', 'tok'), None, 'head'), may hold values from -0.125 to 0.125
- w_down: bfloat16 [16, 1536, 2560], P(('grp', 'tok'), None, 'head'), may hold values from -0.15625 to 0.15625
Outputs:
- hidden_out: bfloat16 [2, 1024, 2560], P('grp', 'tok', 'head')
The draws below stay inside these ranges and needn't reach their ends.
Inputs may be any that keep to these rules, and one draw needn't show every extreme that they name: `expert_ids`: each token names 6 different experts. Among the tokens of one device (aligned blocks of 128 tokens of a group) no expert is named more than 64 times.
All inputs are finite; a program needn't handle non-finite values.
Results may differ from the reference program's by a relative error of at most 0.011.
Values may be sent and summed in bfloat16 or wider, within the bound.
No kernel may reach another device: no remote copies, remote signals or barrier semaphores. Data moves between devices by JAX's collectives and lax.ppermute only.
A program may use at most 64 MiB of HBM per device.

```python
import math
import jax
import jax.numpy as jnp
import numpy as np
from jax import lax

MODEL_DIMENSION = 2560
QUERY_HEADS = 20
KEY_VALUE_HEADS = 4
HEAD_SIZE = 128
FE = 1536
TOP = 6
TOK_DEV = 128
REQS = 16
REQUEST_GROUPS = 2
EXPERTS = 16
SUFFIX_LENGTH = 1024
PREFIX_LENGTH = 512
L_MAX = 256
CAP = 64
N_TOK = 8


def draw_prefix_keys(key, part):
    tensor_shape = (REQUEST_GROUPS, PREFIX_LENGTH, KEY_VALUE_HEADS, HEAD_SIZE)
    drawn = 2.0 * jax.random.truncated_normal(key, -6.0, 6.0, tensor_shape, jnp.float32)
    return drawn.astype(jnp.bfloat16)


def shard_levels(key, extent, shards, low, largest):
    gain = 1.0
    for axis_at, blocks in shards:
        draws = jax.random.uniform(jax.random.fold_in(jax.random.fold_in(key, 6), axis_at), (blocks,), jnp.float32, low / len(shards), largest / len(shards))
        gain = gain * jnp.repeat(jnp.exp(draws), extent[axis_at] // blocks).reshape((-1,) + (1,) * (len(extent) - 1 - axis_at))
    return gain


def split_up(number_of, total, limit, slope):
    loads = [(1 << 20) // math.isqrt(standing ** slope) + 1 for standing in range(2, number_of + 1)]
    rest, given = total - limit - (number_of - 1), [1] * (number_of - 1)
    while rest > 0:
        movable = [i for i in range(number_of - 1) if given[i] < limit]
        mass, remaining = sum([loads[i] for i in movable]), rest
        for i in movable:
            extra = min(limit - given[i], max(1, remaining * loads[i] // mass), rest)
            given[i] = given[i] + extra
            rest = rest - extra
    return np.array([limit] + given)


def ragged(stream_key, number_of, total, bound, skew):
    if number_of == 2:
        one = jax.random.randint(stream_key, (), max(1, total - bound), min(bound, total - 1) + 1)
        return jnp.stack([one, total - one])
    tallies = jnp.asarray(split_up(number_of, total, bound, skew), jnp.int32)
    couples = (number_of - 1) // 2
    donor, receiver = tallies[1:1 + 2 * couples:2], tallies[2:2 + 2 * couples:2]
    slack = jnp.minimum(donor - 1, bound - receiver)
    passed = jax.random.randint(jax.random.fold_in(stream_key, 1), (couples,), 0, 1 << 20) % (slack + 1)
    tallies = tallies.at[1:1 + 2 * couples:2].set(donor - passed).at[2:2 + 2 * couples:2].set(receiver + passed)
    return tallies[jax.random.permutation(jax.random.fold_in(stream_key, 2), number_of)]


def assign_block(own_key, own, number, rows, number_of, top, limit, slope):
    ranking = jax.random.permutation(own_key, number_of)
    crowded, common = portions_of(number_of, rows * top, limit, slope, True), portions_of(number_of, rows * top, limit, slope, False)
    places = jnp.arange(number_of)

    def named(sizes, rotation):
        used = int((sizes > 0).sum())
        fixed = max(1, used // 4)
        moved = fixed + (places - fixed + rotation * (used - fixed)) % max(1, number_of - fixed)
        return jnp.zeros((number_of,), jnp.int32).at[ranking[jnp.where(places < fixed, places, moved)]].set(jnp.asarray(sizes, jnp.int32))

    sizes = jnp.where(number % 4 == 0, named(crowded, number // 4), named(common, number - number // 4 - 1))
    mixed = jax.random.permutation(jax.random.fold_in(own, 3), number_of)
    giver, receiver = mixed[0:number_of // 2 * 2:2], mixed[1:number_of // 2 * 2:2]
    room = jnp.minimum(sizes[giver] - 1, limit - sizes[receiver]) // 2
    room = jnp.where((giver == ranking[0]) | (receiver == ranking[0]) | (sizes[receiver] == 0), 0, jnp.maximum(room, 0))
    moved = jax.random.randint(jax.random.fold_in(own, 4), (number_of // 2,), 0, 1 << 20) % (room + 1)
    sizes = sizes.at[giver].add(-moved).at[receiver].add(moved)
    members = jnp.searchsorted(jnp.cumsum(sizes), jnp.arange(rows * top), side="right").astype(jnp.int32)
    grid = members.reshape(top, rows).T
    grid = grid[jax.random.permutation(jax.random.fold_in(own, 1), rows)]
    rotation = jax.random.randint(jax.random.fold_in(own, 2), (rows, 1), 0, top)
    return jnp.take_along_axis(grid, (jnp.arange(top)[None, :] + rotation) % top, axis=1)


def portions_of(amount, total, reach, lean, full):
    portions = [(1 << 20) // math.isqrt(grade ** lean) + 1 for grade in range(1, amount + 1)]
    largest = reach if full else min(reach, max(-(-total // amount), total * portions[0] // sum(portions)))
    least = 1 if total - largest >= amount - 1 else 0
    counts, rest = [largest] + [least] * (amount - 1), total - largest - least * (amount - 1)
    while rest > 0:
        movable = [i for i in range(1, amount) if counts[i] < largest] or [i for i in range(1, amount) if counts[i] < reach]
        pool, left = sum([portions[i] for i in movable]), rest
        for i in movable:
            extra = min(reach - counts[i], max(1, left * portions[i] // pool), rest)
            counts[i] = counts[i] + extra
            rest = rest - extra
    return np.array(counts)


def centred(stream_key, extent, width, reach, shards=(), kind=jnp.bfloat16):
    values = width * jax.random.normal(stream_key, extent, jnp.float32)
    if shards:
        values = values * shard_levels(stream_key, extent, shards, -0.22, 0.18)
    return jnp.clip(values, -reach, reach).astype(kind)


def setup_inputs(seed: int = 0) -> dict:
    splits = jax.random.split(jax.random.key(seed), 16)
    hidden_in = centred(splits[0], (REQUEST_GROUPS, SUFFIX_LENGTH, MODEL_DIMENSION), 1.0, 6.0, ((0, 2), (1, 8), (2, 2)))
    attn_gain = jnp.clip(1.0 + 0.1 * jax.random.normal(splits[1], (MODEL_DIMENSION,), jnp.float32), 0.5, 1.5).astype(jnp.bfloat16)
    w_query = centred(splits[2], (MODEL_DIMENSION, QUERY_HEADS * HEAD_SIZE), MODEL_DIMENSION ** -0.5, 0.125, ((0, 2), (1, 2)))
    key_projection_weight = centred(splits[3], (MODEL_DIMENSION, KEY_VALUE_HEADS * HEAD_SIZE), (MODEL_DIMENSION // 4) ** -0.5, 0.25, ((0, 2), (1, 2)))
    value_projection_weight = centred(splits[4], (MODEL_DIMENSION, KEY_VALUE_HEADS * HEAD_SIZE), MODEL_DIMENSION ** -0.5, 0.125, ((0, 2), (1, 2)))
    w_out = centred(splits[5], (MODEL_DIMENSION, QUERY_HEADS * HEAD_SIZE), (QUERY_HEADS * HEAD_SIZE) ** -0.5, 0.125, ((0, 2), (1, 2)))
    prefix_keys = draw_prefix_keys(jax.random.fold_in(splits[15], 71), 0)
    cached_prefix_values = centred(splits[7], (REQUEST_GROUPS, PREFIX_LENGTH, KEY_VALUE_HEADS, HEAD_SIZE), 1.0, 6.0, ((0, 2), (1, 8), (2, 2)))
    request_lengths = jax.vmap(lambda own: ragged(own, REQS, SUFFIX_LENGTH, L_MAX, 2))(jax.random.split(splits[8], REQUEST_GROUPS)).reshape((REQUEST_GROUPS, REQS)).astype(jnp.int32)
    moe_gain = jnp.clip(1.0 + 0.1 * jax.random.normal(splits[9], (MODEL_DIMENSION,), jnp.float32), 0.5, 1.5).astype(jnp.bfloat16)
    expert_ids_keys = jax.random.split(jax.random.fold_in(splits[10], 1), REQUEST_GROUPS * SUFFIX_LENGTH // TOK_DEV)
    expert_ids_turns = jax.random.permutation(jax.random.fold_in(splits[10], 3), REQUEST_GROUPS * SUFFIX_LENGTH // TOK_DEV)
    expert_ids = jax.vmap(lambda own, number: assign_block(jax.random.fold_in(splits[10], 2), own, number, TOK_DEV, EXPERTS, TOP, CAP, 2))(expert_ids_keys, expert_ids_turns).reshape((REQUEST_GROUPS, SUFFIX_LENGTH, TOP))
    route_weights = jnp.clip(0.05 + 0.25 * jax.random.uniform(splits[11], (REQUEST_GROUPS, SUFFIX_LENGTH, TOP), jnp.float32) ** shard_levels(splits[11], (REQUEST_GROUPS, SUFFIX_LENGTH, TOP), ((0, 2), (1, 8)), -0.2, 0.2), 0.05, 0.3)
    w_gate = centred(splits[12], (EXPERTS, MODEL_DIMENSION, FE), MODEL_DIMENSION ** -0.5, 0.125, ((0, 16), (2, 2)))
    w_up = centred(splits[13], (EXPERTS, MODEL_DIMENSION, FE), MODEL_DIMENSION ** -0.5, 0.125, ((0, 16), (2, 2)))
    w_down = centred(splits[14], (EXPERTS, FE, MODEL_DIMENSION), FE ** -0.5, 0.15625, ((0, 16), (2, 2)))
    return {"hidden_in": hidden_in, "attn_gain": attn_gain, "w_query": w_query, "key_projection_weight": key_projection_weight, "value_projection_weight": value_projection_weight, "w_out": w_out, "prefix_keys": prefix_keys, "cached_prefix_values": cached_prefix_values, "request_lengths": request_lengths, "moe_gain": moe_gain, "expert_ids": expert_ids, "route_weights": route_weights, "w_gate": w_gate, "w_up": w_up, "w_down": w_down}


ROPE_BASE = 500000.0
NORM_EPS = 1e-06
MASKED = -1e+30

def rms_norm(values_in, gain_vector):
    widened = values_in.astype(jnp.float32)
    mean_sq = lax.optimization_barrier(jnp.mean(widened * widened, axis=-1, keepdims=True))
    return (widened * lax.rsqrt(mean_sq + NORM_EPS) * gain_vector.astype(jnp.float32)).astype(jnp.bfloat16)

def apply_rotary(product, token_positions):
    half_dim = product.shape[-1] // 2
    frequency = jnp.exp(jnp.arange(half_dim, dtype=jnp.float32) * (-2.0 * math.log(ROPE_BASE) / product.shape[-1]))
    angles = token_positions.astype(jnp.float32)[:, None] * frequency[None, :]
    cosine = jnp.cos(angles)[:, None, :]
    sine_part = jnp.sin(angles)[:, None, :]
    first_half = product[..., :half_dim]
    second_half = product[..., half_dim:]
    turned = jnp.concatenate([first_half * cosine - second_half * sine_part, second_half * cosine + first_half * sine_part], axis=-1)
    return turned.astype(jnp.bfloat16)

def reference(hidden_in, attn_gain, w_query, key_projection_weight, value_projection_weight, w_out, prefix_keys, cached_prefix_values, request_lengths, moe_gain, expert_ids, route_weights, w_gate, w_up, w_down):
    scale = HEAD_SIZE ** (-0.5)
    group_length = QUERY_HEADS // KEY_VALUE_HEADS
    mids = []
    for grp_index in range(REQUEST_GROUPS):
        stream = hidden_in[grp_index]
        attention_input = rms_norm(stream, attn_gain)
        lengths = request_lengths[grp_index]
        request_ends = jnp.cumsum(lengths).astype(jnp.int32)
        starts = (request_ends - lengths).astype(jnp.int32)
        token_index = jnp.arange(SUFFIX_LENGTH, dtype=jnp.int32)
        own_start = lax.optimization_barrier(jnp.max(jnp.where(starts[None, :] <= token_index[:, None], starts[None, :], 0), axis=1)).astype(jnp.int32)
        token_positions = (PREFIX_LENGTH + token_index - own_start).astype(jnp.int32)
        query = apply_rotary(jnp.dot(attention_input, w_query, preferred_element_type=jnp.float32).reshape(SUFFIX_LENGTH, QUERY_HEADS, HEAD_SIZE), token_positions)
        request_suffix_keys = apply_rotary(jnp.dot(attention_input, key_projection_weight, preferred_element_type=jnp.float32).reshape(SUFFIX_LENGTH, KEY_VALUE_HEADS, HEAD_SIZE), token_positions)
        request_suffix_values = jnp.dot(attention_input, value_projection_weight, preferred_element_type=jnp.float32).astype(jnp.bfloat16).reshape(SUFFIX_LENGTH, KEY_VALUE_HEADS, HEAD_SIZE)
        visible = (token_index[None, :] >= own_start[:, None]) & (token_index[None, :] <= token_index[:, None])
        cache_keys = prefix_keys[grp_index]
        cache_values = cached_prefix_values[grp_index]

        def one_head(head_number):
            kv_index = head_number // group_length
            head_query = lax.dynamic_index_in_dim(query, head_number, axis=1, keepdims=False)
            pre_keys = lax.dynamic_index_in_dim(cache_keys, kv_index, axis=1, keepdims=False)
            pre_values = lax.dynamic_index_in_dim(cache_values, kv_index, axis=1, keepdims=False)
            suf_keys = lax.dynamic_index_in_dim(request_suffix_keys, kv_index, axis=1, keepdims=False)
            suf_values = lax.dynamic_index_in_dim(request_suffix_values, kv_index, axis=1, keepdims=False)
            score_pre = jnp.dot(head_query, pre_keys.T, preferred_element_type=jnp.float32) * scale
            score_suf = jnp.where(visible, jnp.dot(head_query, suf_keys.T, preferred_element_type=jnp.float32) * scale, MASKED)
            row_max = jnp.maximum(lax.optimization_barrier(jnp.max(score_pre, axis=1)), lax.optimization_barrier(jnp.max(score_suf, axis=1)))[:, None]
            prob_pre = jnp.exp(score_pre - row_max)
            prob_suf = jnp.where(visible, jnp.exp(score_suf - row_max), 0.0)
            denominator = lax.optimization_barrier(jnp.sum(prob_pre, axis=1)) + lax.optimization_barrier(jnp.sum(prob_suf, axis=1))
            numerator = jnp.dot(prob_pre.astype(jnp.bfloat16), pre_values, preferred_element_type=jnp.float32)
            numerator = numerator + jnp.dot(prob_suf.astype(jnp.bfloat16), suf_values, preferred_element_type=jnp.float32)
            return (numerator / denominator[:, None]).astype(jnp.bfloat16)
        heads_out = lax.map(one_head, jnp.arange(QUERY_HEADS, dtype=jnp.int32))
        attended = jnp.transpose(heads_out, (1, 0, 2)).reshape(SUFFIX_LENGTH, QUERY_HEADS * HEAD_SIZE)
        projected = jnp.dot(attended, w_out.T, preferred_element_type=jnp.float32)
        mids.append((stream.astype(jnp.float32) + projected).astype(jnp.bfloat16))
    mid = jnp.stack(mids)
    moe_in = rms_norm(mid, moe_gain)
    blocks = REQUEST_GROUPS * N_TOK
    per_block = TOK_DEV * TOP
    chosen = expert_ids.reshape(blocks, per_block).astype(jnp.int32)
    onehot = (chosen[:, :, None] == jnp.arange(EXPERTS, dtype=jnp.int32)[None, None, :]).astype(jnp.int32)
    running_count = jnp.cumsum(onehot, axis=1).astype(jnp.int32)
    slot_rank = (lax.optimization_barrier(jnp.sum(onehot * running_count, axis=2)) - 1).astype(jnp.int32)
    block_index = jnp.broadcast_to(jnp.arange(blocks, dtype=jnp.int32)[:, None], (blocks, per_block))
    token_of = (block_index * TOK_DEV + jnp.arange(per_block, dtype=jnp.int32)[None, :] // TOP).astype(jnp.int32)
    table = jnp.full((EXPERTS, blocks, CAP), blocks * TOK_DEV, jnp.int32).at[chosen, block_index, slot_rank].set(token_of)
    flat_in = moe_in.reshape(blocks * TOK_DEV, MODEL_DIMENSION)

    def one_expert(operands):
        rows_index, gate_matrix, up_matrix, down_matrix = operands
        flat_rows = jnp.take(flat_in, rows_index.reshape(-1), axis=0, mode='fill', fill_value=0)
        gate_act = jnp.dot(flat_rows, gate_matrix, preferred_element_type=jnp.float32)
        up_act = jnp.dot(flat_rows, up_matrix, preferred_element_type=jnp.float32)
        hidden = (jax.nn.silu(gate_act) * up_act).astype(jnp.bfloat16)
        return jnp.dot(hidden, down_matrix, preferred_element_type=jnp.float32).astype(jnp.bfloat16)
    expert_out = lax.map(one_expert, (table, w_gate, w_up, w_down))
    flat_out = expert_out.reshape(EXPERTS * blocks * CAP, MODEL_DIMENSION)
    pick_index = (chosen * (blocks * CAP) + block_index * CAP + slot_rank).astype(jnp.int32)

    def one_block(operands):
        pick_row, weight_row = operands
        picked = jnp.take(flat_out, pick_row, axis=0).astype(jnp.float32)
        return lax.optimization_barrier(jnp.sum((picked * weight_row[:, None]).reshape(TOK_DEV, TOP, MODEL_DIMENSION), axis=1))
    moe_out = lax.map(one_block, (pick_index, route_weights.reshape(blocks, per_block)))
    final = mid.reshape(blocks * TOK_DEV, MODEL_DIMENSION).astype(jnp.float32) + moe_out.reshape(blocks * TOK_DEV, MODEL_DIMENSION)
    return final.astype(jnp.bfloat16).reshape(REQUEST_GROUPS, SUFFIX_LENGTH, MODEL_DIMENSION)
```

```python
import math

import jax
import jax.numpy as jnp
from jax import lax
from jax.sharding import PartitionSpec as P

ROPE_BASE = 500000.0
NORM_EPS = 1e-06
MASKED = -1e30


def shifted(block, axis, distance):
    devices = range(lax.axis_size(axis))
    route = [(i - distance, i) for i in devices if i - distance in devices]
    return lax.ppermute(block, axis, route)


def rms_norm(values_in, gain_vector):
    widened = values_in.astype(jnp.float32)
    mean_sq = jnp.mean(widened * widened, axis=-1, keepdims=True)
    return (widened * lax.rsqrt(mean_sq + NORM_EPS) * gain_vector.astype(jnp.float32)).astype(
        jnp.bfloat16
    )


def apply_rotary(product, token_positions):
    half_dim = product.shape[-1] // 2
    frequency = jnp.exp(
        jnp.arange(half_dim, dtype=jnp.float32) * (-2.0 * math.log(ROPE_BASE) / product.shape[-1])
    )
    angles = token_positions.astype(jnp.float32)[:, None] * frequency[None, :]
    cosine = jnp.cos(angles)[:, None, :]
    sine_part = jnp.sin(angles)[:, None, :]
    first_half = product[..., :half_dim]
    second_half = product[..., half_dim:]
    turned = jnp.concatenate(
        [
            first_half * cosine - second_half * sine_part,
            second_half * cosine + first_half * sine_part,
        ],
        axis=-1,
    )
    return turned.astype(jnp.bfloat16)


def attend(running, queries, keys_block, values_block, visible):
    row_max, row_total, summed = running
    scores = jnp.einsum(
        "tcrd,kcd->ctrk", queries, keys_block, preferred_element_type=jnp.float32
    ) * queries.shape[-1] ** (-0.5)
    if visible is not None:
        scores = jnp.where(visible[None, :, None, :], scores, MASKED)
    new_max = jnp.maximum(row_max, jnp.max(scores, axis=-1))
    weights = jnp.exp(scores - new_max[..., None])
    if visible is not None:
        weights = jnp.where(visible[None, :, None, :], weights, 0.0)
    factor = jnp.exp(row_max - new_max)
    row_total = row_total * factor + jnp.sum(weights, axis=-1)
    summed = summed * factor[..., None] + jnp.einsum(
        "ctrk,kcd->ctrd",
        weights.astype(jnp.bfloat16),
        values_block,
        preferred_element_type=jnp.float32,
    )
    return (new_max, row_total, summed)


def turned_by(block, axis, distance):
    devices = lax.axis_size(axis)
    return lax.ppermute(block, axis, [(i, (i + distance) % devices) for i in range(devices)])


def others_over(block, axis):
    return [block] + [turned_by(block, axis, d) for d in range(1, lax.axis_size(axis))]


def split_product(activations, blocks, axis):
    count = len(blocks)
    rank = lax.axis_index(axis)
    rows = blocks[0].shape[0]
    total = None
    for distance, block in enumerate(blocks):
        part = lax.dynamic_slice_in_dim(
            activations, ((rank - distance) % count) * rows, rows, 1
        )
        product = jnp.dot(part, block, preferred_element_type=jnp.float32)
        total = product if total is None else total + product
    return total


def on_device(
    hidden_in,
    attn_gain,
    w_query,
    key_projection_weight,
    value_projection_weight,
    w_out,
    prefix_keys,
    cached_prefix_values,
    request_lengths,
    moe_gain,
    expert_ids,
    route_weights,
    w_gate,
    w_up,
    w_down,
):
    tok_count = lax.axis_size("tok")
    grp_count = lax.axis_size("grp")
    head_count = lax.axis_size("head")
    tok_rank = lax.axis_index("tok")
    grp_rank = lax.axis_index("grp")
    head_rank = lax.axis_index("head")
    tok_dev = hidden_in.shape[1]
    model_width = attn_gain.shape[0]
    head_dim = prefix_keys.shape[3]
    kv_local = prefix_keys.shape[2]
    kv_width = kv_local * head_dim
    group_length = w_query.shape[1] // kv_width
    prefix_total = prefix_keys.shape[1] * tok_count
    share_width = model_width // head_count
    experts = grp_count * tok_count
    top_count = expert_ids.shape[2]
    capacity = 4 * tok_dev * top_count // (3 * experts)

    quarter = hidden_in[0]
    features = lax.all_gather(quarter, "head", axis=1, tiled=True)
    query_blocks = others_over(w_query, "grp")
    key_blocks = others_over(key_projection_weight, "grp")
    value_blocks = others_over(value_projection_weight, "grp")
    full_out = lax.all_gather(w_out, "grp", axis=0, tiled=True)

    prefix = jnp.concatenate(
        [prefix_keys[0].reshape(-1, kv_width), cached_prefix_values[0].reshape(-1, kv_width)], axis=1
    )
    prefix = lax.all_gather(prefix, "tok", axis=0, tiled=True)

    ids = expert_ids[0]
    named = ids[None, :, :] == jnp.arange(experts, dtype=jnp.int32)[:, None, None]
    routing = jnp.concatenate(
        [
            jnp.sum(jnp.where(named, route_weights[0][None], 0.0), axis=2),
            jnp.sum(named.astype(jnp.float32), axis=2),
        ],
        axis=0,
    )
    routing = lax.all_gather(routing, "tok", axis=0, tiled=True)
    routing = routing.reshape(tok_count, 2, experts, tok_dev)

    gate_blocks = others_over(w_gate[0], "grp")
    up_blocks = others_over(w_up[0], "grp")
    down_blocks = others_over(w_down[0], "grp")

    attention_input = rms_norm(features, attn_gain)
    lengths = request_lengths[0]
    request_ends = jnp.cumsum(lengths)
    starts = request_ends - lengths
    token_index = tok_rank * tok_dev + jnp.arange(tok_dev, dtype=jnp.int32)
    own_start = jnp.max(
        jnp.where(starts[None, :] <= token_index[:, None], starts[None, :], 0), axis=1
    )
    token_positions = prefix_total + token_index - own_start
    key_product = split_product(attention_input, key_blocks, "grp")
    value_product = split_product(attention_input, value_blocks, "grp")
    query_product = split_product(attention_input, query_blocks, "grp")
    queries = apply_rotary(
        query_product.reshape(tok_dev, kv_local * group_length, head_dim), token_positions
    )
    queries = queries.reshape(tok_dev, kv_local, group_length, head_dim)
    request_suffix_keys = apply_rotary(
        key_product.reshape(tok_dev, kv_local, head_dim), token_positions
    )
    request_suffix_values = value_product.astype(jnp.bfloat16).reshape(tok_dev, kv_local, head_dim)
    running = (
        jnp.full((kv_local, tok_dev, group_length), MASKED, jnp.float32),
        jnp.zeros((kv_local, tok_dev, group_length), jnp.float32),
        jnp.zeros((kv_local, tok_dev, group_length, head_dim), jnp.float32),
    )
    running = attend(
        running,
        queries,
        prefix[:, :kv_width].reshape(prefix_total, kv_local, head_dim),
        prefix[:, kv_width:].reshape(prefix_total, kv_local, head_dim),
        None,
    )

    def visible_from(first_index, count):
        key_index = first_index + jnp.arange(count, dtype=jnp.int32)
        return (key_index[None, :] >= own_start[:, None]) & (
            key_index[None, :] <= token_index[:, None]
        )

    running = attend(
        running,
        queries,
        request_suffix_keys,
        request_suffix_values,
        visible_from(tok_rank * tok_dev, tok_dev),
    )
    longest = tok_dev * tok_count // 4
    reach_devices = (longest - 1 + tok_dev - 1) // tok_dev
    stacked = jnp.stack([request_suffix_keys, request_suffix_values])
    for distance in range(1, reach_devices + 1):
        arrived = shifted(stacked, "tok", distance)
        running = attend(
            running,
            queries,
            arrived[0],
            arrived[1],
            visible_from((tok_rank - distance) * tok_dev, tok_dev),
        )
    row_max, row_total, summed = running
    attended = (summed / row_total[..., None]).astype(jnp.bfloat16)
    attended = jnp.transpose(attended, (1, 0, 2, 3)).reshape(
        tok_dev, kv_local * group_length * head_dim
    )
    partial_value = lax.dot_general(
        attended, full_out, (((1,), (1,)), ((), ())), preferred_element_type=jnp.float32
    )
    mixed = lax.dynamic_slice_in_dim(partial_value, head_rank * share_width, share_width, 1)
    for distance in range(1, head_count):
        target = (head_rank + distance) % head_count
        leaving = lax.dynamic_slice_in_dim(partial_value, target * share_width, share_width, 1)
        mixed = mixed + turned_by(leaving.astype(jnp.bfloat16), "head", distance).astype(jnp.float32)
    mid_quarter = (quarter.astype(jnp.float32) + mixed).astype(jnp.bfloat16)
    mid_full = lax.all_gather(mid_quarter, "head", axis=1, tiled=True)
    moe_in = rms_norm(mid_full, moe_gain)
    gathered = lax.all_gather(moe_in, "tok", axis=0, tiled=True)
    gathered = gathered.reshape(tok_count, tok_dev, model_width)

    causal = (
        jnp.arange(tok_dev, dtype=jnp.int32)[:, None] <= jnp.arange(tok_dev, dtype=jnp.int32)[None, :]
    ).astype(jnp.bfloat16)
    slots = jnp.arange(capacity, dtype=jnp.int32)
    picks, hiddens, row_weights = [], [], []
    for distance in range(grp_count):
        expert = ((grp_rank - distance) % grp_count) * tok_count + tok_rank
        own = lax.dynamic_index_in_dim(routing, expert, axis=2, keepdims=False)
        weight, mask = own[:, 0], own[:, 1]
        place = jnp.dot(mask.astype(jnp.bfloat16), causal, preferred_element_type=jnp.float32)
        place = jnp.where(mask > 0.5, place.astype(jnp.int32) - 1, -1)
        pick = place[:, None, :] == slots[None, :, None]
        row_weights.append(jnp.sum(jnp.where(pick, weight[:, None, :], 0.0), axis=2))
        pick = pick.astype(jnp.bfloat16)
        picks.append(pick)
        rows = jnp.einsum("bct,btf->bcf", pick, gathered, preferred_element_type=jnp.float32)
        rows = rows.astype(jnp.bfloat16).reshape(tok_count * capacity, model_width)
        gate_act = jnp.dot(rows, gate_blocks[distance], preferred_element_type=jnp.float32)
        up_act = jnp.dot(rows, up_blocks[distance], preferred_element_type=jnp.float32)
        hidden = (jax.nn.silu(gate_act) * up_act).astype(jnp.bfloat16)
        hiddens.append(lax.all_gather(hidden, "head", axis=1, tiled=True))
    summed_out = None
    for distance in range(grp_count):
        result = jnp.dot(
            hiddens[distance], down_blocks[distance], preferred_element_type=jnp.float32
        )
        result = result.reshape(tok_count, capacity, share_width)
        result = (result * row_weights[distance][:, :, None]).astype(jnp.bfloat16)
        part = jnp.einsum("bct,bcf->btf", picks[distance], result, preferred_element_type=jnp.float32)
        summed_out = part if summed_out is None else summed_out + part
    summed_out = summed_out.astype(jnp.bfloat16).reshape(tok_count * tok_dev, share_width)
    weighted = lax.psum_scatter(summed_out, "tok", scatter_dimension=0, tiled=True)
    output = (mid_quarter.astype(jnp.float32) + weighted.astype(jnp.float32)).astype(jnp.bfloat16)
    return output[None]


def solution(mesh):
    return jax.shard_map(
        on_device,
        mesh=mesh,
        in_specs=(
            P("grp", "tok", "head"),
            P(),
            P("grp", "head"),
            P("grp", "head"),
            P("grp", "head"),
            P("grp", "head"),
            P("grp", "tok", "head", None),
            P("grp", "tok", "head", None),
            P("grp", None),
            P(),
            P("grp", "tok", None),
            P("grp", "tok", None),
            P(("grp", "tok"), None, "head"),
            P(("grp", "tok"), None, "head"),
            P(("grp", "tok"), None, "head"),
        ),
        out_specs=P("grp", "tok", "head"),
        check_vma=False,
    )
```

```python
import math

import jax
import jax.numpy as jnp
from jax import lax
from jax.sharding import PartitionSpec as P

ROPE_BASE = 500000.0
NORM_EPS = 1e-06
MASKED = -1e30


def shifted(block, axis, distance):
    devices = range(lax.axis_size(axis))
    route = [(i - distance, i) for i in devices if i - distance in devices]
    return lax.ppermute(block, axis, route)


def rms_norm(values_in, gain_vector):
    widened = values_in.astype(jnp.float32)
    mean_sq = jnp.mean(widened * widened, axis=-1, keepdims=True)
    return (widened * lax.rsqrt(mean_sq + NORM_EPS) * gain_vector.astype(jnp.float32)).astype(
        jnp.bfloat16
    )


def apply_rotary(product, token_positions):
    half_dim = product.shape[-1] // 2
    frequency = jnp.exp(
        jnp.arange(half_dim, dtype=jnp.float32) * (-2.0 * math.log(ROPE_BASE) / product.shape[-1])
    )
    angles = token_positions.astype(jnp.float32)[:, None] * frequency[None, :]
    cosine = jnp.cos(angles)[:, None, :]
    sine_part = jnp.sin(angles)[:, None, :]
    first_half = product[..., :half_dim]
    second_half = product[..., half_dim:]
    turned = jnp.concatenate(
        [
            first_half * cosine - second_half * sine_part,
            second_half * cosine + first_half * sine_part,
        ],
        axis=-1,
    )
    return turned.astype(jnp.bfloat16)


def attend(running, queries, keys_block, values_block, visible):
    row_max, row_total, summed = running
    scores = jnp.einsum(
        "tcrd,kcd->ctrk", queries, keys_block, preferred_element_type=jnp.float32
    ) * queries.shape[-1] ** (-0.5)
    if visible is not None:
        scores = jnp.where(visible[None, :, None, :], scores, MASKED)
    new_max = jnp.maximum(row_max, jnp.max(scores, axis=-1))
    weights = jnp.exp(scores - new_max[..., None])
    if visible is not None:
        weights = jnp.where(visible[None, :, None, :], weights, 0.0)
    factor = jnp.exp(row_max - new_max)
    row_total = row_total * factor + jnp.sum(weights, axis=-1)
    summed = summed * factor[..., None] + jnp.einsum(
        "ctrk,kcd->ctrd",
        weights.astype(jnp.bfloat16),
        values_block,
        preferred_element_type=jnp.float32,
    )
    return (new_max, row_total, summed)


def turned_by(block, axis, distance):
    devices = lax.axis_size(axis)
    return lax.ppermute(block, axis, [(i, (i + distance) % devices) for i in range(devices)])


def along_ring(block, distance):
    devices = lax.axis_size("tok")
    order = list(range(0, devices, 2)) + list(range(devices - 1 - devices % 2, 0, -2))
    route = [(order[i], order[(i + distance) % devices]) for i in range(devices)]
    return lax.ppermute(block, "tok", route)


def ring_gather(block):
    half = lax.axis_size("tok") // 2
    middle = block.shape[1] // 2
    blocks = {0: block}
    ahead = behind = block
    for step in range(1, half):
        ahead = along_ring(ahead, 1)
        behind = along_ring(behind, -1)
        blocks[step] = ahead
        blocks[-step] = behind
    blocks[half] = jnp.concatenate(
        [along_ring(ahead[:, :middle], 1), along_ring(behind[:, middle:], -1)], axis=1
    )
    return blocks


def ring_sum(parts):
    half = lax.axis_size("tok") // 2
    middle = parts[0].shape[1] // 2
    left = along_ring(parts[half][:, :middle].astype(jnp.bfloat16), -1).astype(jnp.float32)
    right = along_ring(parts[half][:, middle:].astype(jnp.bfloat16), 1).astype(jnp.float32)
    left = parts[half - 1] + jnp.pad(left, ((0, 0), (0, parts[0].shape[1] - middle)))
    right = parts[1 - half] + jnp.pad(right, ((0, 0), (middle, 0)))
    for step in range(half - 2, -1, -1):
        left = along_ring(left.astype(jnp.bfloat16), -1).astype(jnp.float32)
        right = along_ring(right.astype(jnp.bfloat16), 1).astype(jnp.float32)
        if step:
            left = left + parts[step]
            right = right + parts[-step]
    return parts[0] + left + right


def side_by_side(block, axis):
    count = lax.axis_size(axis)
    rank = lax.axis_index(axis)
    blocks = others_over(block, axis)
    columns = []
    for place in range(count):
        column = blocks[0]
        for distance in range(1, count):
            column = jnp.where((rank - place) % count == distance, blocks[distance], column)
        columns.append(column)
    return jnp.concatenate(columns, axis=1)


def three_pieces(values):
    pieces = []
    for _ in range(3):
        piece = lax.reduce_precision(values, 8, 7)
        pieces.append(piece.astype(jnp.bfloat16))
        values = values - piece
    return pieces


def others_over(block, axis):
    return [block] + [turned_by(block, axis, d) for d in range(1, lax.axis_size(axis))]


def split_product(activations, blocks, axis):
    count = len(blocks)
    rank = lax.axis_index(axis)
    rows = blocks[0].shape[0]
    total = None
    for distance, block in enumerate(blocks):
        part = lax.dynamic_slice_in_dim(
            activations, ((rank - distance) % count) * rows, rows, 1
        )
        product = jnp.dot(part, block, preferred_element_type=jnp.float32)
        total = product if total is None else total + product
    return total


def on_device(
    hidden_in,
    attn_gain,
    w_query,
    key_projection_weight,
    value_projection_weight,
    w_out,
    prefix_keys,
    cached_prefix_values,
    request_lengths,
    moe_gain,
    expert_ids,
    route_weights,
    w_gate,
    w_up,
    w_down,
):
    tok_count = lax.axis_size("tok")
    grp_count = lax.axis_size("grp")
    head_count = lax.axis_size("head")
    tok_rank = lax.axis_index("tok")
    grp_rank = lax.axis_index("grp")
    head_rank = lax.axis_index("head")
    tok_dev = hidden_in.shape[1]
    model_width = attn_gain.shape[0]
    head_dim = prefix_keys.shape[3]
    kv_local = prefix_keys.shape[2]
    kv_width = kv_local * head_dim
    group_length = w_query.shape[1] // kv_width
    prefix_total = prefix_keys.shape[1] * tok_count
    share_width = model_width // head_count
    experts = grp_count * tok_count
    top_count = expert_ids.shape[2]
    capacity = 4 * tok_dev * top_count // (3 * experts)

    quarter = hidden_in[0]
    features = lax.all_gather(quarter, "head", axis=1, tiled=True)
    query_blocks = others_over(w_query, "grp")
    key_blocks = others_over(key_projection_weight, "grp")
    value_blocks = others_over(value_projection_weight, "grp")
    full_out = lax.all_gather(w_out, "grp", axis=0, tiled=True)

    ids = expert_ids[0]
    named = ids[None, :, :] == jnp.arange(experts, dtype=jnp.int32)[:, None, None]
    routing = three_pieces(jnp.sum(jnp.where(named, route_weights[0][None], 0.0), axis=2))
    routing.append(jnp.sum(named.astype(jnp.float32), axis=2).astype(jnp.bfloat16))
    beside = 2 * kv_width // tok_dev
    payload = jnp.concatenate(
        [
            jnp.concatenate(
                [
                    prefix_keys[0].reshape(-1, kv_width),
                    cached_prefix_values[0].reshape(-1, kv_width),
                ],
                axis=1,
            )
        ]
        + [jnp.concatenate(routing[i : i + beside], axis=1) for i in range(0, 4, beside)],
        axis=0,
    )
    half_ring = tok_count // 2
    payloads = {0: payload}
    for distance in range(1, half_ring):
        payloads[distance] = along_ring(payload, distance)
        payloads[-distance] = along_ring(payload, -distance)
    payloads[half_ring] = along_ring(payload, half_ring)
    prefix_dev = prefix_keys.shape[1]
    prefix = jnp.concatenate([block[:prefix_dev] for block in payloads.values()], axis=0)

    gate_blocks = others_over(w_gate[0], "grp")
    up_blocks = others_over(w_up[0], "grp")
    down_blocks = others_over(w_down[0], "grp")

    attention_input = rms_norm(features, attn_gain)
    lengths = request_lengths[0]
    request_ends = jnp.cumsum(lengths)
    starts = request_ends - lengths
    token_index = tok_rank * tok_dev + jnp.arange(tok_dev, dtype=jnp.int32)
    own_start = jnp.max(
        jnp.where(starts[None, :] <= token_index[:, None], starts[None, :], 0), axis=1
    )
    token_positions = prefix_total + token_index - own_start
    key_product = split_product(attention_input, key_blocks, "grp")
    value_product = split_product(attention_input, value_blocks, "grp")
    query_product = split_product(attention_input, query_blocks, "grp")
    queries = apply_rotary(
        query_product.reshape(tok_dev, kv_local * group_length, head_dim), token_positions
    )
    queries = queries.reshape(tok_dev, kv_local, group_length, head_dim)
    request_suffix_keys = apply_rotary(
        key_product.reshape(tok_dev, kv_local, head_dim), token_positions
    )
    request_suffix_values = value_product.astype(jnp.bfloat16).reshape(tok_dev, kv_local, head_dim)
    running = (
        jnp.full((kv_local, tok_dev, group_length), MASKED, jnp.float32),
        jnp.zeros((kv_local, tok_dev, group_length), jnp.float32),
        jnp.zeros((kv_local, tok_dev, group_length, head_dim), jnp.float32),
    )
    running = attend(
        running,
        queries,
        prefix[:, :kv_width].reshape(prefix_total, kv_local, head_dim),
        prefix[:, kv_width:].reshape(prefix_total, kv_local, head_dim),
        None,
    )

    def visible_from(first_index, count):
        key_index = first_index + jnp.arange(count, dtype=jnp.int32)
        return (key_index[None, :] >= own_start[:, None]) & (
            key_index[None, :] <= token_index[:, None]
        )

    running = attend(
        running,
        queries,
        request_suffix_keys,
        request_suffix_values,
        visible_from(tok_rank * tok_dev, tok_dev),
    )
    longest = tok_dev * tok_count // 4
    reach_devices = (longest - 1 + tok_dev - 1) // tok_dev
    stacked = jnp.stack([request_suffix_keys, request_suffix_values])
    for distance in range(1, reach_devices + 1):
        arrived = shifted(stacked, "tok", distance)
        running = attend(
            running,
            queries,
            arrived[0],
            arrived[1],
            visible_from((tok_rank - distance) * tok_dev, tok_dev),
        )
    row_max, row_total, summed = running
    attended = (summed / row_total[..., None]).astype(jnp.bfloat16)
    attended = jnp.transpose(attended, (1, 0, 2, 3)).reshape(
        tok_dev, kv_local * group_length * head_dim
    )
    partial_value = lax.dot_general(
        attended, full_out, (((1,), (1,)), ((), ())), preferred_element_type=jnp.float32
    )
    mixed = lax.dynamic_slice_in_dim(partial_value, head_rank * share_width, share_width, 1)
    for distance in range(1, head_count):
        target = (head_rank + distance) % head_count
        leaving = lax.dynamic_slice_in_dim(partial_value, target * share_width, share_width, 1)
        mixed = mixed + turned_by(leaving.astype(jnp.bfloat16), "head", distance).astype(jnp.float32)
    mid_quarter = (quarter.astype(jnp.float32) + mixed).astype(jnp.bfloat16)
    mid_full = lax.all_gather(mid_quarter, "head", axis=1, tiled=True)
    moe_in = rms_norm(mid_full, moe_gain)
    arrived_tokens = ring_gather(moe_in)

    causal = (
        jnp.arange(tok_dev, dtype=jnp.int32)[:, None] <= jnp.arange(tok_dev, dtype=jnp.int32)[None, :]
    ).astype(jnp.bfloat16)
    slots = jnp.arange(capacity, dtype=jnp.int32)

    def routing_of(distance, expert):
        table = payloads[distance][prefix_dev:]
        pieces = []
        for i in range(4):
            rows = table[i // beside * experts : (i // beside + 1) * experts]
            column = i % beside * tok_dev
            row = lax.dynamic_slice_in_dim(rows[:, column : column + tok_dev], expert, 1, 0)
            pieces.append(row.astype(jnp.float32))
        return pieces[0] + pieces[1] + pieces[2], pieces[3]

    chunks = [[0, 1, -1]] + [[step, -step] for step in range(2, half_ring)] + [[half_ring]]
    parts = {}
    for chunk in chunks:
        tokens = jnp.stack([arrived_tokens[d] for d in chunk])
        picks, row_weights, hiddens = [], [], []
        for distance in range(grp_count):
            expert = ((grp_rank - distance) % grp_count) * tok_count + tok_rank
            tables = [routing_of(d, expert) for d in chunk]
            weight = jnp.concatenate([table[0] for table in tables], axis=0)
            mask = jnp.concatenate([table[1] for table in tables], axis=0)
            place = jnp.dot(mask.astype(jnp.bfloat16), causal, preferred_element_type=jnp.float32)
            place = jnp.where(mask > 0.5, place.astype(jnp.int32) - 1, -1)
            pick = place[:, None, :] == slots[None, :, None]
            row_weights.append(jnp.sum(jnp.where(pick, weight[:, None, :], 0.0), axis=2))
            pick = pick.astype(jnp.bfloat16)
            picks.append(pick)
            rows = jnp.einsum("bct,btf->bcf", pick, tokens, preferred_element_type=jnp.float32)
            rows = rows.astype(jnp.bfloat16).reshape(len(chunk) * capacity, model_width)
            gate_act = jnp.dot(rows, gate_blocks[distance], preferred_element_type=jnp.float32)
            up_act = jnp.dot(rows, up_blocks[distance], preferred_element_type=jnp.float32)
            hiddens.append((jax.nn.silu(gate_act) * up_act).astype(jnp.bfloat16))
        hidden = side_by_side(jnp.concatenate(hiddens, axis=0), "head")
        summed_out = None
        for distance in range(grp_count):
            own_rows = hidden[distance * len(chunk) * capacity :][: len(chunk) * capacity]
            result = jnp.dot(own_rows, down_blocks[distance], preferred_element_type=jnp.float32)
            result = result.reshape(len(chunk), capacity, share_width)
            result = (result * row_weights[distance][:, :, None]).astype(jnp.bfloat16)
            part = jnp.einsum(
                "bct,bcf->btf", picks[distance], result, preferred_element_type=jnp.float32
            )
            summed_out = part if summed_out is None else summed_out + part
        for place, d in enumerate(chunk):
            parts[d] = summed_out[place]
    weighted = ring_sum(parts)
    output = (mid_quarter.astype(jnp.float32) + weighted).astype(jnp.bfloat16)
    return output[None]


def solution(mesh):
    return jax.shard_map(
        on_device,
        mesh=mesh,
        in_specs=(
            P("grp", "tok", "head"),
            P(),
            P("grp", "head"),
            P("grp", "head"),
            P("grp", "head"),
            P("grp", "head"),
            P("grp", "tok", "head", None),
            P("grp", "tok", "head", None),
            P("grp", None),
            P(),
            P("grp", "tok", None),
            P("grp", "tok", None),
            P(("grp", "tok"), None, "head"),
            P(("grp", "tok"), None, "head"),
            P(("grp", "tok"), None, "head"),
        ),
        out_specs=P("grp", "tok", "head"),
        check_vma=False,
    )
```

```python
import math

import jax
import jax.numpy as jnp
from jax import lax
from jax.experimental import pallas as pl
from jax.experimental.pallas import tpu as pltpu
from jax.sharding import PartitionSpec as P

ROPE_BASE = 500000.0
NORM_EPS = 1e-06
MASKED = -1e30
VMEM_LIMIT = 40 * 1024 * 1024


def shifted(block, axis, distance):
    devices = range(lax.axis_size(axis))
    route = [(i - distance, i) for i in devices if i - distance in devices]
    return lax.ppermute(block, axis, route)


def rms_norm(values_in, gain_vector):
    widened = values_in.astype(jnp.float32)
    mean_sq = jnp.mean(widened * widened, axis=-1, keepdims=True)
    return (widened * lax.rsqrt(mean_sq + NORM_EPS) * gain_vector.astype(jnp.float32)).astype(
        jnp.bfloat16
    )


def apply_rotary(product, token_positions):
    half_dim = product.shape[-1] // 2
    frequency = jnp.exp(
        jnp.arange(half_dim, dtype=jnp.float32) * (-2.0 * math.log(ROPE_BASE) / product.shape[-1])
    )
    angles = token_positions.astype(jnp.float32)[:, None] * frequency[None, :]
    cosine = jnp.cos(angles)[:, None, :]
    sine_part = jnp.sin(angles)[:, None, :]
    first_half = product[..., :half_dim]
    second_half = product[..., half_dim:]
    turned = jnp.concatenate(
        [
            first_half * cosine - second_half * sine_part,
            second_half * cosine + first_half * sine_part,
        ],
        axis=-1,
    )
    return turned.astype(jnp.bfloat16)


def attend(running, queries, keys_block, values_block, visible):
    row_max, row_total, summed = running
    scores = jnp.einsum(
        "tcrd,kcd->ctrk", queries, keys_block, preferred_element_type=jnp.float32
    ) * queries.shape[-1] ** (-0.5)
    if visible is not None:
        scores = jnp.where(visible[None, :, None, :], scores, MASKED)
    new_max = jnp.maximum(row_max, jnp.max(scores, axis=-1))
    weights = jnp.exp(scores - new_max[..., None])
    if visible is not None:
        weights = jnp.where(visible[None, :, None, :], weights, 0.0)
    factor = jnp.exp(row_max - new_max)
    row_total = row_total * factor + jnp.sum(weights, axis=-1)
    summed = summed * factor[..., None] + jnp.einsum(
        "ctrk,kcd->ctrd",
        weights.astype(jnp.bfloat16),
        values_block,
        preferred_element_type=jnp.float32,
    )
    return (new_max, row_total, summed)


def turned_by(block, axis, distance):
    devices = lax.axis_size(axis)
    return lax.ppermute(block, axis, [(i, (i + distance) % devices) for i in range(devices)])


def along_ring(block, distance):
    devices = lax.axis_size("tok")
    order = list(range(0, devices, 2)) + list(range(devices - 1 - devices % 2, 0, -2))
    route = [(order[i], order[(i + distance) % devices]) for i in range(devices)]
    return lax.ppermute(block, "tok", route)


def ring_sum(parts):
    half = lax.axis_size("tok") // 2
    middle = parts[0].shape[1] // 2
    left = along_ring(parts[half][:, :middle].astype(jnp.bfloat16), -1).astype(jnp.float32)
    right = along_ring(parts[half][:, middle:].astype(jnp.bfloat16), 1).astype(jnp.float32)
    left = parts[half - 1] + jnp.pad(left, ((0, 0), (0, parts[0].shape[1] - middle)))
    right = parts[1 - half] + jnp.pad(right, ((0, 0), (middle, 0)))
    for step in range(half - 2, -1, -1):
        left = along_ring(left.astype(jnp.bfloat16), -1).astype(jnp.float32)
        right = along_ring(right.astype(jnp.bfloat16), 1).astype(jnp.float32)
        if step:
            left = left + parts[step]
            right = right + parts[-step]
    return parts[0] + left + right


def three_pieces(values):
    pieces = []
    for _ in range(3):
        piece = lax.reduce_precision(values, 8, 7)
        pieces.append(piece.astype(jnp.bfloat16))
        values = values - piece
    return pieces


def others_over(block, axis):
    return [block] + [turned_by(block, axis, d) for d in range(1, lax.axis_size(axis))]


def split_product(activations, blocks, axis):
    count = len(blocks)
    rank = lax.axis_index(axis)
    rows = blocks[0].shape[0]
    total = None
    for distance, block in enumerate(blocks):
        part = lax.dynamic_slice_in_dim(
            activations, ((rank - distance) % count) * rows, rows, 1
        )
        product = jnp.dot(part, block, preferred_element_type=jnp.float32)
        total = product if total is None else total + product
    return total


def width_tile(width, sizes):
    for size in sizes:
        if width % size == 0:
            return size
    return width


def picked_by(table_ref, expert, experts, tok_dev, capacity):
    beside = table_ref.shape[1] // tok_dev
    own = lax.broadcasted_iota(jnp.int32, (experts, tok_dev), 0) == expert

    def piece(i):
        rows = pl.ds(i // beside * experts, experts)
        columns = pl.ds(i % beside * tok_dev, tok_dev)
        values = table_ref[rows, columns].astype(jnp.float32)
        return jnp.sum(jnp.where(own, values, 0.0), axis=0, keepdims=True)

    weight = piece(0) + piece(1) + piece(2)
    mask = piece(3)
    upto = lax.broadcasted_iota(jnp.int32, (tok_dev, tok_dev), 0) <= lax.broadcasted_iota(
        jnp.int32, (tok_dev, tok_dev), 1
    )
    upto = jnp.where(upto, 1.0, 0.0).astype(jnp.bfloat16)
    many = jnp.broadcast_to(mask, (16, tok_dev)).astype(jnp.bfloat16)
    place = jnp.dot(many, upto, preferred_element_type=jnp.float32)[0:1]
    place = jnp.where(mask > 0.5, place - 1.0, -1.0).astype(jnp.int32)
    slots = lax.broadcasted_iota(jnp.int32, (capacity, tok_dev), 0)
    pick = jnp.where(slots == place, 1.0, 0.0)
    return pick.astype(jnp.bfloat16), jnp.sum(pick * weight, axis=1, keepdims=True)


def hidden_units(chosen, tables, blocks, gates, ups, experts, capacity):
    count, grp_count = len(blocks), len(gates)
    tok_dev = blocks[0][0].shape[0]
    model_width, hidden_width = gates[0].shape
    tile = width_tile(hidden_width, (256, 384, 128))
    steps = hidden_width // tile
    pieces = [len(block) for block in blocks]
    columns = sum(pieces)

    def body(chosen_ref, *refs):
        table_refs, refs = refs[:count], refs[count:]
        token_refs, refs = refs[:columns], refs[columns:]
        gate_refs, refs = refs[:grp_count], refs[grp_count:]
        up_refs, refs = refs[:grp_count], refs[grp_count:]
        out_ref, rows_ref = refs
        which, step = pl.program_id(0), pl.program_id(1)

        @pl.when(step == 0)
        def _():
            at = 0
            for i in range(count):
                pick, _ = picked_by(table_refs[i], chosen_ref[which], experts, tok_dev, capacity)
                first = 0
                for token_ref in token_refs[at : at + pieces[i]]:
                    width = token_ref.shape[1]
                    rows_ref[pl.ds(i * capacity, capacity), pl.ds(first, width)] = jnp.dot(
                        pick, token_ref[...], preferred_element_type=jnp.float32
                    ).astype(jnp.bfloat16)
                    first += width
                at += pieces[i]

        for g in range(grp_count):

            @pl.when(which == g)
            def _(g=g):
                rows = rows_ref[...]
                gate = jnp.dot(rows, gate_refs[g][...], preferred_element_type=jnp.float32)
                up = jnp.dot(rows, up_refs[g][...], preferred_element_type=jnp.float32)
                out_ref[0] = (gate / (1.0 + jnp.exp(-gate)) * up).astype(jnp.bfloat16)

    def whole(array):
        return pl.BlockSpec(array.shape, lambda e, n, ids: (0, 0))

    def weight_spec(g):
        def place(e, n, ids):
            return (0, jnp.where(e == g, n, jnp.where(e > g, steps - 1, 0)))

        return pl.BlockSpec((model_width, tile), place)

    flat = [part for block in blocks for part in block]
    specs = [whole(table) for table in tables] + [whole(part) for part in flat]
    specs += [weight_spec(g) for g in range(grp_count)] * 2
    return pl.pallas_call(
        body,
        out_shape=jax.ShapeDtypeStruct((grp_count, count * capacity, hidden_width), jnp.bfloat16),
        grid_spec=pltpu.PrefetchScalarGridSpec(
            num_scalar_prefetch=1,
            grid=(grp_count, steps),
            in_specs=specs,
            out_specs=pl.BlockSpec((1, count * capacity, tile), lambda e, n, ids: (e, 0, n)),
            scratch_shapes=[pltpu.VMEM((count * capacity, model_width), jnp.bfloat16)],
        ),
        compiler_params=pltpu.CompilerParams(vmem_limit_bytes=VMEM_LIMIT),
        name="hidden_units",
    )(chosen, *tables, *flat, *gates, *ups)


def token_sums(chosen, tables, hiddens, downs, tok_dev, experts, capacity):
    count, grp_count, head_count = len(tables), len(downs), len(hiddens)
    rows_each = hiddens[0].shape[2]
    share_width = downs[0].shape[1]
    tile = width_tile(share_width, (640,))

    def body(chosen_ref, *refs):
        table_refs, refs = refs[:count], refs[count:]
        hidden_refs, refs = refs[:head_count], refs[head_count:]
        down_refs, out_refs = refs[:grp_count], refs[grp_count:]
        which = pl.program_id(1)
        rank = chosen_ref[grp_count]
        for g in range(grp_count):

            @pl.when(which == g)
            def _(g=g):
                result = None
                for distance in range(head_count):
                    first = (rank - distance + head_count) % head_count * rows_each
                    down = down_refs[g][pl.ds(pl.multiple_of(first, rows_each), rows_each), :]
                    part = jnp.dot(
                        hidden_refs[distance][0], down, preferred_element_type=jnp.float32
                    )
                    result = part if result is None else result + part
                for i in range(count):
                    pick, weight = picked_by(
                        table_refs[i], chosen_ref[g], experts, tok_dev, capacity
                    )
                    scaled = result[i * capacity : (i + 1) * capacity] * weight
                    part = lax.dot_general(
                        pick,
                        scaled.astype(jnp.bfloat16),
                        (((0,), (0,)), ((), ())),
                        preferred_element_type=jnp.float32,
                    )
                    out_refs[i][...] = part if g == 0 else out_refs[i][...] + part

    specs = [pl.BlockSpec(table.shape, lambda n, e, ids: (0, 0)) for table in tables]
    specs += [
        pl.BlockSpec((1,) + hidden.shape[1:], lambda n, e, ids: (e, 0, 0)) for hidden in hiddens
    ]
    specs += [pl.BlockSpec((down.shape[0], tile), lambda n, e, ids: (0, n)) for down in downs]
    return pl.pallas_call(
        body,
        out_shape=[jax.ShapeDtypeStruct((tok_dev, share_width), jnp.float32)] * count,
        grid_spec=pltpu.PrefetchScalarGridSpec(
            num_scalar_prefetch=1,
            grid=(share_width // tile, grp_count),
            in_specs=specs,
            out_specs=[pl.BlockSpec((tok_dev, tile), lambda n, e, ids: (0, n))] * count,
        ),
        compiler_params=pltpu.CompilerParams(vmem_limit_bytes=VMEM_LIMIT),
        name="token_sums",
    )(chosen, *tables, *hiddens, *downs)


def on_device(
    hidden_in,
    attn_gain,
    w_query,
    key_projection_weight,
    value_projection_weight,
    w_out,
    prefix_keys,
    cached_prefix_values,
    request_lengths,
    moe_gain,
    expert_ids,
    route_weights,
    w_gate,
    w_up,
    w_down,
):
    tok_count = lax.axis_size("tok")
    grp_count = lax.axis_size("grp")
    head_count = lax.axis_size("head")
    tok_rank = lax.axis_index("tok")
    grp_rank = lax.axis_index("grp")
    head_rank = lax.axis_index("head")
    tok_dev = hidden_in.shape[1]
    model_width = attn_gain.shape[0]
    head_dim = prefix_keys.shape[3]
    kv_local = prefix_keys.shape[2]
    kv_width = kv_local * head_dim
    group_length = w_query.shape[1] // kv_width
    prefix_total = prefix_keys.shape[1] * tok_count
    share_width = model_width // head_count
    experts = grp_count * tok_count
    top_count = expert_ids.shape[2]
    capacity = 4 * tok_dev * top_count // (3 * experts)

    quarter = hidden_in[0]
    features = lax.all_gather(quarter, "head", axis=1, tiled=True)
    query_blocks = others_over(w_query, "grp")
    key_blocks = others_over(key_projection_weight, "grp")
    value_blocks = others_over(value_projection_weight, "grp")
    full_out = lax.all_gather(w_out, "grp", axis=0, tiled=True)

    ids = expert_ids[0]
    named = ids[None, :, :] == jnp.arange(experts, dtype=jnp.int32)[:, None, None]
    routing = three_pieces(jnp.sum(jnp.where(named, route_weights[0][None], 0.0), axis=2))
    routing.append(jnp.sum(named.astype(jnp.float32), axis=2).astype(jnp.bfloat16))
    beside = 2 * kv_width // tok_dev
    payload = jnp.concatenate(
        [
            jnp.concatenate(
                [
                    prefix_keys[0].reshape(-1, kv_width),
                    cached_prefix_values[0].reshape(-1, kv_width),
                ],
                axis=1,
            )
        ]
        + [jnp.concatenate(routing[i : i + beside], axis=1) for i in range(0, 4, beside)],
        axis=0,
    )
    half_ring = tok_count // 2
    payloads = {0: payload}
    for distance in range(1, half_ring):
        payloads[distance] = along_ring(payload, distance)
        payloads[-distance] = along_ring(payload, -distance)
    payloads[half_ring] = along_ring(payload, half_ring)
    prefix_dev = prefix_keys.shape[1]
    prefix = jnp.concatenate([block[:prefix_dev] for block in payloads.values()], axis=0)

    gate_blocks = others_over(w_gate[0], "grp")
    up_blocks = others_over(w_up[0], "grp")
    down_blocks = others_over(w_down[0], "grp")

    attention_input = rms_norm(features, attn_gain)
    lengths = request_lengths[0]
    request_ends = jnp.cumsum(lengths)
    starts = request_ends - lengths
    token_index = tok_rank * tok_dev + jnp.arange(tok_dev, dtype=jnp.int32)
    own_start = jnp.max(
        jnp.where(starts[None, :] <= token_index[:, None], starts[None, :], 0), axis=1
    )
    token_positions = prefix_total + token_index - own_start
    key_product = split_product(attention_input, key_blocks, "grp")
    value_product = split_product(attention_input, value_blocks, "grp")
    query_product = split_product(attention_input, query_blocks, "grp")
    queries = apply_rotary(
        query_product.reshape(tok_dev, kv_local * group_length, head_dim), token_positions
    )
    queries = queries.reshape(tok_dev, kv_local, group_length, head_dim)
    request_suffix_keys = apply_rotary(
        key_product.reshape(tok_dev, kv_local, head_dim), token_positions
    )
    request_suffix_values = value_product.astype(jnp.bfloat16).reshape(tok_dev, kv_local, head_dim)
    running = (
        jnp.full((kv_local, tok_dev, group_length), MASKED, jnp.float32),
        jnp.zeros((kv_local, tok_dev, group_length), jnp.float32),
        jnp.zeros((kv_local, tok_dev, group_length, head_dim), jnp.float32),
    )
    running = attend(
        running,
        queries,
        prefix[:, :kv_width].reshape(prefix_total, kv_local, head_dim),
        prefix[:, kv_width:].reshape(prefix_total, kv_local, head_dim),
        None,
    )

    def visible_from(first_index, count):
        key_index = first_index + jnp.arange(count, dtype=jnp.int32)
        return (key_index[None, :] >= own_start[:, None]) & (
            key_index[None, :] <= token_index[:, None]
        )

    running = attend(
        running,
        queries,
        request_suffix_keys,
        request_suffix_values,
        visible_from(tok_rank * tok_dev, tok_dev),
    )
    longest = tok_dev * tok_count // 4
    reach_devices = (longest - 1 + tok_dev - 1) // tok_dev
    stacked = jnp.stack([request_suffix_keys, request_suffix_values])
    for distance in range(1, reach_devices + 1):
        arrived = shifted(stacked, "tok", distance)
        running = attend(
            running,
            queries,
            arrived[0],
            arrived[1],
            visible_from((tok_rank - distance) * tok_dev, tok_dev),
        )
    row_max, row_total, summed = running
    attended = (summed / row_total[..., None]).astype(jnp.bfloat16)
    attended = jnp.transpose(attended, (1, 0, 2, 3)).reshape(
        tok_dev, kv_local * group_length * head_dim
    )
    partial_value = lax.dot_general(
        attended, full_out, (((1,), (1,)), ((), ())), preferred_element_type=jnp.float32
    )
    mixed = lax.dynamic_slice_in_dim(partial_value, head_rank * share_width, share_width, 1)
    for distance in range(1, head_count):
        target = (head_rank + distance) % head_count
        leaving = lax.dynamic_slice_in_dim(partial_value, target * share_width, share_width, 1)
        mixed = mixed + turned_by(leaving.astype(jnp.bfloat16), "head", distance).astype(jnp.float32)
    mid_quarter = (quarter.astype(jnp.float32) + mixed).astype(jnp.bfloat16)
    mid_full = lax.all_gather(mid_quarter, "head", axis=1, tiled=True)
    moe_in = rms_norm(mid_full, moe_gain)
    tables = {d: block[prefix_dev:] for d, block in payloads.items()}
    chosen = jnp.stack(
        [((grp_rank - d) % grp_count) * tok_count + tok_rank for d in range(grp_count)]
        + [head_rank]
    ).astype(jnp.int32)

    def units_of(chunk, blocks):
        return hidden_units(
            chosen, [tables[d] for d in chunk], blocks, gate_blocks, up_blocks, experts, capacity
        )

    parts = {}

    def sum_up(chunk, exchanged):
        sums = token_sums(
            chosen, [tables[d] for d in chunk], exchanged, down_blocks, tok_dev, experts, capacity
        )
        parts.update(zip(chunk, sums))

    middle = model_width // 2
    ahead, behind = moe_in, moe_in
    chunk, blocks = [0], [[moe_in]]
    waiting = []
    for step in range(1, half_ring + 1):
        last = step == half_ring
        sent = (ahead[:, :middle], behind[:, middle:]) if last else (ahead, behind)
        arriving = (along_ring(sent[0], 1), along_ring(sent[1], -1))
        hidden = units_of(chunk, blocks)
        if len(waiting) > 1:
            sum_up(*waiting.pop(0))
        (ahead, behind), hidden, parts = lax.optimization_barrier((arriving, hidden, parts))
        waiting.append((chunk, others_over(hidden, "head")))
        chunk = [half_ring] if last else [step, -step]
        blocks = [[ahead, behind]] if last else [[ahead], [behind]]
    waiting.append((chunk, others_over(units_of(chunk, blocks), "head")))
    for entry in waiting:
        sum_up(*entry)
    weighted = ring_sum(parts)
    output = (mid_quarter.astype(jnp.float32) + weighted).astype(jnp.bfloat16)
    return output[None]


def solution(mesh):
    return jax.shard_map(
        on_device,
        mesh=mesh,
        in_specs=(
            P("grp", "tok", "head"),
            P(),
            P("grp", "head"),
            P("grp", "head"),
            P("grp", "head"),
            P("grp", "head"),
            P("grp", "tok", "head", None),
            P("grp", "tok", "head", None),
            P("grp", None),
            P(),
            P("grp", "tok", None),
            P("grp", "tok", None),
            P(("grp", "tok"), None, "head"),
            P(("grp", "tok"), None, "head"),
            P(("grp", "tok"), None, "head"),
        ),
        out_specs=P("grp", "tok", "head"),
        check_vma=False,
    )
```

```python
import math

import jax
import jax.numpy as jnp
from jax import lax
from jax.experimental import pallas as pl
from jax.experimental.pallas import tpu as pltpu
from jax.sharding import PartitionSpec as P

ROPE_BASE = 500000.0
NORM_EPS = 1e-06
MASKED = -1e30
VMEM_LIMIT = 56 * 1024 * 1024


def shifted(block, axis, distance):
    devices = range(lax.axis_size(axis))
    route = [(i - distance, i) for i in devices if i - distance in devices]
    return lax.ppermute(block, axis, route)


def rms_norm(values_in, gain_vector):
    widened = values_in.astype(jnp.float32)
    mean_sq = jnp.mean(widened * widened, axis=-1, keepdims=True)
    return (widened * lax.rsqrt(mean_sq + NORM_EPS) * gain_vector.astype(jnp.float32)).astype(
        jnp.bfloat16
    )


def apply_rotary(product, token_positions):
    half_dim = product.shape[-1] // 2
    frequency = jnp.exp(
        jnp.arange(half_dim, dtype=jnp.float32) * (-2.0 * math.log(ROPE_BASE) / product.shape[-1])
    )
    angles = token_positions.astype(jnp.float32)[:, None] * frequency[None, :]
    cosine = jnp.cos(angles)[:, None, :]
    sine_part = jnp.sin(angles)[:, None, :]
    first_half = product[..., :half_dim]
    second_half = product[..., half_dim:]
    turned = jnp.concatenate(
        [
            first_half * cosine - second_half * sine_part,
            second_half * cosine + first_half * sine_part,
        ],
        axis=-1,
    )
    return turned.astype(jnp.bfloat16)


def attend(running, queries, keys_block, values_block, visible):
    row_max, row_total, summed = running
    scores = jnp.einsum(
        "tcrd,kcd->ctrk", queries, keys_block, preferred_element_type=jnp.float32
    ) * queries.shape[-1] ** (-0.5)
    if visible is not None:
        scores = jnp.where(visible[None, :, None, :], scores, MASKED)
    new_max = jnp.maximum(row_max, jnp.max(scores, axis=-1))
    weights = jnp.exp(scores - new_max[..., None])
    if visible is not None:
        weights = jnp.where(visible[None, :, None, :], weights, 0.0)
    factor = jnp.exp(row_max - new_max)
    row_total = row_total * factor + jnp.sum(weights, axis=-1)
    summed = summed * factor[..., None] + jnp.einsum(
        "ctrk,kcd->ctrd",
        weights.astype(jnp.bfloat16),
        values_block,
        preferred_element_type=jnp.float32,
    )
    return (new_max, row_total, summed)


def turned_by(block, axis, distance):
    devices = lax.axis_size(axis)
    return lax.ppermute(block, axis, [(i, (i + distance) % devices) for i in range(devices)])


def along_ring(block, distance):
    devices = lax.axis_size("tok")
    order = list(range(0, devices, 2)) + list(range(devices - 1 - devices % 2, 0, -2))
    route = [(order[i], order[(i + distance) % devices]) for i in range(devices)]
    return lax.ppermute(block, "tok", route)


def ring_sum(parts):
    half = lax.axis_size("tok") // 2
    middle = parts[0].shape[1] // 2
    left = along_ring(parts[half][:, :middle].astype(jnp.bfloat16), -1).astype(jnp.float32)
    right = along_ring(parts[half][:, middle:].astype(jnp.bfloat16), 1).astype(jnp.float32)
    left = parts[half - 1] + jnp.pad(left, ((0, 0), (0, parts[0].shape[1] - middle)))
    right = parts[1 - half] + jnp.pad(right, ((0, 0), (middle, 0)))
    for step in range(half - 2, -1, -1):
        left = along_ring(left.astype(jnp.bfloat16), -1).astype(jnp.float32)
        right = along_ring(right.astype(jnp.bfloat16), 1).astype(jnp.float32)
        if step:
            left = left + parts[step]
            right = right + parts[-step]
    return parts[0] + left + right


def three_pieces(values):
    pieces = []
    for _ in range(3):
        piece = lax.reduce_precision(values, 8, 7)
        pieces.append(piece.astype(jnp.bfloat16))
        values = values - piece
    return pieces


def others_over(block, axis):
    return [block] + [turned_by(block, axis, d) for d in range(1, lax.axis_size(axis))]


def split_product(activations, blocks, axis):
    count = len(blocks)
    rank = lax.axis_index(axis)
    rows = blocks[0].shape[0]
    total = None
    for distance, block in enumerate(blocks):
        part = lax.dynamic_slice_in_dim(
            activations, ((rank - distance) % count) * rows, rows, 1
        )
        product = jnp.dot(part, block, preferred_element_type=jnp.float32)
        total = product if total is None else total + product
    return total


def width_tile(width, sizes):
    for size in sizes:
        if width % size == 0:
            return size
    return width


def picked_by(table_ref, expert, experts, tok_dev, capacity):
    beside = table_ref.shape[1] // tok_dev
    own = lax.broadcasted_iota(jnp.int32, (experts, tok_dev), 0) == expert

    def piece(i):
        rows = pl.ds(i // beside * experts, experts)
        columns = pl.ds(i % beside * tok_dev, tok_dev)
        values = table_ref[rows, columns].astype(jnp.float32)
        return jnp.sum(jnp.where(own, values, 0.0), axis=0, keepdims=True)

    weight = piece(0) + piece(1) + piece(2)
    mask = piece(3)
    upto = lax.broadcasted_iota(jnp.int32, (tok_dev, tok_dev), 0) <= lax.broadcasted_iota(
        jnp.int32, (tok_dev, tok_dev), 1
    )
    upto = jnp.where(upto, 1.0, 0.0).astype(jnp.bfloat16)
    many = jnp.broadcast_to(mask, (16, tok_dev)).astype(jnp.bfloat16)
    place = jnp.dot(many, upto, preferred_element_type=jnp.float32)[0:1]
    place = jnp.where(mask > 0.5, place - 1.0, -1.0).astype(jnp.int32)
    slots = lax.broadcasted_iota(jnp.int32, (capacity, tok_dev), 0)
    pick = jnp.where(slots == place, 1.0, 0.0)
    return pick.astype(jnp.bfloat16), jnp.sum(pick * weight, axis=1, keepdims=True)


def hidden_units(chosen, tables, blocks, gates, ups, experts, capacity):
    count, grp_count = len(blocks), len(gates)
    tok_dev = blocks[0][0].shape[0]
    model_width, hidden_width = gates[0].shape
    tile = width_tile(hidden_width, (256, 384, 128))
    steps = hidden_width // tile
    pieces = [len(block) for block in blocks]
    columns = sum(pieces)

    def body(chosen_ref, *refs):
        table_refs, refs = refs[:count], refs[count:]
        token_refs, refs = refs[:columns], refs[columns:]
        gate_refs, refs = refs[:grp_count], refs[grp_count:]
        up_refs, refs = refs[:grp_count], refs[grp_count:]
        out_ref, rows_ref, weight_ref, arrived = refs
        copies = {}
        for g in range(grp_count):
            for n in range(steps):
                for k, ref in enumerate((gate_refs[g], up_refs[g])):
                    copies[g, n, k] = pltpu.make_async_copy(
                        ref.at[:, pl.ds(n * tile, tile)],
                        weight_ref.at[g, n, k],
                        arrived.at[(g * steps + n) * 2 + k],
                    )
                    copies[g, n, k].start()
        for g in range(grp_count):
            at = 0
            for i in range(count):
                pick, _ = picked_by(table_refs[i], chosen_ref[g], experts, tok_dev, capacity)
                first = 0
                for token_ref in token_refs[at : at + pieces[i]]:
                    width = token_ref.shape[1]
                    rows_ref[g, pl.ds(i * capacity, capacity), pl.ds(first, width)] = jnp.dot(
                        pick, token_ref[...], preferred_element_type=jnp.float32
                    ).astype(jnp.bfloat16)
                    first += width
                at += pieces[i]
        for g in range(grp_count):
            for n in range(steps):
                acts = []
                for k in range(2):
                    copies[g, n, k].wait()
                    acts.append(
                        jnp.dot(
                            rows_ref[g], weight_ref[g, n, k], preferred_element_type=jnp.float32
                        )
                    )
                gate, up = acts
                out_ref[g, :, pl.ds(n * tile, tile)] = (
                    gate / (1.0 + jnp.exp(-gate)) * up
                ).astype(jnp.bfloat16)

    in_vmem = pl.BlockSpec(memory_space=pltpu.VMEM)
    in_hbm = pl.BlockSpec(memory_space=pltpu.HBM)
    flat = [part for block in blocks for part in block]
    return pl.pallas_call(
        body,
        out_shape=jax.ShapeDtypeStruct((grp_count, count * capacity, hidden_width), jnp.bfloat16),
        in_specs=[pl.BlockSpec(memory_space=pltpu.SMEM)]
        + [in_vmem] * (count + columns)
        + [in_hbm] * (2 * grp_count),
        out_specs=in_vmem,
        scratch_shapes=[
            pltpu.VMEM((grp_count, count * capacity, model_width), jnp.bfloat16),
            pltpu.VMEM((grp_count, steps, 2, model_width, tile), jnp.bfloat16),
            pltpu.SemaphoreType.DMA((grp_count * steps * 2,)),
        ],
        compiler_params=pltpu.CompilerParams(vmem_limit_bytes=VMEM_LIMIT),
        name="hidden_units",
    )(chosen, *tables, *flat, *gates, *ups)


def token_sums(chosen, tables, hiddens, downs, tok_dev, experts, capacity):
    count, grp_count, head_count = len(tables), len(downs), len(hiddens)
    rows_each = hiddens[0].shape[2]
    share_width = downs[0].shape[1]
    tile = width_tile(share_width, (256, 640))
    steps = share_width // tile

    def body(chosen_ref, *refs):
        table_refs, refs = refs[:count], refs[count:]
        hidden_refs, refs = refs[:head_count], refs[head_count:]
        down_refs, refs = refs[:grp_count], refs[grp_count:]
        out_refs, (weight_ref, arrived) = refs[:count], refs[count:]
        rank = chosen_ref[grp_count]
        copies = {}
        for n in range(steps):
            for g in range(grp_count):
                for k in range(head_count):
                    first = (rank - k + head_count) % head_count * rows_each
                    copies[n, g, k] = pltpu.make_async_copy(
                        down_refs[g].at[
                            pl.ds(pl.multiple_of(first, rows_each), rows_each),
                            pl.ds(n * tile, tile),
                        ],
                        weight_ref.at[n, g, k],
                        arrived.at[(n * grp_count + g) * head_count + k],
                    )
                    copies[n, g, k].start()
        picks = [
            [
                picked_by(table_refs[i], chosen_ref[g], experts, tok_dev, capacity)
                for g in range(grp_count)
            ]
            for i in range(count)
        ]
        both = [jnp.concatenate([pick for pick, _ in own], axis=0) for own in picks]
        for n in range(steps):
            results = []
            for g in range(grp_count):
                result = None
                for k in range(head_count):
                    copies[n, g, k].wait()
                    part = jnp.dot(
                        hidden_refs[k][g], weight_ref[n, g, k], preferred_element_type=jnp.float32
                    )
                    result = part if result is None else result + part
                results.append(result)
            for i in range(count):
                scaled = jnp.concatenate(
                    [
                        (results[g][i * capacity : (i + 1) * capacity] * picks[i][g][1]).astype(
                            jnp.bfloat16
                        )
                        for g in range(grp_count)
                    ],
                    axis=0,
                )
                out_refs[i][:, pl.ds(n * tile, tile)] = lax.dot_general(
                    both[i], scaled, (((0,), (0,)), ((), ())), preferred_element_type=jnp.float32
                )

    in_vmem = pl.BlockSpec(memory_space=pltpu.VMEM)
    in_hbm = pl.BlockSpec(memory_space=pltpu.HBM)
    return pl.pallas_call(
        body,
        out_shape=[jax.ShapeDtypeStruct((tok_dev, share_width), jnp.float32)] * count,
        in_specs=[pl.BlockSpec(memory_space=pltpu.SMEM)]
        + [in_vmem] * (count + head_count)
        + [in_hbm] * grp_count,
        out_specs=[in_vmem] * count,
        scratch_shapes=[
            pltpu.VMEM((steps, grp_count, head_count, rows_each, tile), jnp.bfloat16),
            pltpu.SemaphoreType.DMA((steps * grp_count * head_count,)),
        ],
        compiler_params=pltpu.CompilerParams(vmem_limit_bytes=VMEM_LIMIT),
        name="token_sums",
    )(chosen, *tables, *hiddens, *downs)


def on_device(
    hidden_in,
    attn_gain,
    w_query,
    key_projection_weight,
    value_projection_weight,
    w_out,
    prefix_keys,
    cached_prefix_values,
    request_lengths,
    moe_gain,
    expert_ids,
    route_weights,
    w_gate,
    w_up,
    w_down,
):
    tok_count = lax.axis_size("tok")
    grp_count = lax.axis_size("grp")
    head_count = lax.axis_size("head")
    tok_rank = lax.axis_index("tok")
    grp_rank = lax.axis_index("grp")
    head_rank = lax.axis_index("head")
    tok_dev = hidden_in.shape[1]
    model_width = attn_gain.shape[0]
    head_dim = prefix_keys.shape[3]
    kv_local = prefix_keys.shape[2]
    kv_width = kv_local * head_dim
    group_length = w_query.shape[1] // kv_width
    prefix_total = prefix_keys.shape[1] * tok_count
    share_width = model_width // head_count
    experts = grp_count * tok_count
    top_count = expert_ids.shape[2]
    capacity = 4 * tok_dev * top_count // (3 * experts)

    quarter = hidden_in[0]
    features = lax.all_gather(quarter, "head", axis=1, tiled=True)
    query_blocks = others_over(w_query, "grp")
    key_blocks = others_over(key_projection_weight, "grp")
    value_blocks = others_over(value_projection_weight, "grp")
    full_out = lax.all_gather(w_out, "grp", axis=0, tiled=True)

    ids = expert_ids[0]
    named = ids[None, :, :] == jnp.arange(experts, dtype=jnp.int32)[:, None, None]
    routing = three_pieces(jnp.sum(jnp.where(named, route_weights[0][None], 0.0), axis=2))
    routing.append(jnp.sum(named.astype(jnp.float32), axis=2).astype(jnp.bfloat16))
    beside = 2 * kv_width // tok_dev
    payload = jnp.concatenate(
        [
            jnp.concatenate(
                [
                    prefix_keys[0].reshape(-1, kv_width),
                    cached_prefix_values[0].reshape(-1, kv_width),
                ],
                axis=1,
            )
        ]
        + [jnp.concatenate(routing[i : i + beside], axis=1) for i in range(0, 4, beside)],
        axis=0,
    )
    half_ring = tok_count // 2
    payloads = {0: payload}
    for distance in range(1, half_ring):
        payloads[distance] = along_ring(payload, distance)
        payloads[-distance] = along_ring(payload, -distance)
    payloads[half_ring] = along_ring(payload, half_ring)
    prefix_dev = prefix_keys.shape[1]
    prefix = jnp.concatenate([block[:prefix_dev] for block in payloads.values()], axis=0)

    gate_blocks = others_over(w_gate[0], "grp")
    up_blocks = others_over(w_up[0], "grp")
    down_blocks = others_over(w_down[0], "grp")

    attention_input = rms_norm(features, attn_gain)
    lengths = request_lengths[0]
    request_ends = jnp.cumsum(lengths)
    starts = request_ends - lengths
    token_index = tok_rank * tok_dev + jnp.arange(tok_dev, dtype=jnp.int32)
    own_start = jnp.max(
        jnp.where(starts[None, :] <= token_index[:, None], starts[None, :], 0), axis=1
    )
    token_positions = prefix_total + token_index - own_start
    key_product = split_product(attention_input, key_blocks, "grp")
    value_product = split_product(attention_input, value_blocks, "grp")
    query_product = split_product(attention_input, query_blocks, "grp")
    queries = apply_rotary(
        query_product.reshape(tok_dev, kv_local * group_length, head_dim), token_positions
    )
    queries = queries.reshape(tok_dev, kv_local, group_length, head_dim)
    request_suffix_keys = apply_rotary(
        key_product.reshape(tok_dev, kv_local, head_dim), token_positions
    )
    request_suffix_values = value_product.astype(jnp.bfloat16).reshape(tok_dev, kv_local, head_dim)
    running = (
        jnp.full((kv_local, tok_dev, group_length), MASKED, jnp.float32),
        jnp.zeros((kv_local, tok_dev, group_length), jnp.float32),
        jnp.zeros((kv_local, tok_dev, group_length, head_dim), jnp.float32),
    )
    running = attend(
        running,
        queries,
        prefix[:, :kv_width].reshape(prefix_total, kv_local, head_dim),
        prefix[:, kv_width:].reshape(prefix_total, kv_local, head_dim),
        None,
    )

    def visible_from(first_index, count):
        key_index = first_index + jnp.arange(count, dtype=jnp.int32)
        return (key_index[None, :] >= own_start[:, None]) & (
            key_index[None, :] <= token_index[:, None]
        )

    running = attend(
        running,
        queries,
        request_suffix_keys,
        request_suffix_values,
        visible_from(tok_rank * tok_dev, tok_dev),
    )
    longest = tok_dev * tok_count // 4
    reach_devices = (longest - 1 + tok_dev - 1) // tok_dev
    stacked = jnp.stack([request_suffix_keys, request_suffix_values])
    for distance in range(1, reach_devices + 1):
        arrived = shifted(stacked, "tok", distance)
        running = attend(
            running,
            queries,
            arrived[0],
            arrived[1],
            visible_from((tok_rank - distance) * tok_dev, tok_dev),
        )
    row_max, row_total, summed = running
    attended = (summed / row_total[..., None]).astype(jnp.bfloat16)
    attended = jnp.transpose(attended, (1, 0, 2, 3)).reshape(
        tok_dev, kv_local * group_length * head_dim
    )
    partial_value = lax.dot_general(
        attended, full_out, (((1,), (1,)), ((), ())), preferred_element_type=jnp.float32
    )
    mixed = lax.dynamic_slice_in_dim(partial_value, head_rank * share_width, share_width, 1)
    for distance in range(1, head_count):
        target = (head_rank + distance) % head_count
        leaving = lax.dynamic_slice_in_dim(partial_value, target * share_width, share_width, 1)
        mixed = mixed + turned_by(leaving.astype(jnp.bfloat16), "head", distance).astype(jnp.float32)
    mid_quarter = (quarter.astype(jnp.float32) + mixed).astype(jnp.bfloat16)
    mid_full = lax.all_gather(mid_quarter, "head", axis=1, tiled=True)
    moe_in = rms_norm(mid_full, moe_gain)
    tables = {d: block[prefix_dev:] for d, block in payloads.items()}
    chosen = jnp.stack(
        [((grp_rank - d) % grp_count) * tok_count + tok_rank for d in range(grp_count)]
        + [head_rank]
    ).astype(jnp.int32)

    def units_of(chunk, blocks):
        return hidden_units(
            chosen, [tables[d] for d in chunk], blocks, gate_blocks, up_blocks, experts, capacity
        )

    parts = {}

    def sum_up(chunk, exchanged):
        sums = token_sums(
            chosen, [tables[d] for d in chunk], exchanged, down_blocks, tok_dev, experts, capacity
        )
        parts.update(zip(chunk, sums))

    middle = model_width // 2
    ahead, behind = moe_in, moe_in
    pending, chunk, exchanged = {0: [moe_in]}, None, None
    for step in range(1, half_ring + 1):
        last = step == half_ring
        sent = (ahead[:, :middle], behind[:, middle:]) if last else (ahead, behind)
        arriving = (along_ring(sent[0], 1), along_ring(sent[1], -1))
        hidden = None
        if chunk is not None:
            hidden = units_of(list(chunk), list(chunk.values()))
        elif exchanged is not None:
            sum_up(*exchanged)
            exchanged = None
        (ahead, behind), hidden, parts = lax.optimization_barrier((arriving, hidden, parts))
        if chunk is not None:
            exchanged = (list(chunk), others_over(hidden, "head"))
            chunk = None
        if not last:
            pending.update({step: [ahead], -step: [behind]})
            if step % 2 or step == half_ring - 1:
                chunk, pending = pending, {}
    pending[half_ring] = [ahead, behind]
    hidden = units_of(list(pending), list(pending.values()))
    arriving = others_over(hidden, "head")
    if exchanged is not None:
        sum_up(*exchanged)
        arriving, parts = lax.optimization_barrier((arriving, parts))
    sum_up(list(pending), arriving)
    weighted = ring_sum(parts)
    output = (mid_quarter.astype(jnp.float32) + weighted).astype(jnp.bfloat16)
    return output[None]


def solution(mesh):
    return jax.shard_map(
        on_device,
        mesh=mesh,
        in_specs=(
            P("grp", "tok", "head"),
            P(),
            P("grp", "head"),
            P("grp", "head"),
            P("grp", "head"),
            P("grp", "head"),
            P("grp", "tok", "head", None),
            P("grp", "tok", "head", None),
            P("grp", None),
            P(),
            P("grp", "tok", None),
            P("grp", "tok", None),
            P(("grp", "tok"), None, "head"),
            P(("grp", "tok"), None, "head"),
            P(("grp", "tok"), None, "head"),
        ),
        out_specs=P("grp", "tok", "head"),
        check_vma=False,
    )
```

```python
import math

import jax
import jax.numpy as jnp
from jax import lax
from jax.experimental import pallas as pl
from jax.experimental.pallas import tpu as pltpu
from jax.sharding import PartitionSpec as P

ROPE_BASE = 500000.0
NORM_EPS = 1e-06
MASKED = -1e30
VMEM_LIMIT = 40 * 1024 * 1024


def shifted(block, axis, distance):
    devices = range(lax.axis_size(axis))
    route = [(i - distance, i) for i in devices if i - distance in devices]
    return lax.ppermute(block, axis, route)


def rms_norm(values_in, gain_vector):
    widened = values_in.astype(jnp.float32)
    mean_sq = jnp.mean(widened * widened, axis=-1, keepdims=True)
    return (widened * lax.rsqrt(mean_sq + NORM_EPS) * gain_vector.astype(jnp.float32)).astype(
        jnp.bfloat16
    )


def apply_rotary(product, token_positions):
    half_dim = product.shape[-1] // 2
    frequency = jnp.exp(
        jnp.arange(half_dim, dtype=jnp.float32) * (-2.0 * math.log(ROPE_BASE) / product.shape[-1])
    )
    angles = token_positions.astype(jnp.float32)[:, None] * frequency[None, :]
    cosine = jnp.cos(angles)[:, None, :]
    sine_part = jnp.sin(angles)[:, None, :]
    first_half = product[..., :half_dim]
    second_half = product[..., half_dim:]
    turned = jnp.concatenate(
        [
            first_half * cosine - second_half * sine_part,
            second_half * cosine + first_half * sine_part,
        ],
        axis=-1,
    )
    return turned.astype(jnp.bfloat16)


def turned_by(block, axis, distance):
    devices = lax.axis_size(axis)
    return lax.ppermute(block, axis, [(i, (i + distance) % devices) for i in range(devices)])


def along_ring(block, distance):
    devices = lax.axis_size("tok")
    order = list(range(0, devices, 2)) + list(range(devices - 1 - devices % 2, 0, -2))
    route = [(order[i], order[(i + distance) % devices]) for i in range(devices)]
    return lax.ppermute(block, "tok", route)


def ring_sum(parts, late):
    half = lax.axis_size("tok") // 2
    middle = parts[0].shape[1] // 2
    left = along_ring(parts[half][:, :middle].astype(jnp.bfloat16), -1)
    right = along_ring(parts[half][:, middle:].astype(jnp.bfloat16), 1)
    parts = {**parts, **late()}
    left, right, parts = lax.optimization_barrier((left, right, parts))
    left = parts[half - 1] + jnp.pad(
        left.astype(jnp.float32), ((0, 0), (0, parts[0].shape[1] - middle))
    )
    right = parts[1 - half] + jnp.pad(right.astype(jnp.float32), ((0, 0), (middle, 0)))
    for step in range(half - 2, -1, -1):
        left = along_ring(left.astype(jnp.bfloat16), -1).astype(jnp.float32)
        right = along_ring(right.astype(jnp.bfloat16), 1).astype(jnp.float32)
        if step:
            left = left + parts[step]
            right = right + parts[-step]
    return parts[0] + left + right


def side_by_side(block, axis):
    count = lax.axis_size(axis)
    rank = lax.axis_index(axis)
    blocks = others_over(block, axis)
    columns = []
    for place in range(count):
        column = blocks[0]
        for distance in range(1, count):
            column = jnp.where((rank - place) % count == distance, blocks[distance], column)
        columns.append(column)
    return jnp.concatenate(columns, axis=1)


def others_over(block, axis):
    return [block] + [turned_by(block, axis, d) for d in range(1, lax.axis_size(axis))]


def split_product(activations, blocks, axis):
    count = len(blocks)
    rank = lax.axis_index(axis)
    rows = blocks[0].shape[0]
    total = None
    for distance, block in enumerate(blocks):
        part = lax.dynamic_slice_in_dim(
            activations, ((rank - distance) % count) * rows, rows, 1
        )
        product = jnp.dot(part, block, preferred_element_type=jnp.float32)
        total = product if total is None else total + product
    return total


def width_tile(width, sizes):
    for size in sizes:
        if width % size == 0:
            return size
    return width


def picked_by(payload_ref, first_row, expert, experts, tok_dev, capacity):
    beside = payload_ref.shape[1] // tok_dev
    own = lax.broadcasted_iota(jnp.int32, (experts, tok_dev), 0) == expert

    def piece(i):
        rows = pl.ds(first_row + i // beside * experts, experts)
        columns = pl.ds(i % beside * tok_dev, tok_dev)
        values = payload_ref[rows, columns].astype(jnp.float32)
        return jnp.sum(jnp.where(own, values, 0.0), axis=0, keepdims=True)

    weight = piece(0) + piece(1) + piece(2)
    mask = piece(3)
    upto = lax.broadcasted_iota(jnp.int32, (tok_dev, tok_dev), 0) <= lax.broadcasted_iota(
        jnp.int32, (tok_dev, tok_dev), 1
    )
    upto = jnp.where(upto, 1.0, 0.0).astype(jnp.bfloat16)
    many = jnp.broadcast_to(mask, (16, tok_dev)).astype(jnp.bfloat16)
    place = jnp.dot(many, upto, preferred_element_type=jnp.float32)[0:1]
    place = jnp.where(mask > 0.5, place - 1.0, -1.0).astype(jnp.int32)
    slots = lax.broadcasted_iota(jnp.int32, (capacity, tok_dev), 0)
    pick = jnp.where(slots == place, 1.0, 0.0)
    return pick.astype(jnp.bfloat16), jnp.sum(pick * weight, axis=1, keepdims=True)


def payload_of(keys, values, ids, weights, experts):
    prefix_dev, kv_width = keys.shape
    tok_dev, top_count = ids.shape
    beside = 2 * kv_width // tok_dev
    rows = prefix_dev + 4 // beside * experts

    def body(keys_ref, values_ref, ids_ref, weights_ref, out_ref):
        out_ref[pl.ds(0, prefix_dev), pl.ds(0, kv_width)] = keys_ref[...]
        out_ref[pl.ds(0, prefix_dev), pl.ds(kv_width, kv_width)] = values_ref[...]
        lanes = lax.broadcasted_iota(jnp.int32, (tok_dev, 128), 1)
        dense = jnp.zeros((tok_dev, 128), jnp.float32)
        mask = jnp.zeros((tok_dev, 128), jnp.float32)
        for k in range(top_count):
            named = lanes == ids_ref[:, k : k + 1]
            dense = dense + jnp.where(named, weights_ref[:, k : k + 1], 0.0)
            mask = mask + jnp.where(named, 1.0, 0.0)
        rest = jnp.transpose(dense)[:experts]
        pieces = []
        for _ in range(3):
            pieces.append(rest.astype(jnp.bfloat16))
            rest = rest - pieces[-1].astype(jnp.float32)
        pieces.append(jnp.transpose(mask)[:experts].astype(jnp.bfloat16))
        for i, piece in enumerate(pieces):
            out_ref[
                pl.ds(prefix_dev + i // beside * experts, experts),
                pl.ds(i % beside * tok_dev, tok_dev),
            ] = piece

    return pl.pallas_call(
        body,
        out_shape=jax.ShapeDtypeStruct((rows, 2 * kv_width), jnp.bfloat16),
        name="payload",
    )(keys, values, ids, weights)


def attention(queries, suffix, payloads, prefix_dev, lengths, tok_rank, head_dim):
    tok_dev, query_width = queries.shape
    kv_width = suffix[0].shape[1] // 2
    kv_local = kv_width // head_dim
    group_length = query_width // kv_width
    requests = lengths.shape[0]
    prefix_rows = prefix_dev * len(payloads)
    keys_total = prefix_rows + tok_dev * len(suffix)

    def body(lengths_ref, rank_ref, query_ref, *refs):
        suffix_refs, refs = refs[: len(suffix)], refs[len(suffix) :]
        payload_refs, out_ref = refs[:-1], refs[-1]
        token = rank_ref[0] * tok_dev + lax.broadcasted_iota(jnp.int32, (tok_dev, tok_dev), 0)
        start = jnp.int32(0)
        own_start = jnp.zeros((tok_dev, tok_dev), jnp.int32)
        for request in range(requests):
            own_start = jnp.where(token >= start, jnp.maximum(own_start, start), own_start)
            start = start + lengths_ref[request]
        bias = [jnp.zeros((tok_dev, prefix_rows), jnp.float32)]
        for distance in range(len(suffix)):
            key = (rank_ref[0] - distance) * tok_dev + lax.broadcasted_iota(
                jnp.int32, (tok_dev, tok_dev), 1
            )
            bias.append(jnp.where((key >= own_start) & (key <= token), 0.0, MASKED))
        bias = jnp.concatenate(bias, axis=1)
        bias = jnp.concatenate([bias] * group_length, axis=0)
        for c in range(kv_local):
            columns = pl.ds(c * head_dim, head_dim)
            keys = jnp.concatenate(
                [ref[pl.ds(0, prefix_dev), columns] for ref in payload_refs]
                + [ref[:, columns] for ref in suffix_refs],
                axis=0,
            )
            columns = pl.ds(kv_width + c * head_dim, head_dim)
            values = jnp.concatenate(
                [ref[pl.ds(0, prefix_dev), columns] for ref in payload_refs]
                + [ref[:, columns] for ref in suffix_refs],
                axis=0,
            )
            first = c * group_length
            query = jnp.concatenate(
                [
                    query_ref[:, pl.ds((first + r) * head_dim, head_dim)]
                    for r in range(group_length)
                ],
                axis=0,
            )
            scores = lax.dot_general(
                query, keys, (((1,), (1,)), ((), ())), preferred_element_type=jnp.float32
            )
            scores = scores * head_dim ** (-0.5) + bias
            probs = jnp.exp(scores - jnp.max(scores, axis=1, keepdims=True))
            total = jnp.sum(probs, axis=1, keepdims=True)
            summed = jnp.dot(
                probs.astype(jnp.bfloat16), values, preferred_element_type=jnp.float32
            )
            attended = (summed / total).astype(jnp.bfloat16)
            for r in range(group_length):
                out_ref[:, pl.ds((first + r) * head_dim, head_dim)] = attended[
                    r * tok_dev : (r + 1) * tok_dev
                ]

    in_vmem = pl.BlockSpec(memory_space=pltpu.VMEM)
    in_smem = pl.BlockSpec(memory_space=pltpu.SMEM)
    return pl.pallas_call(
        body,
        out_shape=jax.ShapeDtypeStruct((tok_dev, query_width), jnp.bfloat16),
        in_specs=[in_smem] * 2 + [in_vmem] * (1 + len(suffix) + len(payloads)),
        out_specs=in_vmem,
        compiler_params=pltpu.CompilerParams(vmem_limit_bytes=VMEM_LIMIT),
        name="attention",
    )(lengths, tok_rank[None], queries, *suffix, *payloads)


def hidden_units(chosen, tables, first_row, blocks, gates, ups, experts, capacity):
    count, grp_count = len(blocks), len(gates)
    tok_dev = blocks[0][0].shape[0]
    model_width, hidden_width = gates[0].shape
    tile = width_tile(hidden_width, (256, 384, 128))
    steps = hidden_width // tile
    pieces = [len(block) for block in blocks]
    columns = sum(pieces)

    def body(chosen_ref, *refs):
        table_refs, refs = refs[:count], refs[count:]
        token_refs, refs = refs[:columns], refs[columns:]
        gate_refs, refs = refs[:grp_count], refs[grp_count:]
        up_refs, refs = refs[:grp_count], refs[grp_count:]
        out_ref, rows_ref = refs
        which, step = pl.program_id(0), pl.program_id(1)

        @pl.when((step == 0) & (which == 0))
        def _():
            at = 0
            for i in range(count):
                pick = jnp.concatenate(
                    [
                        picked_by(
                            table_refs[i], first_row, chosen_ref[g], experts, tok_dev, capacity
                        )[0]
                        for g in range(grp_count)
                    ],
                    axis=0,
                )
                first = 0
                for token_ref in token_refs[at : at + pieces[i]]:
                    width = token_ref.shape[1]
                    picked = jnp.dot(
                        pick, token_ref[...], preferred_element_type=jnp.float32
                    ).astype(jnp.bfloat16)
                    for g in range(grp_count):
                        rows_ref[g, pl.ds(i * capacity, capacity), pl.ds(first, width)] = picked[
                            g * capacity : (g + 1) * capacity
                        ]
                    first += width
                at += pieces[i]

        for g in range(grp_count):

            @pl.when(which == g)
            def _(g=g):
                rows = rows_ref[g]
                gate = jnp.dot(rows, gate_refs[g][...], preferred_element_type=jnp.float32)
                up = jnp.dot(rows, up_refs[g][...], preferred_element_type=jnp.float32)
                out_ref[0] = (gate / (1.0 + jnp.exp(-gate)) * up).astype(jnp.bfloat16)

    def whole(array):
        return pl.BlockSpec(array.shape, lambda e, n, ids: (0, 0))

    def weight_spec(g):
        def place(e, n, ids):
            return (0, jnp.where(e == g, n, jnp.where(e > g, steps - 1, 0)))

        return pl.BlockSpec((model_width, tile), place)

    flat = [part for block in blocks for part in block]
    specs = [whole(table) for table in tables] + [whole(part) for part in flat]
    specs += [weight_spec(g) for g in range(grp_count)] * 2
    return pl.pallas_call(
        body,
        out_shape=jax.ShapeDtypeStruct((grp_count, count * capacity, hidden_width), jnp.bfloat16),
        grid_spec=pltpu.PrefetchScalarGridSpec(
            num_scalar_prefetch=1,
            grid=(grp_count, steps),
            in_specs=specs,
            out_specs=pl.BlockSpec((1, count * capacity, tile), lambda e, n, ids: (e, 0, n)),
            scratch_shapes=[pltpu.VMEM((grp_count, count * capacity, model_width), jnp.bfloat16)],
        ),
        compiler_params=pltpu.CompilerParams(vmem_limit_bytes=VMEM_LIMIT),
        name="hidden_units",
    )(chosen, *tables, *flat, *gates, *ups)


def token_sums(chosen, tables, first_row, hiddens, downs, tok_dev, experts, capacity):
    count, grp_count, head_count = len(tables), len(downs), len(hiddens)
    rows_each = hiddens[0].shape[2]
    share_width = downs[0].shape[1]
    tile = width_tile(share_width, (256, 640))

    def body(chosen_ref, *refs):
        table_refs, refs = refs[:count], refs[count:]
        hidden_refs, refs = refs[:head_count], refs[head_count:]
        down_refs, refs = refs[:grp_count], refs[grp_count:]
        out_refs, (pick_ref, weight_ref, scaled_ref) = refs[:count], refs[count:]
        which = pl.program_id(1)
        rank = chosen_ref[grp_count]

        @pl.when((pl.program_id(0) == 0) & (which == 0))
        def _():
            for i in range(count):
                for g in range(grp_count):
                    pick, weight = picked_by(
                        table_refs[i], first_row, chosen_ref[g], experts, tok_dev, capacity
                    )
                    pick_ref[i, pl.ds(g * capacity, capacity), :] = pick
                    weight_ref[g, pl.ds(i * capacity, capacity), :] = weight

        for g in range(grp_count):

            @pl.when(which == g)
            def _(g=g):
                result = None
                for distance in range(head_count):
                    first = (rank - distance + head_count) % head_count * rows_each
                    down = down_refs[g][pl.ds(pl.multiple_of(first, rows_each), rows_each), :]
                    part = jnp.dot(
                        hidden_refs[distance][g], down, preferred_element_type=jnp.float32
                    )
                    result = part if result is None else result + part
                scaled = (result * weight_ref[g]).astype(jnp.bfloat16)
                for i in range(count):
                    scaled_ref[i, pl.ds(g * capacity, capacity), :] = scaled[
                        i * capacity : (i + 1) * capacity
                    ]
                if g == grp_count - 1:
                    for i in range(count):
                        out_refs[i][...] = lax.dot_general(
                            pick_ref[i],
                            scaled_ref[i],
                            (((0,), (0,)), ((), ())),
                            preferred_element_type=jnp.float32,
                        )

    specs = [pl.BlockSpec(table.shape, lambda n, e, ids: (0, 0)) for table in tables]
    specs += [pl.BlockSpec(hidden.shape, lambda n, e, ids: (0, 0, 0)) for hidden in hiddens]
    specs += [pl.BlockSpec((down.shape[0], tile), lambda n, e, ids: (0, n)) for down in downs]
    return pl.pallas_call(
        body,
        out_shape=[jax.ShapeDtypeStruct((tok_dev, share_width), jnp.float32)] * count,
        grid_spec=pltpu.PrefetchScalarGridSpec(
            num_scalar_prefetch=1,
            grid=(share_width // tile, grp_count),
            in_specs=specs,
            out_specs=[pl.BlockSpec((tok_dev, tile), lambda n, e, ids: (0, n))] * count,
            scratch_shapes=[
                pltpu.VMEM((count, grp_count * capacity, tok_dev), jnp.bfloat16),
                pltpu.VMEM((grp_count, count * capacity, 1), jnp.float32),
                pltpu.VMEM((count, grp_count * capacity, tile), jnp.bfloat16),
            ],
        ),
        compiler_params=pltpu.CompilerParams(vmem_limit_bytes=VMEM_LIMIT),
        name="token_sums",
    )(chosen, *tables, *hiddens, *downs)


def on_device(
    hidden_in,
    attn_gain,
    w_query,
    key_projection_weight,
    value_projection_weight,
    w_out,
    prefix_keys,
    cached_prefix_values,
    request_lengths,
    moe_gain,
    expert_ids,
    route_weights,
    w_gate,
    w_up,
    w_down,
):
    tok_count = lax.axis_size("tok")
    grp_count = lax.axis_size("grp")
    head_count = lax.axis_size("head")
    tok_rank = lax.axis_index("tok")
    grp_rank = lax.axis_index("grp")
    head_rank = lax.axis_index("head")
    tok_dev = hidden_in.shape[1]
    model_width = attn_gain.shape[0]
    head_dim = prefix_keys.shape[3]
    kv_local = prefix_keys.shape[2]
    kv_width = kv_local * head_dim
    group_length = w_query.shape[1] // kv_width
    prefix_total = prefix_keys.shape[1] * tok_count
    share_width = model_width // head_count
    experts = grp_count * tok_count
    top_count = expert_ids.shape[2]
    capacity = 4 * tok_dev * top_count // (3 * experts)

    quarter = hidden_in[0]
    features = side_by_side(quarter, "head")
    query_blocks = others_over(w_query, "grp")
    key_blocks = others_over(key_projection_weight, "grp")
    value_blocks = others_over(value_projection_weight, "grp")
    full_out = lax.all_gather(w_out, "grp", axis=0, tiled=True)

    payload = payload_of(
        prefix_keys[0].reshape(-1, kv_width),
        cached_prefix_values[0].reshape(-1, kv_width),
        expert_ids[0],
        route_weights[0],
        experts,
    )
    half_ring = tok_count // 2
    payloads = {0: payload}
    for distance in range(1, half_ring):
        payloads[distance] = along_ring(payload, distance)
        payloads[-distance] = along_ring(payload, -distance)
    payloads[half_ring] = along_ring(payload, half_ring)
    prefix_dev = prefix_keys.shape[1]

    gate_blocks = others_over(w_gate[0], "grp")
    up_blocks = others_over(w_up[0], "grp")
    down_blocks = others_over(w_down[0], "grp")

    attention_input = rms_norm(features, attn_gain)
    lengths = request_lengths[0]
    request_ends = jnp.cumsum(lengths)
    starts = request_ends - lengths
    token_index = tok_rank * tok_dev + jnp.arange(tok_dev, dtype=jnp.int32)
    own_start = jnp.max(
        jnp.where(starts[None, :] <= token_index[:, None], starts[None, :], 0), axis=1
    )
    token_positions = prefix_total + token_index - own_start
    key_product = split_product(attention_input, key_blocks, "grp")
    value_product = split_product(attention_input, value_blocks, "grp")
    query_product = split_product(attention_input, query_blocks, "grp")
    queries = apply_rotary(
        query_product.reshape(tok_dev, kv_local * group_length, head_dim), token_positions
    )
    queries = queries.reshape(tok_dev, kv_local * group_length * head_dim)
    request_suffix_keys = apply_rotary(
        key_product.reshape(tok_dev, kv_local, head_dim), token_positions
    )
    suffix = jnp.concatenate(
        [request_suffix_keys.reshape(tok_dev, kv_width), value_product.astype(jnp.bfloat16)], axis=1
    )
    longest = tok_dev * tok_count // 4
    reach_devices = (longest - 1 + tok_dev - 1) // tok_dev
    attended = attention(
        queries,
        [suffix] + [shifted(suffix, "tok", d) for d in range(1, reach_devices + 1)],
        list(payloads.values()),
        prefix_dev,
        lengths,
        tok_rank,
        head_dim,
    )
    partial_value = lax.dot_general(
        attended, full_out, (((1,), (1,)), ((), ())), preferred_element_type=jnp.float32
    )
    mixed = lax.dynamic_slice_in_dim(partial_value, head_rank * share_width, share_width, 1)
    for distance in range(1, head_count):
        target = (head_rank + distance) % head_count
        leaving = lax.dynamic_slice_in_dim(partial_value, target * share_width, share_width, 1)
        mixed = mixed + turned_by(leaving.astype(jnp.bfloat16), "head", distance).astype(jnp.float32)
    mid_quarter = (quarter.astype(jnp.float32) + mixed).astype(jnp.bfloat16)
    mid_full = lax.all_gather(mid_quarter, "head", axis=1, tiled=True)
    moe_in = rms_norm(mid_full, moe_gain)
    chosen = jnp.stack(
        [((grp_rank - d) % grp_count) * tok_count + tok_rank for d in range(grp_count)]
        + [head_rank]
    ).astype(jnp.int32)

    def units_of(chunk, blocks):
        tables = [payloads[d] for d in chunk]
        hidden = hidden_units(
            chosen, tables, prefix_dev, blocks, gate_blocks, up_blocks, experts, capacity
        )
        return hidden

    def sums_of(chunk, exchanged):
        tables = [payloads[d] for d in chunk]
        sums = token_sums(
            chosen, tables, prefix_dev, exchanged, down_blocks, tok_dev, experts, capacity
        )
        return dict(zip(chunk, sums))

    middle = model_width // 2
    ahead, behind = moe_in, moe_in
    chunk, blocks = [0], [[moe_in]]
    parts, waiting = {}, []
    for step in range(1, half_ring + 1):
        last = step == half_ring
        sent = (ahead[:, :middle], behind[:, middle:]) if last else (ahead, behind)
        arriving = (along_ring(sent[0], 1), along_ring(sent[1], -1))
        hidden = units_of(chunk, blocks)
        if waiting and not last:
            parts.update(sums_of(*waiting.pop(0)))
        (ahead, behind), hidden, parts = lax.optimization_barrier((arriving, hidden, parts))
        waiting.append((chunk, others_over(hidden, "head")))
        chunk = [half_ring] if last else [step, -step]
        blocks = [[ahead, behind]] if last else [[ahead], [behind]]
    exchanged = others_over(units_of(chunk, blocks), "head")
    parts.update(sums_of(*waiting.pop(0)))
    exchanged, parts = lax.optimization_barrier((exchanged, parts))
    parts.update(sums_of(chunk, exchanged))

    def late():
        own, arrived = waiting.pop(0)
        arrived, _ = lax.optimization_barrier((arrived, parts[half_ring]))
        return sums_of(own, arrived)

    weighted = ring_sum(parts, late)
    output = (mid_quarter.astype(jnp.float32) + weighted).astype(jnp.bfloat16)
    return output[None]


def solution(mesh):
    return jax.shard_map(
        on_device,
        mesh=mesh,
        in_specs=(
            P("grp", "tok", "head"),
            P(),
            P("grp", "head"),
            P("grp", "head"),
            P("grp", "head"),
            P("grp", "head"),
            P("grp", "tok", "head", None),
            P("grp", "tok", "head", None),
            P("grp", None),
            P(),
            P("grp", "tok", None),
            P("grp", "tok", None),
            P(("grp", "tok"), None, "head"),
            P(("grp", "tok"), None, "head"),
            P(("grp", "tok"), None, "head"),
        ),
        out_specs=P("grp", "tok", "head"),
        check_vma=False,
    )
```

```python
import math

import jax
import jax.numpy as jnp
from jax import lax
from jax.experimental import pallas as pl
from jax.experimental.pallas import tpu as pltpu
from jax.sharding import PartitionSpec as P

ROPE_BASE = 500000.0
NORM_EPS = 1e-06
MASKED = -1e30
VMEM_LIMIT = 40 * 1024 * 1024
SMALL_LIMIT = 14 * 1024 * 1024


def shifted(block, axis, distance):
    devices = range(lax.axis_size(axis))
    route = [(i - distance, i) for i in devices if i - distance in devices]
    return lax.ppermute(block, axis, route)


def rms_norm(values_in, gain_vector):
    widened = values_in.astype(jnp.float32)
    mean_sq = jnp.mean(widened * widened, axis=-1, keepdims=True)
    return (widened * lax.rsqrt(mean_sq + NORM_EPS) * gain_vector.astype(jnp.float32)).astype(
        jnp.bfloat16
    )


def apply_rotary(product, token_positions):
    half_dim = product.shape[-1] // 2
    frequency = jnp.exp(
        jnp.arange(half_dim, dtype=jnp.float32) * (-2.0 * math.log(ROPE_BASE) / product.shape[-1])
    )
    angles = token_positions.astype(jnp.float32)[:, None] * frequency[None, :]
    cosine = jnp.cos(angles)[:, None, :]
    sine_part = jnp.sin(angles)[:, None, :]
    first_half = product[..., :half_dim]
    second_half = product[..., half_dim:]
    turned = jnp.concatenate(
        [
            first_half * cosine - second_half * sine_part,
            second_half * cosine + first_half * sine_part,
        ],
        axis=-1,
    )
    return turned.astype(jnp.bfloat16)


def turned_by(block, axis, distance):
    devices = lax.axis_size(axis)
    return lax.ppermute(block, axis, [(i, (i + distance) % devices) for i in range(devices)])


def along_ring(block, distance):
    devices = lax.axis_size("tok")
    order = list(range(0, devices, 2)) + list(range(devices - 1 - devices % 2, 0, -2))
    route = [(order[i], order[(i + distance) % devices]) for i in range(devices)]
    return lax.ppermute(block, "tok", route)


def ring_sum(parts, late):
    half = lax.axis_size("tok") // 2
    middle = parts[0].shape[1] // 2
    left = along_ring(parts[half][:, :middle].astype(jnp.bfloat16), -1)
    right = along_ring(parts[half][:, middle:].astype(jnp.bfloat16), 1)
    parts = {**parts, **late()}
    left, right, parts = lax.optimization_barrier((left, right, parts))
    left = parts[half - 1] + jnp.pad(
        left.astype(jnp.float32), ((0, 0), (0, parts[0].shape[1] - middle))
    )
    right = parts[1 - half] + jnp.pad(right.astype(jnp.float32), ((0, 0), (middle, 0)))
    for step in range(half - 2, -1, -1):
        left = along_ring(left.astype(jnp.bfloat16), -1).astype(jnp.float32)
        right = along_ring(right.astype(jnp.bfloat16), 1).astype(jnp.float32)
        if step:
            left = left + parts[step]
            right = right + parts[-step]
    return parts[0] + left + right


def side_by_side(block, axis):
    count = lax.axis_size(axis)
    rank = lax.axis_index(axis)
    blocks = others_over(block, axis)
    columns = []
    for place in range(count):
        column = blocks[0]
        for distance in range(1, count):
            column = jnp.where((rank - place) % count == distance, blocks[distance], column)
        columns.append(column)
    return jnp.concatenate(columns, axis=1)


def others_over(block, axis):
    return [block] + [turned_by(block, axis, d) for d in range(1, lax.axis_size(axis))]


def split_product(activations, blocks, axis):
    count = len(blocks)
    rank = lax.axis_index(axis)
    rows = blocks[0].shape[0]
    total = None
    for distance, block in enumerate(blocks):
        part = lax.dynamic_slice_in_dim(
            activations, ((rank - distance) % count) * rows, rows, 1
        )
        product = jnp.dot(part, block, preferred_element_type=jnp.float32)
        total = product if total is None else total + product
    return total


def width_tile(width, sizes):
    for size in sizes:
        if width % size == 0:
            return size
    return width


def picked_by(payload_ref, first_row, expert, experts, tok_dev, capacity):
    beside = payload_ref.shape[1] // tok_dev
    own = lax.broadcasted_iota(jnp.int32, (experts, tok_dev), 0) == expert

    def piece(i):
        rows = pl.ds(first_row + i // beside * experts, experts)
        columns = pl.ds(i % beside * tok_dev, tok_dev)
        values = payload_ref[rows, columns].astype(jnp.float32)
        return jnp.sum(jnp.where(own, values, 0.0), axis=0, keepdims=True)

    weight = piece(0) + piece(1) + piece(2)
    mask = piece(3)
    upto = lax.broadcasted_iota(jnp.int32, (tok_dev, tok_dev), 0) <= lax.broadcasted_iota(
        jnp.int32, (tok_dev, tok_dev), 1
    )
    upto = jnp.where(upto, 1.0, 0.0).astype(jnp.bfloat16)
    many = jnp.broadcast_to(mask, (16, tok_dev)).astype(jnp.bfloat16)
    place = jnp.dot(many, upto, preferred_element_type=jnp.float32)[0:1]
    place = jnp.where(mask > 0.5, place - 1.0, -1.0).astype(jnp.int32)
    slots = lax.broadcasted_iota(jnp.int32, (capacity, tok_dev), 0)
    pick = jnp.where(slots == place, 1.0, 0.0)
    return pick.astype(jnp.bfloat16), jnp.sum(pick * weight, axis=1, keepdims=True)


def payload_of(keys, values, ids, weights, experts):
    prefix_dev, kv_width = keys.shape
    tok_dev, top_count = ids.shape
    beside = 2 * kv_width // tok_dev
    rows = prefix_dev + 4 // beside * experts

    def body(keys_ref, values_ref, ids_ref, weights_ref, out_ref):
        out_ref[pl.ds(0, prefix_dev), pl.ds(0, kv_width)] = keys_ref[...]
        out_ref[pl.ds(0, prefix_dev), pl.ds(kv_width, kv_width)] = values_ref[...]
        lanes = lax.broadcasted_iota(jnp.int32, (tok_dev, 128), 1)
        dense = jnp.zeros((tok_dev, 128), jnp.float32)
        mask = jnp.zeros((tok_dev, 128), jnp.float32)
        for k in range(top_count):
            named = lanes == ids_ref[:, k : k + 1]
            dense = dense + jnp.where(named, weights_ref[:, k : k + 1], 0.0)
            mask = mask + jnp.where(named, 1.0, 0.0)
        rest = jnp.transpose(dense)[:experts]
        pieces = []
        for _ in range(3):
            pieces.append(rest.astype(jnp.bfloat16))
            rest = rest - pieces[-1].astype(jnp.float32)
        pieces.append(jnp.transpose(mask)[:experts].astype(jnp.bfloat16))
        for i, piece in enumerate(pieces):
            out_ref[
                pl.ds(prefix_dev + i // beside * experts, experts),
                pl.ds(i % beside * tok_dev, tok_dev),
            ] = piece

    return pl.pallas_call(
        body,
        out_shape=jax.ShapeDtypeStruct((rows, 2 * kv_width), jnp.bfloat16),
        name="payload",
    )(keys, values, ids, weights)


def attention(queries, suffix, payloads, prefix_dev, lengths, tok_rank, head_dim):
    tok_dev, query_width = queries.shape
    kv_width = suffix[0].shape[1] // 2
    kv_local = kv_width // head_dim
    group_length = query_width // kv_width
    requests = lengths.shape[0]
    prefix_rows = prefix_dev * len(payloads)
    keys_total = prefix_rows + tok_dev * len(suffix)

    def body(lengths_ref, rank_ref, query_ref, *refs):
        suffix_refs, refs = refs[: len(suffix)], refs[len(suffix) :]
        payload_refs, out_ref = refs[:-1], refs[-1]
        token = rank_ref[0] * tok_dev + lax.broadcasted_iota(jnp.int32, (tok_dev, tok_dev), 0)
        start = jnp.int32(0)
        own_start = jnp.zeros((tok_dev, tok_dev), jnp.int32)
        for request in range(requests):
            own_start = jnp.where(token >= start, jnp.maximum(own_start, start), own_start)
            start = start + lengths_ref[request]
        bias = [jnp.zeros((tok_dev, prefix_rows), jnp.float32)]
        for distance in range(len(suffix)):
            key = (rank_ref[0] - distance) * tok_dev + lax.broadcasted_iota(
                jnp.int32, (tok_dev, tok_dev), 1
            )
            bias.append(jnp.where((key >= own_start) & (key <= token), 0.0, MASKED))
        bias = jnp.concatenate(bias, axis=1)
        bias = jnp.concatenate([bias] * group_length, axis=0)
        for c in range(kv_local):
            columns = pl.ds(c * head_dim, head_dim)
            keys = jnp.concatenate(
                [ref[pl.ds(0, prefix_dev), columns] for ref in payload_refs]
                + [ref[:, columns] for ref in suffix_refs],
                axis=0,
            )
            columns = pl.ds(kv_width + c * head_dim, head_dim)
            values = jnp.concatenate(
                [ref[pl.ds(0, prefix_dev), columns] for ref in payload_refs]
                + [ref[:, columns] for ref in suffix_refs],
                axis=0,
            )
            first = c * group_length
            query = jnp.concatenate(
                [
                    query_ref[:, pl.ds((first + r) * head_dim, head_dim)]
                    for r in range(group_length)
                ],
                axis=0,
            )
            scores = lax.dot_general(
                query, keys, (((1,), (1,)), ((), ())), preferred_element_type=jnp.float32
            )
            scores = scores * head_dim ** (-0.5) + bias
            probs = jnp.exp(scores - jnp.max(scores, axis=1, keepdims=True))
            total = jnp.sum(probs, axis=1, keepdims=True)
            summed = jnp.dot(
                probs.astype(jnp.bfloat16), values, preferred_element_type=jnp.float32
            )
            attended = (summed / total).astype(jnp.bfloat16)
            for r in range(group_length):
                out_ref[:, pl.ds((first + r) * head_dim, head_dim)] = attended[
                    r * tok_dev : (r + 1) * tok_dev
                ]

    in_vmem = pl.BlockSpec(memory_space=pltpu.VMEM)
    in_smem = pl.BlockSpec(memory_space=pltpu.SMEM)
    return pl.pallas_call(
        body,
        out_shape=jax.ShapeDtypeStruct((tok_dev, query_width), jnp.bfloat16),
        in_specs=[in_smem] * 2 + [in_vmem] * (1 + len(suffix) + len(payloads)),
        out_specs=in_vmem,
        compiler_params=pltpu.CompilerParams(vmem_limit_bytes=VMEM_LIMIT),
        name="attention",
    )(lengths, tok_rank[None], queries, *suffix, *payloads)


def slots_of(chosen, payloads, first_row, grp_count, tok_dev, experts, capacity):
    count = len(payloads)

    def body(chosen_ref, *refs):
        payload_refs, (pick_ref, weight_ref) = refs[:count], refs[count:]
        for i in range(count):
            for g in range(grp_count):
                pick, weight = picked_by(
                    payload_refs[i], first_row, chosen_ref[g], experts, tok_dev, capacity
                )
                pick_ref[i, pl.ds(g * capacity, capacity), :] = pick
                weight_ref[i, pl.ds(g * capacity, capacity), :] = jnp.broadcast_to(
                    weight, (capacity, 128)
                )

    in_vmem = pl.BlockSpec(memory_space=pltpu.VMEM)
    slots = grp_count * capacity
    return pl.pallas_call(
        body,
        out_shape=[
            jax.ShapeDtypeStruct((count, slots, tok_dev), jnp.bfloat16),
            jax.ShapeDtypeStruct((count, slots, 128), jnp.float32),
        ],
        in_specs=[pl.BlockSpec(memory_space=pltpu.SMEM)] + [in_vmem] * count,
        out_specs=[in_vmem] * 2,
        compiler_params=pltpu.CompilerParams(vmem_limit_bytes=SMALL_LIMIT),
        name="slots",
    )(chosen, *payloads)


def hidden_units(picks, places, blocks, gates, ups, capacity):
    count, grp_count = len(blocks), len(gates)
    model_width, hidden_width = gates[0].shape
    tile = width_tile(hidden_width, (256, 384, 128))
    pieces = [len(block) for block in blocks]
    columns = sum(pieces)

    def body(pick_ref, *refs):
        token_refs, refs = refs[:columns], refs[columns:]
        gate_refs, refs = refs[:grp_count], refs[grp_count:]
        up_refs, refs = refs[:grp_count], refs[grp_count:]
        out_ref, rows_ref = refs
        at = 0
        for i in range(count):
            pick = pick_ref[places[i]]
            first = 0
            for token_ref in token_refs[at : at + pieces[i]]:
                width = token_ref.shape[1]
                picked = jnp.dot(
                    pick, token_ref[...], preferred_element_type=jnp.float32
                ).astype(jnp.bfloat16)
                for g in range(grp_count):
                    rows_ref[g, pl.ds(i * capacity, capacity), pl.ds(first, width)] = picked[
                        g * capacity : (g + 1) * capacity
                    ]
                first += width
            at += pieces[i]
        for g in range(grp_count):
            for n in range(0, hidden_width, tile):
                own = pl.ds(n, tile)
                gate = jnp.dot(
                    rows_ref[g], gate_refs[g][:, own], preferred_element_type=jnp.float32
                )
                up = jnp.dot(rows_ref[g], up_refs[g][:, own], preferred_element_type=jnp.float32)
                out_ref[g, :, own] = (gate / (1.0 + jnp.exp(-gate)) * up).astype(jnp.bfloat16)

    in_vmem = pl.BlockSpec(memory_space=pltpu.VMEM)
    flat = [part for block in blocks for part in block]
    return pl.pallas_call(
        body,
        out_shape=jax.ShapeDtypeStruct((grp_count, count * capacity, hidden_width), jnp.bfloat16),
        in_specs=[in_vmem] * (1 + columns + 2 * grp_count),
        out_specs=in_vmem,
        scratch_shapes=[pltpu.VMEM((grp_count, count * capacity, model_width), jnp.bfloat16)],
        compiler_params=pltpu.CompilerParams(vmem_limit_bytes=SMALL_LIMIT),
        name="hidden_units",
    )(picks, *flat, *gates, *ups)


def token_sums(rank, picks, weights, places, hiddens, downs, tok_dev, capacity):
    count, grp_count, head_count = len(places), len(downs), len(hiddens)
    rows_each = hiddens[0].shape[2]
    share_width = downs[0].shape[1]
    tile = width_tile(share_width, (256, 640))

    def body(rank_ref, pick_ref, weight_ref, *refs):
        hidden_refs, refs = refs[:head_count], refs[head_count:]
        down_refs, out_refs = refs[:grp_count], refs[grp_count:]
        firsts = [
            pl.multiple_of((rank_ref[0] - k + head_count) % head_count * rows_each, rows_each)
            for k in range(head_count)
        ]
        for n in range(0, share_width, tile):
            own = pl.ds(n, tile)
            results = []
            for g in range(grp_count):
                result = None
                for k in range(head_count):
                    part = jnp.dot(
                        hidden_refs[k][g],
                        down_refs[g][pl.ds(firsts[k], rows_each), own],
                        preferred_element_type=jnp.float32,
                    )
                    result = part if result is None else result + part
                results.append(result)
            for i in range(count):
                scaled = jnp.concatenate(
                    [result[i * capacity : (i + 1) * capacity] for result in results], axis=0
                )
                scaled = (scaled * weight_ref[places[i], :, 0:1]).astype(jnp.bfloat16)
                out_refs[i][:, own] = lax.dot_general(
                    pick_ref[places[i]],
                    scaled,
                    (((0,), (0,)), ((), ())),
                    preferred_element_type=jnp.float32,
                )

    in_vmem = pl.BlockSpec(memory_space=pltpu.VMEM)
    return pl.pallas_call(
        body,
        out_shape=[jax.ShapeDtypeStruct((tok_dev, share_width), jnp.float32)] * count,
        in_specs=[pl.BlockSpec(memory_space=pltpu.SMEM)]
        + [in_vmem] * (2 + head_count + grp_count),
        out_specs=[in_vmem] * count,
        compiler_params=pltpu.CompilerParams(vmem_limit_bytes=SMALL_LIMIT),
        name="token_sums",
    )(rank, picks, weights, *hiddens, *downs)


def on_device(
    hidden_in,
    attn_gain,
    w_query,
    key_projection_weight,
    value_projection_weight,
    w_out,
    prefix_keys,
    cached_prefix_values,
    request_lengths,
    moe_gain,
    expert_ids,
    route_weights,
    w_gate,
    w_up,
    w_down,
):
    tok_count = lax.axis_size("tok")
    grp_count = lax.axis_size("grp")
    head_count = lax.axis_size("head")
    tok_rank = lax.axis_index("tok")
    grp_rank = lax.axis_index("grp")
    head_rank = lax.axis_index("head")
    tok_dev = hidden_in.shape[1]
    model_width = attn_gain.shape[0]
    head_dim = prefix_keys.shape[3]
    kv_local = prefix_keys.shape[2]
    kv_width = kv_local * head_dim
    group_length = w_query.shape[1] // kv_width
    prefix_total = prefix_keys.shape[1] * tok_count
    share_width = model_width // head_count
    experts = grp_count * tok_count
    top_count = expert_ids.shape[2]
    capacity = 4 * tok_dev * top_count // (3 * experts)

    quarter = hidden_in[0]
    features = side_by_side(quarter, "head")
    query_blocks = others_over(w_query, "grp")
    key_blocks = others_over(key_projection_weight, "grp")
    value_blocks = others_over(value_projection_weight, "grp")
    full_out = lax.all_gather(w_out, "grp", axis=0, tiled=True)

    payload = payload_of(
        prefix_keys[0].reshape(-1, kv_width),
        cached_prefix_values[0].reshape(-1, kv_width),
        expert_ids[0],
        route_weights[0],
        experts,
    )
    half_ring = tok_count // 2
    payloads = {0: payload}
    for distance in range(1, half_ring):
        payloads[distance] = along_ring(payload, distance)
        payloads[-distance] = along_ring(payload, -distance)
    payloads[half_ring] = along_ring(payload, half_ring)
    prefix_dev = prefix_keys.shape[1]

    gate_blocks = others_over(w_gate[0], "grp")
    up_blocks = others_over(w_up[0], "grp")
    down_blocks = others_over(w_down[0], "grp")

    attention_input = rms_norm(features, attn_gain)
    lengths = request_lengths[0]
    request_ends = jnp.cumsum(lengths)
    starts = request_ends - lengths
    token_index = tok_rank * tok_dev + jnp.arange(tok_dev, dtype=jnp.int32)
    own_start = jnp.max(
        jnp.where(starts[None, :] <= token_index[:, None], starts[None, :], 0), axis=1
    )
    token_positions = prefix_total + token_index - own_start
    key_product = split_product(attention_input, key_blocks, "grp")
    value_product = split_product(attention_input, value_blocks, "grp")
    query_product = split_product(attention_input, query_blocks, "grp")
    queries = apply_rotary(
        query_product.reshape(tok_dev, kv_local * group_length, head_dim), token_positions
    )
    queries = queries.reshape(tok_dev, kv_local * group_length * head_dim)
    request_suffix_keys = apply_rotary(
        key_product.reshape(tok_dev, kv_local, head_dim), token_positions
    )
    suffix = jnp.concatenate(
        [request_suffix_keys.reshape(tok_dev, kv_width), value_product.astype(jnp.bfloat16)], axis=1
    )
    longest = tok_dev * tok_count // 4
    reach_devices = (longest - 1 + tok_dev - 1) // tok_dev
    attended = attention(
        queries,
        [suffix] + [shifted(suffix, "tok", d) for d in range(1, reach_devices + 1)],
        list(payloads.values()),
        prefix_dev,
        lengths,
        tok_rank,
        head_dim,
    )
    partial_value = lax.dot_general(
        attended, full_out, (((1,), (1,)), ((), ())), preferred_element_type=jnp.float32
    )
    mixed = lax.dynamic_slice_in_dim(partial_value, head_rank * share_width, share_width, 1)
    for distance in range(1, head_count):
        target = (head_rank + distance) % head_count
        leaving = lax.dynamic_slice_in_dim(partial_value, target * share_width, share_width, 1)
        mixed = mixed + turned_by(leaving.astype(jnp.bfloat16), "head", distance).astype(jnp.float32)
    mid_quarter = (quarter.astype(jnp.float32) + mixed).astype(jnp.bfloat16)
    mid_full = lax.all_gather(mid_quarter, "head", axis=1, tiled=True)
    moe_in = rms_norm(mid_full, moe_gain)
    chosen = jnp.stack(
        [((grp_rank - d) % grp_count) * tok_count + tok_rank for d in range(grp_count)]
    ).astype(jnp.int32)
    place_of = {d: i for i, d in enumerate(payloads)}
    picks, slot_weights = slots_of(
        chosen, list(payloads.values()), prefix_dev, grp_count, tok_dev, experts, capacity
    )

    def units_of(chunk, blocks):
        places = [place_of[d] for d in chunk]
        return hidden_units(picks, places, blocks, gate_blocks, up_blocks, capacity)

    def sums_of(chunk, exchanged):
        places = [place_of[d] for d in chunk]
        sums = token_sums(
            head_rank[None], picks, slot_weights, places, exchanged, down_blocks, tok_dev, capacity
        )
        return dict(zip(chunk, sums))

    middle = model_width // 2
    ahead, behind = moe_in, moe_in
    chunk, blocks = [0], [[moe_in]]
    parts, waiting = {}, []
    for step in range(1, half_ring + 1):
        last = step == half_ring
        sent = (ahead[:, :middle], behind[:, middle:]) if last else (ahead, behind)
        arriving = (along_ring(sent[0], 1), along_ring(sent[1], -1))
        hidden = units_of(chunk, blocks)
        if waiting and not last:
            parts.update(sums_of(*waiting.pop(0)))
        (ahead, behind), hidden, parts = lax.optimization_barrier((arriving, hidden, parts))
        waiting.append((chunk, others_over(hidden, "head")))
        chunk = [half_ring] if last else [step, -step]
        blocks = [[ahead, behind]] if last else [[ahead], [behind]]
    exchanged = others_over(units_of(chunk, blocks), "head")
    parts.update(sums_of(*waiting.pop(0)))
    exchanged, parts = lax.optimization_barrier((exchanged, parts))
    parts.update(sums_of(chunk, exchanged))

    def late():
        own, arrived = waiting.pop(0)
        arrived, _ = lax.optimization_barrier((arrived, parts[half_ring]))
        return sums_of(own, arrived)

    weighted = ring_sum(parts, late)
    output = (mid_quarter.astype(jnp.float32) + weighted).astype(jnp.bfloat16)
    return output[None]


def solution(mesh):
    return jax.shard_map(
        on_device,
        mesh=mesh,
        in_specs=(
            P("grp", "tok", "head"),
            P(),
            P("grp", "head"),
            P("grp", "head"),
            P("grp", "head"),
            P("grp", "head"),
            P("grp", "tok", "head", None),
            P("grp", "tok", "head", None),
            P("grp", None),
            P(),
            P("grp", "tok", None),
            P("grp", "tok", None),
            P(("grp", "tok"), None, "head"),
            P(("grp", "tok"), None, "head"),
            P(("grp", "tok"), None, "head"),
        ),
        out_specs=P("grp", "tok", "head"),
        check_vma=False,
    )
```

```python
import math

import jax
import jax.numpy as jnp
from jax import lax
from jax.experimental import pallas as pl
from jax.experimental.pallas import tpu as pltpu
from jax.sharding import PartitionSpec as P

ROPE_BASE = 500000.0
NORM_EPS = 1e-06
MASKED = -1e30
VMEM_LIMIT = 40 * 1024 * 1024
SMALL_LIMIT = 18 * 1024 * 1024


def shifted(block, axis, distance):
    devices = range(lax.axis_size(axis))
    route = [(i - distance, i) for i in devices if i - distance in devices]
    return lax.ppermute(block, axis, route)


def rms_norm(values_in, gain_vector):
    widened = values_in.astype(jnp.float32)
    mean_sq = jnp.mean(widened * widened, axis=-1, keepdims=True)
    return (widened * lax.rsqrt(mean_sq + NORM_EPS) * gain_vector.astype(jnp.float32)).astype(
        jnp.bfloat16
    )


def apply_rotary(product, token_positions):
    half_dim = product.shape[-1] // 2
    frequency = jnp.exp(
        jnp.arange(half_dim, dtype=jnp.float32) * (-2.0 * math.log(ROPE_BASE) / product.shape[-1])
    )
    angles = token_positions.astype(jnp.float32)[:, None] * frequency[None, :]
    cosine = jnp.cos(angles)[:, None, :]
    sine_part = jnp.sin(angles)[:, None, :]
    first_half = product[..., :half_dim]
    second_half = product[..., half_dim:]
    turned = jnp.concatenate(
        [
            first_half * cosine - second_half * sine_part,
            second_half * cosine + first_half * sine_part,
        ],
        axis=-1,
    )
    return turned.astype(jnp.bfloat16)


def turned_by(block, axis, distance):
    devices = lax.axis_size(axis)
    return lax.ppermute(block, axis, [(i, (i + distance) % devices) for i in range(devices)])


def along_ring(block, distance):
    devices = lax.axis_size("tok")
    order = list(range(0, devices, 2)) + list(range(devices - 1 - devices % 2, 0, -2))
    route = [(order[i], order[(i + distance) % devices]) for i in range(devices)]
    return lax.ppermute(block, "tok", route)


def ring_sum(parts, late):
    half = lax.axis_size("tok") // 2
    middle = parts[half].shape[1] // 2
    left, right = parts[half][:, :middle], parts[half][:, middle:]
    for step in range(half - 1, -1, -1):
        left = along_ring(left.astype(jnp.bfloat16), -1)
        right = along_ring(right.astype(jnp.bfloat16), 1)
        if late:
            left, right, more = lax.optimization_barrier((left, right, late.pop(0)()))
            parts = {**parts, **more}
        left, right = left.astype(jnp.float32), right.astype(jnp.float32)
        if step == half - 1:
            left = jnp.pad(left, ((0, 0), (0, middle)))
            right = jnp.pad(right, ((0, 0), (middle, 0)))
        if step:
            left, right = parts[step] + left, parts[-step] + right
    return parts[0] + left + right


def side_by_side(block, axis):
    count = lax.axis_size(axis)
    rank = lax.axis_index(axis)
    blocks = others_over(block, axis)
    columns = []
    for place in range(count):
        column = blocks[0]
        for distance in range(1, count):
            column = jnp.where((rank - place) % count == distance, blocks[distance], column)
        columns.append(column)
    return jnp.concatenate(columns, axis=1)


def others_over(block, axis):
    return [block] + [turned_by(block, axis, d) for d in range(1, lax.axis_size(axis))]


def split_product(activations, blocks, axis):
    count = len(blocks)
    rank = lax.axis_index(axis)
    rows = blocks[0].shape[0]
    total = None
    for distance, block in enumerate(blocks):
        part = lax.dynamic_slice_in_dim(
            activations, ((rank - distance) % count) * rows, rows, 1
        )
        product = jnp.dot(part, block, preferred_element_type=jnp.float32)
        total = product if total is None else total + product
    return total


def width_tile(width, sizes):
    for size in sizes:
        if width % size == 0:
            return size
    return width


def picked_by(payload_ref, first_row, expert, experts, tok_dev, capacity):
    beside = payload_ref.shape[1] // tok_dev
    own = lax.broadcasted_iota(jnp.int32, (experts, tok_dev), 0) == expert

    def piece(i):
        rows = pl.ds(first_row + i // beside * experts, experts)
        columns = pl.ds(i % beside * tok_dev, tok_dev)
        values = payload_ref[rows, columns].astype(jnp.float32)
        return jnp.sum(jnp.where(own, values, 0.0), axis=0, keepdims=True)

    weight = piece(0) + piece(1) + piece(2)
    mask = piece(3)
    upto = lax.broadcasted_iota(jnp.int32, (tok_dev, tok_dev), 0) <= lax.broadcasted_iota(
        jnp.int32, (tok_dev, tok_dev), 1
    )
    upto = jnp.where(upto, 1.0, 0.0).astype(jnp.bfloat16)
    many = jnp.broadcast_to(mask, (16, tok_dev)).astype(jnp.bfloat16)
    place = jnp.dot(many, upto, preferred_element_type=jnp.float32)[0:1]
    place = jnp.where(mask > 0.5, place - 1.0, -1.0).astype(jnp.int32)
    slots = lax.broadcasted_iota(jnp.int32, (capacity, tok_dev), 0)
    pick = jnp.where(slots == place, 1.0, 0.0)
    return pick.astype(jnp.bfloat16), jnp.sum(pick * weight, axis=1, keepdims=True)


def payload_of(keys, values, ids, weights, experts):
    prefix_dev, kv_width = keys.shape
    tok_dev, top_count = ids.shape
    beside = 2 * kv_width // tok_dev
    rows = prefix_dev + 4 // beside * experts

    def body(keys_ref, values_ref, ids_ref, weights_ref, out_ref):
        out_ref[pl.ds(0, prefix_dev), pl.ds(0, kv_width)] = keys_ref[...]
        out_ref[pl.ds(0, prefix_dev), pl.ds(kv_width, kv_width)] = values_ref[...]
        lanes = lax.broadcasted_iota(jnp.int32, (tok_dev, 128), 1)
        dense = jnp.zeros((tok_dev, 128), jnp.float32)
        mask = jnp.zeros((tok_dev, 128), jnp.float32)
        for k in range(top_count):
            named = lanes == ids_ref[:, k : k + 1]
            dense = dense + jnp.where(named, weights_ref[:, k : k + 1], 0.0)
            mask = mask + jnp.where(named, 1.0, 0.0)
        rest = jnp.transpose(dense)[:experts]
        pieces = []
        for _ in range(3):
            pieces.append(rest.astype(jnp.bfloat16))
            rest = rest - pieces[-1].astype(jnp.float32)
        pieces.append(jnp.transpose(mask)[:experts].astype(jnp.bfloat16))
        for i, piece in enumerate(pieces):
            out_ref[
                pl.ds(prefix_dev + i // beside * experts, experts),
                pl.ds(i % beside * tok_dev, tok_dev),
            ] = piece

    return pl.pallas_call(
        body,
        out_shape=jax.ShapeDtypeStruct((rows, 2 * kv_width), jnp.bfloat16),
        name="payload",
    )(keys, values, ids, weights)


def attention(queries, suffix, payloads, prefix_dev, lengths, tok_rank, head_dim):
    tok_dev, query_width = queries.shape
    kv_width = suffix[0].shape[1] // 2
    kv_local = kv_width // head_dim
    group_length = query_width // kv_width
    requests = lengths.shape[0]
    prefix_rows = prefix_dev * len(payloads)
    keys_total = prefix_rows + tok_dev * len(suffix)

    def body(lengths_ref, rank_ref, query_ref, *refs):
        suffix_refs, refs = refs[: len(suffix)], refs[len(suffix) :]
        payload_refs, out_ref = refs[:-1], refs[-1]
        token = rank_ref[0] * tok_dev + lax.broadcasted_iota(jnp.int32, (tok_dev, tok_dev), 0)
        start = jnp.int32(0)
        own_start = jnp.zeros((tok_dev, tok_dev), jnp.int32)
        for request in range(requests):
            own_start = jnp.where(token >= start, jnp.maximum(own_start, start), own_start)
            start = start + lengths_ref[request]
        bias = [jnp.zeros((tok_dev, prefix_rows), jnp.float32)]
        for distance in range(len(suffix)):
            key = (rank_ref[0] - distance) * tok_dev + lax.broadcasted_iota(
                jnp.int32, (tok_dev, tok_dev), 1
            )
            bias.append(jnp.where((key >= own_start) & (key <= token), 0.0, MASKED))
        bias = jnp.concatenate(bias, axis=1)
        bias = jnp.concatenate([bias] * group_length, axis=0)
        for c in range(kv_local):
            columns = pl.ds(c * head_dim, head_dim)
            keys = jnp.concatenate(
                [ref[pl.ds(0, prefix_dev), columns] for ref in payload_refs]
                + [ref[:, columns] for ref in suffix_refs],
                axis=0,
            )
            columns = pl.ds(kv_width + c * head_dim, head_dim)
            values = jnp.concatenate(
                [ref[pl.ds(0, prefix_dev), columns] for ref in payload_refs]
                + [ref[:, columns] for ref in suffix_refs],
                axis=0,
            )
            first = c * group_length
            query = jnp.concatenate(
                [
                    query_ref[:, pl.ds((first + r) * head_dim, head_dim)]
                    for r in range(group_length)
                ],
                axis=0,
            )
            scores = lax.dot_general(
                query, keys, (((1,), (1,)), ((), ())), preferred_element_type=jnp.float32
            )
            scores = scores * head_dim ** (-0.5) + bias
            probs = jnp.exp(scores - jnp.max(scores, axis=1, keepdims=True))
            total = jnp.sum(probs, axis=1, keepdims=True)
            summed = jnp.dot(
                probs.astype(jnp.bfloat16), values, preferred_element_type=jnp.float32
            )
            attended = (summed / total).astype(jnp.bfloat16)
            for r in range(group_length):
                out_ref[:, pl.ds((first + r) * head_dim, head_dim)] = attended[
                    r * tok_dev : (r + 1) * tok_dev
                ]

    in_vmem = pl.BlockSpec(memory_space=pltpu.VMEM)
    in_smem = pl.BlockSpec(memory_space=pltpu.SMEM)
    return pl.pallas_call(
        body,
        out_shape=jax.ShapeDtypeStruct((tok_dev, query_width), jnp.bfloat16),
        in_specs=[in_smem] * 2 + [in_vmem] * (1 + len(suffix) + len(payloads)),
        out_specs=in_vmem,
        compiler_params=pltpu.CompilerParams(vmem_limit_bytes=VMEM_LIMIT),
        name="attention",
    )(lengths, tok_rank[None], queries, *suffix, *payloads)


def slots_of(chosen, payloads, first_row, grp_count, tok_dev, experts, capacity):
    count = len(payloads)

    def body(chosen_ref, *refs):
        payload_refs, (pick_ref, weight_ref) = refs[:count], refs[count:]
        for i in range(count):
            for g in range(grp_count):
                pick, weight = picked_by(
                    payload_refs[i], first_row, chosen_ref[g], experts, tok_dev, capacity
                )
                pick_ref[i, pl.ds(g * capacity, capacity), :] = pick
                weight_ref[i, pl.ds(g * capacity, capacity), :] = jnp.broadcast_to(
                    weight, (capacity, 128)
                )

    in_vmem = pl.BlockSpec(memory_space=pltpu.VMEM)
    slots = grp_count * capacity
    return pl.pallas_call(
        body,
        out_shape=[
            jax.ShapeDtypeStruct((count, slots, tok_dev), jnp.bfloat16),
            jax.ShapeDtypeStruct((count, slots, 128), jnp.float32),
        ],
        in_specs=[pl.BlockSpec(memory_space=pltpu.SMEM)] + [in_vmem] * count,
        out_specs=[in_vmem] * 2,
        compiler_params=pltpu.CompilerParams(vmem_limit_bytes=SMALL_LIMIT),
        name="slots",
    )(chosen, *payloads)


def hidden_units(rank, picks, places, blocks, gain, gates, ups, capacity):
    count, grp_count = len(blocks), len(gates)
    model_width, hidden_width = gates[0].shape
    head_count = len(blocks[0])
    share = blocks[0][0].shape[1]
    tile = width_tile(hidden_width, (256, 384, 128))

    def body(rank_ref, pick_ref, gain_ref, *refs):
        token_refs, refs = refs[: count * head_count], refs[count * head_count :]
        gate_refs, refs = refs[:grp_count], refs[grp_count:]
        up_refs, refs = refs[:grp_count], refs[grp_count:]
        out_ref, rows_ref, picked_ref = refs
        shares = [(rank_ref[0] - d + head_count) % head_count for d in range(head_count)]
        firsts = [pl.multiple_of(place * share, share) for place in shares]
        for i in range(count):
            pick = pick_ref[places[i]]
            total = None
            for d in range(head_count):
                piece = jnp.dot(
                    pick, token_refs[i * head_count + d][...], preferred_element_type=jnp.float32
                )
                picked_ref[d] = piece
                part = jnp.sum(piece * piece, axis=1, keepdims=True)
                total = part if total is None else total + part
            scale = lax.rsqrt(total / model_width + NORM_EPS)
            for d in range(head_count):
                rows = (picked_ref[d] * scale * gain_ref[shares[d]]).astype(jnp.bfloat16)
                for g in range(grp_count):
                    rows_ref[g, d, pl.ds(i * capacity, capacity), :] = rows[
                        g * capacity : (g + 1) * capacity
                    ]
        for g in range(grp_count):
            for n in range(0, hidden_width, tile):
                own = pl.ds(n, tile)
                acts = []
                for ref in (gate_refs[g], up_refs[g]):
                    act = None
                    for d in range(head_count):
                        part = jnp.dot(
                            rows_ref[g, d],
                            ref[pl.ds(firsts[d], share), own],
                            preferred_element_type=jnp.float32,
                        )
                        act = part if act is None else act + part
                    acts.append(act)
                gate, up = acts
                out_ref[g, :, own] = (gate / (1.0 + jnp.exp(-gate)) * up).astype(jnp.bfloat16)

    in_vmem = pl.BlockSpec(memory_space=pltpu.VMEM)
    flat = [piece for block in blocks for piece in block]
    return pl.pallas_call(
        body,
        out_shape=jax.ShapeDtypeStruct((grp_count, count * capacity, hidden_width), jnp.bfloat16),
        in_specs=[pl.BlockSpec(memory_space=pltpu.SMEM)]
        + [in_vmem] * (2 + len(flat) + 2 * grp_count),
        out_specs=in_vmem,
        scratch_shapes=[
            pltpu.VMEM((grp_count, head_count, count * capacity, share), jnp.bfloat16),
            pltpu.VMEM((head_count, grp_count * capacity, share), jnp.float32),
        ],
        compiler_params=pltpu.CompilerParams(vmem_limit_bytes=SMALL_LIMIT),
        name="hidden_units",
    )(rank, picks, gain, *flat, *gates, *ups)


def token_sums(rank, picks, weights, places, hiddens, downs, tok_dev, capacity):
    count, grp_count, head_count = len(places), len(downs), len(hiddens)
    rows_each = hiddens[0].shape[2]
    share_width = downs[0].shape[1]
    tile = width_tile(share_width, (256, 640))

    def body(rank_ref, pick_ref, weight_ref, *refs):
        hidden_refs, refs = refs[:head_count], refs[head_count:]
        down_refs, out_refs = refs[:grp_count], refs[grp_count:]
        firsts = [
            pl.multiple_of((rank_ref[0] - k + head_count) % head_count * rows_each, rows_each)
            for k in range(head_count)
        ]
        for n in range(0, share_width, tile):
            own = pl.ds(n, tile)
            results = []
            for g in range(grp_count):
                result = None
                for k in range(head_count):
                    part = jnp.dot(
                        hidden_refs[k][g],
                        down_refs[g][pl.ds(firsts[k], rows_each), own],
                        preferred_element_type=jnp.float32,
                    )
                    result = part if result is None else result + part
                results.append(result)
            for i in range(count):
                scaled = jnp.concatenate(
                    [result[i * capacity : (i + 1) * capacity] for result in results], axis=0
                )
                scaled = (scaled * weight_ref[places[i], :, 0:1]).astype(jnp.bfloat16)
                out_refs[i][:, own] = lax.dot_general(
                    pick_ref[places[i]],
                    scaled,
                    (((0,), (0,)), ((), ())),
                    preferred_element_type=jnp.float32,
                )

    in_vmem = pl.BlockSpec(memory_space=pltpu.VMEM)
    return pl.pallas_call(
        body,
        out_shape=[jax.ShapeDtypeStruct((tok_dev, share_width), jnp.float32)] * count,
        in_specs=[pl.BlockSpec(memory_space=pltpu.SMEM)]
        + [in_vmem] * (2 + head_count + grp_count),
        out_specs=[in_vmem] * count,
        compiler_params=pltpu.CompilerParams(vmem_limit_bytes=SMALL_LIMIT),
        name="token_sums",
    )(rank, picks, weights, *hiddens, *downs)


def on_device(
    hidden_in,
    attn_gain,
    w_query,
    key_projection_weight,
    value_projection_weight,
    w_out,
    prefix_keys,
    cached_prefix_values,
    request_lengths,
    moe_gain,
    expert_ids,
    route_weights,
    w_gate,
    w_up,
    w_down,
):
    tok_count = lax.axis_size("tok")
    grp_count = lax.axis_size("grp")
    head_count = lax.axis_size("head")
    tok_rank = lax.axis_index("tok")
    grp_rank = lax.axis_index("grp")
    head_rank = lax.axis_index("head")
    tok_dev = hidden_in.shape[1]
    model_width = attn_gain.shape[0]
    head_dim = prefix_keys.shape[3]
    kv_local = prefix_keys.shape[2]
    kv_width = kv_local * head_dim
    group_length = w_query.shape[1] // kv_width
    prefix_total = prefix_keys.shape[1] * tok_count
    share_width = model_width // head_count
    experts = grp_count * tok_count
    top_count = expert_ids.shape[2]
    capacity = 4 * tok_dev * top_count // (3 * experts)

    quarter = hidden_in[0]
    features = side_by_side(quarter, "head")
    query_blocks = others_over(w_query, "grp")
    key_blocks = others_over(key_projection_weight, "grp")
    value_blocks = others_over(value_projection_weight, "grp")
    out_blocks = others_over(w_out, "grp")

    payload = payload_of(
        prefix_keys[0].reshape(-1, kv_width),
        cached_prefix_values[0].reshape(-1, kv_width),
        expert_ids[0],
        route_weights[0],
        experts,
    )
    half_ring = tok_count // 2
    payloads = {0: payload}
    for distance in range(1, half_ring):
        payloads[distance] = along_ring(payload, distance)
        payloads[-distance] = along_ring(payload, -distance)
    payloads[half_ring] = along_ring(payload, half_ring)
    prefix_dev = prefix_keys.shape[1]

    gate_blocks = others_over(w_gate[0], "grp")
    up_blocks = others_over(w_up[0], "grp")
    down_blocks = others_over(w_down[0], "grp")

    attention_input = rms_norm(features, attn_gain)
    lengths = request_lengths[0]
    request_ends = jnp.cumsum(lengths)
    starts = request_ends - lengths
    token_index = tok_rank * tok_dev + jnp.arange(tok_dev, dtype=jnp.int32)
    own_start = jnp.max(
        jnp.where(starts[None, :] <= token_index[:, None], starts[None, :], 0), axis=1
    )
    token_positions = prefix_total + token_index - own_start
    key_product = split_product(attention_input, key_blocks, "grp")
    value_product = split_product(attention_input, value_blocks, "grp")
    query_product = split_product(attention_input, query_blocks, "grp")
    queries = apply_rotary(
        query_product.reshape(tok_dev, kv_local * group_length, head_dim), token_positions
    )
    queries = queries.reshape(tok_dev, kv_local * group_length * head_dim)
    request_suffix_keys = apply_rotary(
        key_product.reshape(tok_dev, kv_local, head_dim), token_positions
    )
    suffix = jnp.concatenate(
        [request_suffix_keys.reshape(tok_dev, kv_width), value_product.astype(jnp.bfloat16)], axis=1
    )
    longest = tok_dev * tok_count // 4
    reach_devices = (longest - 1 + tok_dev - 1) // tok_dev
    attended = attention(
        queries,
        [suffix] + [shifted(suffix, "tok", d) for d in range(1, reach_devices + 1)],
        list(payloads.values()),
        prefix_dev,
        lengths,
        tok_rank,
        head_dim,
    )
    products = [
        lax.dot_general(
            attended, block, (((1,), (1,)), ((), ())), preferred_element_type=jnp.float32
        )
        for block in out_blocks
    ]
    out_rows = w_out.shape[0]

    def share_of(place):
        first = place * share_width
        distance = (grp_rank - first // out_rows) % grp_count
        block = products[0]
        for d in range(1, grp_count):
            block = jnp.where(distance == d, products[d], block)
        if out_rows == share_width:
            return block
        return lax.dynamic_slice_in_dim(block, first % out_rows, share_width, 1)

    mixed = share_of(head_rank)
    for distance in range(1, head_count):
        leaving = share_of((head_rank + distance) % head_count).astype(jnp.bfloat16)
        mixed = mixed + turned_by(leaving, "head", distance).astype(jnp.float32)
    mid_quarter = (quarter.astype(jnp.float32) + mixed).astype(jnp.bfloat16)
    mid_pieces = others_over(mid_quarter, "head")

    chosen = jnp.stack(
        [((grp_rank - d) % grp_count) * tok_count + tok_rank for d in range(grp_count)]
    ).astype(jnp.int32)
    place_of = {d: i for i, d in enumerate(payloads)}
    picks, slot_weights = slots_of(
        chosen, list(payloads.values()), prefix_dev, grp_count, tok_dev, experts, capacity
    )

    gain = moe_gain.astype(jnp.float32).reshape(head_count, 1, share_width)

    def units_of(chunk, blocks):
        places = [place_of[d] for d in chunk]
        return hidden_units(
            head_rank[None], picks, places, blocks, gain, gate_blocks, up_blocks, capacity
        )

    def sums_of(chunk, exchanged):
        places = [place_of[d] for d in chunk]
        sums = token_sums(
            head_rank[None], picks, slot_weights, places, exchanged, down_blocks, tok_dev, capacity
        )
        return dict(zip(chunk, sums))

    ahead, behind = mid_pieces, mid_pieces
    chunk, blocks = [0], [mid_pieces]
    waiting = []
    for step in range(1, half_ring + 1):
        last = step == half_ring
        middle = head_count // 2
        arriving = [
            [
                None if last and d >= middle else along_ring(ahead[d], 1),
                None if last and d < middle else along_ring(behind[d], -1),
            ]
            for d in range(head_count)
        ]
        hidden = units_of(chunk, blocks)
        for d in range(head_count):
            arriving[d], hidden = lax.optimization_barrier((arriving[d], hidden))
        if waiting:
            own, arrived = waiting.pop()
            arriving[-1], arrived = lax.optimization_barrier((arriving[-1], arrived))
            waiting.append((own, arrived))
        ahead, behind = [pair[0] for pair in arriving], [pair[1] for pair in arriving]
        waiting.append((chunk, others_over(hidden, "head")))
        if last:
            chunk, blocks = [half_ring], [ahead[:middle] + behind[middle:]]
        else:
            chunk, blocks = [step, -step], [ahead, behind]
    exchanged = others_over(units_of(chunk, blocks), "head")
    early = sums_of(*waiting.pop(-2))
    exchanged, early = lax.optimization_barrier((exchanged, early))
    parts = {**early, **sums_of(chunk, exchanged)}
    late = []
    for own, arrived in reversed(waiting):
        late.append(
            lambda own=own, arrived=arrived: sums_of(
                own, lax.optimization_barrier((arrived, parts[half_ring]))[0]
            )
        )
    weighted = ring_sum(parts, late)
    output = (mid_quarter.astype(jnp.float32) + weighted).astype(jnp.bfloat16)
    return output[None]


def solution(mesh):
    return jax.shard_map(
        on_device,
        mesh=mesh,
        in_specs=(
            P("grp", "tok", "head"),
            P(),
            P("grp", "head"),
            P("grp", "head"),
            P("grp", "head"),
            P("grp", "head"),
            P("grp", "tok", "head", None),
            P("grp", "tok", "head", None),
            P("grp", None),
            P(),
            P("grp", "tok", None),
            P("grp", "tok", None),
            P(("grp", "tok"), None, "head"),
            P(("grp", "tok"), None, "head"),
            P(("grp", "tok"), None, "head"),
        ),
        out_specs=P("grp", "tok", "head"),
        check_vma=False,
    )
```

```python
import math

import jax
import jax.numpy as jnp
from jax import lax
from jax.experimental import pallas as pl
from jax.experimental.pallas import tpu as pltpu
from jax.sharding import PartitionSpec as P

ROPE_BASE = 500000.0
NORM_EPS = 1e-06
MASKED = -1e30
VMEM_LIMIT = 40 * 1024 * 1024
SMALL_LIMIT = 20 * 1024 * 1024


def shifted(block, axis, distance):
    devices = range(lax.axis_size(axis))
    route = [(i - distance, i) for i in devices if i - distance in devices]
    return lax.ppermute(block, axis, route)


def rms_norm(values_in, gain_vector):
    widened = values_in.astype(jnp.float32)
    mean_sq = jnp.mean(widened * widened, axis=-1, keepdims=True)
    return (widened * lax.rsqrt(mean_sq + NORM_EPS) * gain_vector.astype(jnp.float32)).astype(
        jnp.bfloat16
    )


def apply_rotary(product, token_positions):
    half_dim = product.shape[-1] // 2
    frequency = jnp.exp(
        jnp.arange(half_dim, dtype=jnp.float32) * (-2.0 * math.log(ROPE_BASE) / product.shape[-1])
    )
    angles = token_positions.astype(jnp.float32)[:, None] * frequency[None, :]
    cosine = jnp.cos(angles)[:, None, :]
    sine_part = jnp.sin(angles)[:, None, :]
    first_half = product[..., :half_dim]
    second_half = product[..., half_dim:]
    turned = jnp.concatenate(
        [
            first_half * cosine - second_half * sine_part,
            second_half * cosine + first_half * sine_part,
        ],
        axis=-1,
    )
    return turned.astype(jnp.bfloat16)


def turned_by(block, axis, distance):
    devices = lax.axis_size(axis)
    return lax.ppermute(block, axis, [(i, (i + distance) % devices) for i in range(devices)])


def along_ring(block, distance):
    devices = lax.axis_size("tok")
    order = list(range(0, devices, 2)) + list(range(devices - 1 - devices % 2, 0, -2))
    route = [(order[i], order[(i + distance) % devices]) for i in range(devices)]
    return lax.ppermute(block, "tok", route)


def ring_sum(parts, late):
    half = lax.axis_size("tok") // 2
    middle = parts[0].shape[1] // 2
    left = along_ring(parts[half][:, :middle].astype(jnp.bfloat16), -1)
    right = along_ring(parts[half][:, middle:].astype(jnp.bfloat16), 1)
    parts = {**parts, **late()}
    left, right, parts = lax.optimization_barrier((left, right, parts))
    left = parts[half - 1] + jnp.pad(
        left.astype(jnp.float32), ((0, 0), (0, parts[0].shape[1] - middle))
    )
    right = parts[1 - half] + jnp.pad(right.astype(jnp.float32), ((0, 0), (middle, 0)))
    for step in range(half - 2, -1, -1):
        left = along_ring(left.astype(jnp.bfloat16), -1).astype(jnp.float32)
        right = along_ring(right.astype(jnp.bfloat16), 1).astype(jnp.float32)
        if step:
            left = left + parts[step]
            right = right + parts[-step]
    return parts[0] + left + right


def side_by_side(block, axis):
    count = lax.axis_size(axis)
    rank = lax.axis_index(axis)
    blocks = others_over(block, axis)
    columns = []
    for place in range(count):
        column = blocks[0]
        for distance in range(1, count):
            column = jnp.where((rank - place) % count == distance, blocks[distance], column)
        columns.append(column)
    return jnp.concatenate(columns, axis=1)


def others_over(block, axis):
    return [block] + [turned_by(block, axis, d) for d in range(1, lax.axis_size(axis))]


def split_product(activations, blocks, axis):
    count = len(blocks)
    rank = lax.axis_index(axis)
    rows = blocks[0].shape[0]
    total = None
    for distance, block in enumerate(blocks):
        part = lax.dynamic_slice_in_dim(
            activations, ((rank - distance) % count) * rows, rows, 1
        )
        product = jnp.dot(part, block, preferred_element_type=jnp.float32)
        total = product if total is None else total + product
    return total


def width_tile(width, sizes):
    for size in sizes:
        if width % size == 0:
            return size
    return width


def picked_by(payload_ref, first_row, expert, experts, tok_dev, capacity):
    beside = payload_ref.shape[1] // tok_dev
    own = lax.broadcasted_iota(jnp.int32, (experts, tok_dev), 0) == expert

    def piece(i):
        rows = pl.ds(first_row + i // beside * experts, experts)
        columns = pl.ds(i % beside * tok_dev, tok_dev)
        values = payload_ref[rows, columns].astype(jnp.float32)
        return jnp.sum(jnp.where(own, values, 0.0), axis=0, keepdims=True)

    weight = piece(0) + piece(1) + piece(2)
    mask = piece(3)
    upto = lax.broadcasted_iota(jnp.int32, (tok_dev, tok_dev), 0) <= lax.broadcasted_iota(
        jnp.int32, (tok_dev, tok_dev), 1
    )
    upto = jnp.where(upto, 1.0, 0.0).astype(jnp.bfloat16)
    many = jnp.broadcast_to(mask, (16, tok_dev)).astype(jnp.bfloat16)
    place = jnp.dot(many, upto, preferred_element_type=jnp.float32)[0:1]
    place = jnp.where(mask > 0.5, place - 1.0, -1.0).astype(jnp.int32)
    slots = lax.broadcasted_iota(jnp.int32, (capacity, tok_dev), 0)
    pick = jnp.where(slots == place, 1.0, 0.0)
    return pick.astype(jnp.bfloat16), jnp.sum(pick * weight, axis=1, keepdims=True)


def payload_of(keys, values, ids, weights, experts):
    prefix_dev, kv_width = keys.shape
    tok_dev, top_count = ids.shape
    beside = 2 * kv_width // tok_dev
    rows = prefix_dev + 4 // beside * experts

    def body(keys_ref, values_ref, ids_ref, weights_ref, out_ref):
        out_ref[pl.ds(0, prefix_dev), pl.ds(0, kv_width)] = keys_ref[...]
        out_ref[pl.ds(0, prefix_dev), pl.ds(kv_width, kv_width)] = values_ref[...]
        lanes = lax.broadcasted_iota(jnp.int32, (tok_dev, 128), 1)
        dense = jnp.zeros((tok_dev, 128), jnp.float32)
        mask = jnp.zeros((tok_dev, 128), jnp.float32)
        for k in range(top_count):
            named = lanes == ids_ref[:, k : k + 1]
            dense = dense + jnp.where(named, weights_ref[:, k : k + 1], 0.0)
            mask = mask + jnp.where(named, 1.0, 0.0)
        rest = jnp.transpose(dense)[:experts]
        pieces = []
        for _ in range(3):
            pieces.append(rest.astype(jnp.bfloat16))
            rest = rest - pieces[-1].astype(jnp.float32)
        pieces.append(jnp.transpose(mask)[:experts].astype(jnp.bfloat16))
        for i, piece in enumerate(pieces):
            out_ref[
                pl.ds(prefix_dev + i // beside * experts, experts),
                pl.ds(i % beside * tok_dev, tok_dev),
            ] = piece

    return pl.pallas_call(
        body,
        out_shape=jax.ShapeDtypeStruct((rows, 2 * kv_width), jnp.bfloat16),
        name="payload",
    )(keys, values, ids, weights)


def attention(queries, suffix, payloads, prefix_dev, lengths, tok_rank, head_dim):
    tok_dev, query_width = queries.shape
    kv_width = suffix[0].shape[1] // 2
    kv_local = kv_width // head_dim
    group_length = query_width // kv_width
    requests = lengths.shape[0]
    prefix_rows = prefix_dev * len(payloads)
    keys_total = prefix_rows + tok_dev * len(suffix)

    def body(lengths_ref, rank_ref, query_ref, *refs):
        suffix_refs, refs = refs[: len(suffix)], refs[len(suffix) :]
        payload_refs, out_ref = refs[:-1], refs[-1]
        token = rank_ref[0] * tok_dev + lax.broadcasted_iota(jnp.int32, (tok_dev, tok_dev), 0)
        start = jnp.int32(0)
        own_start = jnp.zeros((tok_dev, tok_dev), jnp.int32)
        for request in range(requests):
            own_start = jnp.where(token >= start, jnp.maximum(own_start, start), own_start)
            start = start + lengths_ref[request]
        bias = [jnp.zeros((tok_dev, prefix_rows), jnp.float32)]
        for distance in range(len(suffix)):
            key = (rank_ref[0] - distance) * tok_dev + lax.broadcasted_iota(
                jnp.int32, (tok_dev, tok_dev), 1
            )
            bias.append(jnp.where((key >= own_start) & (key <= token), 0.0, MASKED))
        bias = jnp.concatenate(bias, axis=1)
        bias = jnp.concatenate([bias] * group_length, axis=0)
        for c in range(kv_local):
            columns = pl.ds(c * head_dim, head_dim)
            keys = jnp.concatenate(
                [ref[pl.ds(0, prefix_dev), columns] for ref in payload_refs]
                + [ref[:, columns] for ref in suffix_refs],
                axis=0,
            )
            columns = pl.ds(kv_width + c * head_dim, head_dim)
            values = jnp.concatenate(
                [ref[pl.ds(0, prefix_dev), columns] for ref in payload_refs]
                + [ref[:, columns] for ref in suffix_refs],
                axis=0,
            )
            first = c * group_length
            query = jnp.concatenate(
                [
                    query_ref[:, pl.ds((first + r) * head_dim, head_dim)]
                    for r in range(group_length)
                ],
                axis=0,
            )
            scores = lax.dot_general(
                query, keys, (((1,), (1,)), ((), ())), preferred_element_type=jnp.float32
            )
            scores = scores * head_dim ** (-0.5) + bias
            probs = jnp.exp(scores - jnp.max(scores, axis=1, keepdims=True))
            total = jnp.sum(probs, axis=1, keepdims=True)
            summed = jnp.dot(
                probs.astype(jnp.bfloat16), values, preferred_element_type=jnp.float32
            )
            attended = (summed / total).astype(jnp.bfloat16)
            for r in range(group_length):
                out_ref[:, pl.ds((first + r) * head_dim, head_dim)] = attended[
                    r * tok_dev : (r + 1) * tok_dev
                ]

    in_vmem = pl.BlockSpec(memory_space=pltpu.VMEM)
    in_smem = pl.BlockSpec(memory_space=pltpu.SMEM)
    return pl.pallas_call(
        body,
        out_shape=jax.ShapeDtypeStruct((tok_dev, query_width), jnp.bfloat16),
        in_specs=[in_smem] * 2 + [in_vmem] * (1 + len(suffix) + len(payloads)),
        out_specs=in_vmem,
        compiler_params=pltpu.CompilerParams(vmem_limit_bytes=VMEM_LIMIT),
        name="attention",
    )(lengths, tok_rank[None], queries, *suffix, *payloads)


def slots_of(chosen, payloads, first_row, grp_count, tok_dev, experts, capacity):
    count = len(payloads)

    def body(chosen_ref, *refs):
        payload_refs, (pick_ref, weight_ref) = refs[:count], refs[count:]
        for i in range(count):
            for g in range(grp_count):
                pick, weight = picked_by(
                    payload_refs[i], first_row, chosen_ref[g], experts, tok_dev, capacity
                )
                pick_ref[i, pl.ds(g * capacity, capacity), :] = pick
                weight_ref[i, pl.ds(g * capacity, capacity), :] = jnp.broadcast_to(
                    weight, (capacity, 128)
                )

    in_vmem = pl.BlockSpec(memory_space=pltpu.VMEM)
    slots = grp_count * capacity
    return pl.pallas_call(
        body,
        out_shape=[
            jax.ShapeDtypeStruct((count, slots, tok_dev), jnp.bfloat16),
            jax.ShapeDtypeStruct((count, slots, 128), jnp.float32),
        ],
        in_specs=[pl.BlockSpec(memory_space=pltpu.SMEM)] + [in_vmem] * count,
        out_specs=[in_vmem] * 2,
        compiler_params=pltpu.CompilerParams(vmem_limit_bytes=SMALL_LIMIT),
        name="slots",
    )(chosen, *payloads)


def hidden_units(picks, places, blocks, gates, ups, capacity):
    count, grp_count = len(blocks), len(gates)
    model_width, hidden_width = gates[0].shape
    tile = width_tile(hidden_width, (256, 384, 128))
    pieces = [len(block) for block in blocks]
    columns = sum(pieces)

    def body(pick_ref, *refs):
        token_refs, refs = refs[:columns], refs[columns:]
        gate_refs, refs = refs[:grp_count], refs[grp_count:]
        up_refs, refs = refs[:grp_count], refs[grp_count:]
        out_ref, rows_ref = refs
        at = 0
        for i in range(count):
            pick = pick_ref[places[i]]
            first = 0
            for token_ref in token_refs[at : at + pieces[i]]:
                width = token_ref.shape[1]
                picked = jnp.dot(
                    pick, token_ref[...], preferred_element_type=jnp.float32
                ).astype(jnp.bfloat16)
                for g in range(grp_count):
                    rows_ref[g, pl.ds(i * capacity, capacity), pl.ds(first, width)] = picked[
                        g * capacity : (g + 1) * capacity
                    ]
                first += width
            at += pieces[i]
        for g in range(grp_count):
            for n in range(0, hidden_width, tile):
                own = pl.ds(n, tile)
                gate = jnp.dot(
                    rows_ref[g], gate_refs[g][:, own], preferred_element_type=jnp.float32
                )
                up = jnp.dot(rows_ref[g], up_refs[g][:, own], preferred_element_type=jnp.float32)
                out_ref[g, :, own] = (gate / (1.0 + jnp.exp(-gate)) * up).astype(jnp.bfloat16)

    in_vmem = pl.BlockSpec(memory_space=pltpu.VMEM)
    flat = [part for block in blocks for part in block]
    return pl.pallas_call(
        body,
        out_shape=jax.ShapeDtypeStruct((grp_count, count * capacity, hidden_width), jnp.bfloat16),
        in_specs=[in_vmem] * (1 + columns + 2 * grp_count),
        out_specs=in_vmem,
        scratch_shapes=[pltpu.VMEM((grp_count, count * capacity, model_width), jnp.bfloat16)],
        compiler_params=pltpu.CompilerParams(vmem_limit_bytes=SMALL_LIMIT),
        name="hidden_units",
    )(picks, *flat, *gates, *ups)


def token_sums(rank, picks, weights, places, hiddens, downs, tok_dev, capacity):
    count, grp_count, head_count = len(places), len(downs), len(hiddens)
    rows_each = hiddens[0].shape[2]
    share_width = downs[0].shape[1]
    tile = width_tile(share_width, (256, 640))

    def body(rank_ref, pick_ref, weight_ref, *refs):
        hidden_refs, refs = refs[:head_count], refs[head_count:]
        down_refs, out_refs = refs[:grp_count], refs[grp_count:]
        firsts = [
            pl.multiple_of((rank_ref[0] - k + head_count) % head_count * rows_each, rows_each)
            for k in range(head_count)
        ]
        for n in range(0, share_width, tile):
            own = pl.ds(n, tile)
            results = []
            for g in range(grp_count):
                result = None
                for k in range(head_count):
                    part = jnp.dot(
                        hidden_refs[k][g],
                        down_refs[g][pl.ds(firsts[k], rows_each), own],
                        preferred_element_type=jnp.float32,
                    )
                    result = part if result is None else result + part
                results.append(result)
            for i in range(count):
                scaled = jnp.concatenate(
                    [result[i * capacity : (i + 1) * capacity] for result in results], axis=0
                )
                scaled = (scaled * weight_ref[places[i], :, 0:1]).astype(jnp.bfloat16)
                out_refs[i][:, own] = lax.dot_general(
                    pick_ref[places[i]],
                    scaled,
                    (((0,), (0,)), ((), ())),
                    preferred_element_type=jnp.float32,
                )

    in_vmem = pl.BlockSpec(memory_space=pltpu.VMEM)
    return pl.pallas_call(
        body,
        out_shape=[jax.ShapeDtypeStruct((tok_dev, share_width), jnp.float32)] * count,
        in_specs=[pl.BlockSpec(memory_space=pltpu.SMEM)]
        + [in_vmem] * (2 + head_count + grp_count),
        out_specs=[in_vmem] * count,
        compiler_params=pltpu.CompilerParams(vmem_limit_bytes=SMALL_LIMIT),
        name="token_sums",
    )(rank, picks, weights, *hiddens, *downs)


def on_device(
    hidden_in,
    attn_gain,
    w_query,
    key_projection_weight,
    value_projection_weight,
    w_out,
    prefix_keys,
    cached_prefix_values,
    request_lengths,
    moe_gain,
    expert_ids,
    route_weights,
    w_gate,
    w_up,
    w_down,
):
    tok_count = lax.axis_size("tok")
    grp_count = lax.axis_size("grp")
    head_count = lax.axis_size("head")
    tok_rank = lax.axis_index("tok")
    grp_rank = lax.axis_index("grp")
    head_rank = lax.axis_index("head")
    tok_dev = hidden_in.shape[1]
    model_width = attn_gain.shape[0]
    head_dim = prefix_keys.shape[3]
    kv_local = prefix_keys.shape[2]
    kv_width = kv_local * head_dim
    group_length = w_query.shape[1] // kv_width
    prefix_total = prefix_keys.shape[1] * tok_count
    share_width = model_width // head_count
    experts = grp_count * tok_count
    top_count = expert_ids.shape[2]
    capacity = 4 * tok_dev * top_count // (3 * experts)

    quarter = hidden_in[0]
    features = side_by_side(quarter, "head")
    query_blocks = others_over(w_query, "grp")
    key_blocks = others_over(key_projection_weight, "grp")
    value_blocks = others_over(value_projection_weight, "grp")
    full_out = lax.all_gather(w_out, "grp", axis=0, tiled=True)

    payload = payload_of(
        prefix_keys[0].reshape(-1, kv_width),
        cached_prefix_values[0].reshape(-1, kv_width),
        expert_ids[0],
        route_weights[0],
        experts,
    )
    half_ring = tok_count // 2
    payloads = {0: payload}
    for distance in range(1, half_ring):
        payloads[distance] = along_ring(payload, distance)
        payloads[-distance] = along_ring(payload, -distance)
    payloads[half_ring] = along_ring(payload, half_ring)
    prefix_dev = prefix_keys.shape[1]


    attention_input = rms_norm(features, attn_gain)
    lengths = request_lengths[0]
    request_ends = jnp.cumsum(lengths)
    starts = request_ends - lengths
    token_index = tok_rank * tok_dev + jnp.arange(tok_dev, dtype=jnp.int32)
    own_start = jnp.max(
        jnp.where(starts[None, :] <= token_index[:, None], starts[None, :], 0), axis=1
    )
    token_positions = prefix_total + token_index - own_start
    key_product = split_product(attention_input, key_blocks, "grp")
    value_product = split_product(attention_input, value_blocks, "grp")
    query_product = split_product(attention_input, query_blocks, "grp")
    queries = apply_rotary(
        query_product.reshape(tok_dev, kv_local * group_length, head_dim), token_positions
    )
    queries = queries.reshape(tok_dev, kv_local * group_length * head_dim)
    request_suffix_keys = apply_rotary(
        key_product.reshape(tok_dev, kv_local, head_dim), token_positions
    )
    suffix = jnp.concatenate(
        [request_suffix_keys.reshape(tok_dev, kv_width), value_product.astype(jnp.bfloat16)], axis=1
    )
    longest = tok_dev * tok_count // 4
    reach_devices = (longest - 1 + tok_dev - 1) // tok_dev
    reached = [suffix] + [shifted(suffix, "tok", d) for d in range(1, reach_devices + 1)]
    (payloads, reached), expert_weights = lax.optimization_barrier(
        ((payloads, reached), (w_gate, w_up, w_down))
    )
    gate_blocks, up_blocks, down_blocks = [
        others_over(weight[0], "grp") for weight in expert_weights
    ]
    attended = attention(
        queries,
        reached,
        list(payloads.values()),
        prefix_dev,
        lengths,
        tok_rank,
        head_dim,
    )
    halves = []
    for half in range(2):
        columns = slice(half * model_width // 2, (half + 1) * model_width // 2)
        own = lax.dot_general(
            attended, full_out[columns], (((1,), (1,)), ((), ())), preferred_element_type=jnp.float32
        )
        mixed = own + features[:, columns].astype(jnp.float32)
        for arrived in others_over(own.astype(jnp.bfloat16), "head")[1:]:
            mixed = mixed + arrived.astype(jnp.float32)
        halves.append(mixed.astype(jnp.bfloat16))
    mid_full = jnp.concatenate(halves, axis=1)
    mid_quarter = lax.dynamic_slice_in_dim(mid_full, head_rank * share_width, share_width, 1)
    moe_in = rms_norm(mid_full, moe_gain)
    chosen = jnp.stack(
        [((grp_rank - d) % grp_count) * tok_count + tok_rank for d in range(grp_count)]
    ).astype(jnp.int32)
    place_of = {d: i for i, d in enumerate(payloads)}
    picks, slot_weights = slots_of(
        chosen, list(payloads.values()), prefix_dev, grp_count, tok_dev, experts, capacity
    )

    def units_of(chunk, blocks):
        places = [place_of[d] for d in chunk]
        return hidden_units(picks, places, blocks, gate_blocks, up_blocks, capacity)

    def sums_of(chunk, exchanged):
        places = [place_of[d] for d in chunk]
        sums = token_sums(
            head_rank[None], picks, slot_weights, places, exchanged, down_blocks, tok_dev, capacity
        )
        return dict(zip(chunk, sums))

    middle = model_width // 2
    ahead, behind = moe_in, moe_in
    chunk, blocks = [0], [[moe_in]]
    parts, waiting = {}, []
    for step in range(1, half_ring + 1):
        last = step == half_ring
        sent = (ahead[:, :middle], behind[:, middle:]) if last else (ahead, behind)
        arriving = (along_ring(sent[0], 1), along_ring(sent[1], -1))
        hidden = units_of(chunk, blocks)
        if waiting and not last:
            parts.update(sums_of(*waiting.pop(0)))
        (ahead, behind), hidden, parts = lax.optimization_barrier((arriving, hidden, parts))
        waiting.append((chunk, others_over(hidden, "head")))
        chunk = [half_ring] if last else [step, -step]
        blocks = [[ahead, behind]] if last else [[ahead], [behind]]
    exchanged = others_over(units_of(chunk, blocks), "head")
    parts.update(sums_of(*waiting.pop(0)))
    exchanged, parts = lax.optimization_barrier((exchanged, parts))
    parts.update(sums_of(chunk, exchanged))

    def late():
        own, arrived = waiting.pop(0)
        arrived, _ = lax.optimization_barrier((arrived, parts[half_ring]))
        return sums_of(own, arrived)

    weighted = ring_sum(parts, late)
    output = (mid_quarter.astype(jnp.float32) + weighted).astype(jnp.bfloat16)
    return output[None]


def solution(mesh):
    return jax.shard_map(
        on_device,
        mesh=mesh,
        in_specs=(
            P("grp", "tok", "head"),
            P(),
            P("grp", "head"),
            P("grp", "head"),
            P("grp", "head"),
            P("grp", "head"),
            P("grp", "tok", "head", None),
            P("grp", "tok", "head", None),
            P("grp", None),
            P(),
            P("grp", "tok", None),
            P("grp", "tok", None),
            P(("grp", "tok"), None, "head"),
            P(("grp", "tok"), None, "head"),
            P(("grp", "tok"), None, "head"),
        ),
        out_specs=P("grp", "tok", "head"),
        check_vma=False,
    )
```

```python
import math

import jax
import jax.numpy as jnp
from jax import lax
from jax.experimental import pallas as pl
from jax.experimental.pallas import tpu as pltpu
from jax.sharding import PartitionSpec as P

ROPE_BASE = 500000.0
NORM_EPS = 1e-06
MASKED = -1e30
VMEM_LIMIT = 40 * 1024 * 1024
SMALL_LIMIT = 16 * 1024 * 1024


def shifted(block, axis, distance):
    devices = range(lax.axis_size(axis))
    route = [(i - distance, i) for i in devices if i - distance in devices]
    return lax.ppermute(block, axis, route)


def rms_norm(values_in, gain_vector):
    widened = values_in.astype(jnp.float32)
    mean_sq = jnp.mean(widened * widened, axis=-1, keepdims=True)
    return (widened * lax.rsqrt(mean_sq + NORM_EPS) * gain_vector.astype(jnp.float32)).astype(
        jnp.bfloat16
    )


def apply_rotary(product, token_positions):
    half_dim = product.shape[-1] // 2
    frequency = jnp.exp(
        jnp.arange(half_dim, dtype=jnp.float32) * (-2.0 * math.log(ROPE_BASE) / product.shape[-1])
    )
    angles = token_positions.astype(jnp.float32)[:, None] * frequency[None, :]
    cosine = jnp.cos(angles)[:, None, :]
    sine_part = jnp.sin(angles)[:, None, :]
    first_half = product[..., :half_dim]
    second_half = product[..., half_dim:]
    turned = jnp.concatenate(
        [
            first_half * cosine - second_half * sine_part,
            second_half * cosine + first_half * sine_part,
        ],
        axis=-1,
    )
    return turned.astype(jnp.bfloat16)


def turned_by(block, axis, distance):
    devices = lax.axis_size(axis)
    return lax.ppermute(block, axis, [(i, (i + distance) % devices) for i in range(devices)])


def along_ring(block, distance):
    devices = lax.axis_size("tok")
    order = list(range(0, devices, 2)) + list(range(devices - 1 - devices % 2, 0, -2))
    route = [(order[i], order[(i + distance) % devices]) for i in range(devices)]
    return lax.ppermute(block, "tok", route)


def ring_sum(parts, late):
    half = lax.axis_size("tok") // 2
    middle = parts[0].shape[1] // 2
    left = along_ring(parts[half][:, :middle].astype(jnp.bfloat16), -1)
    right = along_ring(parts[half][:, middle:].astype(jnp.bfloat16), 1)
    parts = {**parts, **late()}
    left, right, parts = lax.optimization_barrier((left, right, parts))
    left = parts[half - 1] + jnp.pad(
        left.astype(jnp.float32), ((0, 0), (0, parts[0].shape[1] - middle))
    )
    right = parts[1 - half] + jnp.pad(right.astype(jnp.float32), ((0, 0), (middle, 0)))
    for step in range(half - 2, -1, -1):
        left = along_ring(left.astype(jnp.bfloat16), -1).astype(jnp.float32)
        right = along_ring(right.astype(jnp.bfloat16), 1).astype(jnp.float32)
        if step:
            left = left + parts[step]
            right = right + parts[-step]
    return parts[0] + left + right


def side_by_side(block, axis):
    count = lax.axis_size(axis)
    rank = lax.axis_index(axis)
    blocks = others_over(block, axis)
    columns = []
    for place in range(count):
        column = blocks[0]
        for distance in range(1, count):
            column = jnp.where((rank - place) % count == distance, blocks[distance], column)
        columns.append(column)
    return jnp.concatenate(columns, axis=1)


def others_over(block, axis):
    return [block] + [turned_by(block, axis, d) for d in range(1, lax.axis_size(axis))]


def split_product(activations, blocks, axis):
    count = len(blocks)
    rank = lax.axis_index(axis)
    rows = blocks[0].shape[0]
    total = None
    for distance, block in enumerate(blocks):
        part = lax.dynamic_slice_in_dim(
            activations, ((rank - distance) % count) * rows, rows, 1
        )
        product = jnp.dot(part, block, preferred_element_type=jnp.float32)
        total = product if total is None else total + product
    return total


def width_tile(width, sizes):
    for size in sizes:
        if width % size == 0:
            return size
    return width


def picked_by(payload_ref, first_row, expert, experts, tok_dev, capacity):
    beside = payload_ref.shape[1] // tok_dev
    own = lax.broadcasted_iota(jnp.int32, (experts, tok_dev), 0) == expert

    def piece(i):
        rows = pl.ds(first_row + i // beside * experts, experts)
        columns = pl.ds(i % beside * tok_dev, tok_dev)
        values = payload_ref[rows, columns].astype(jnp.float32)
        return jnp.sum(jnp.where(own, values, 0.0), axis=0, keepdims=True)

    weight = piece(0) + piece(1) + piece(2)
    mask = piece(3)
    upto = lax.broadcasted_iota(jnp.int32, (tok_dev, tok_dev), 0) <= lax.broadcasted_iota(
        jnp.int32, (tok_dev, tok_dev), 1
    )
    upto = jnp.where(upto, 1.0, 0.0).astype(jnp.bfloat16)
    many = jnp.broadcast_to(mask, (16, tok_dev)).astype(jnp.bfloat16)
    place = jnp.dot(many, upto, preferred_element_type=jnp.float32)[0:1]
    place = jnp.where(mask > 0.5, place - 1.0, -1.0).astype(jnp.int32)
    slots = lax.broadcasted_iota(jnp.int32, (capacity, tok_dev), 0)
    pick = jnp.where(slots == place, 1.0, 0.0)
    return pick.astype(jnp.bfloat16), jnp.sum(pick * weight, axis=1, keepdims=True)


def payload_of(keys, values, ids, weights, experts):
    prefix_dev, kv_width = keys.shape
    tok_dev, top_count = ids.shape
    beside = 2 * kv_width // tok_dev
    rows = prefix_dev + 4 // beside * experts

    def body(keys_ref, values_ref, ids_ref, weights_ref, out_ref):
        out_ref[pl.ds(0, prefix_dev), pl.ds(0, kv_width)] = keys_ref[...]
        out_ref[pl.ds(0, prefix_dev), pl.ds(kv_width, kv_width)] = values_ref[...]
        lanes = lax.broadcasted_iota(jnp.int32, (tok_dev, 128), 1)
        dense = jnp.zeros((tok_dev, 128), jnp.float32)
        mask = jnp.zeros((tok_dev, 128), jnp.float32)
        for k in range(top_count):
            named = lanes == ids_ref[:, k : k + 1]
            dense = dense + jnp.where(named, weights_ref[:, k : k + 1], 0.0)
            mask = mask + jnp.where(named, 1.0, 0.0)
        rest = jnp.transpose(dense)[:experts]
        pieces = []
        for _ in range(3):
            pieces.append(rest.astype(jnp.bfloat16))
            rest = rest - pieces[-1].astype(jnp.float32)
        pieces.append(jnp.transpose(mask)[:experts].astype(jnp.bfloat16))
        for i, piece in enumerate(pieces):
            out_ref[
                pl.ds(prefix_dev + i // beside * experts, experts),
                pl.ds(i % beside * tok_dev, tok_dev),
            ] = piece

    return pl.pallas_call(
        body,
        out_shape=jax.ShapeDtypeStruct((rows, 2 * kv_width), jnp.bfloat16),
        name="payload",
    )(keys, values, ids, weights)


def attention(queries, suffix, payloads, prefix_dev, lengths, tok_rank, head_dim):
    tok_dev, query_width = queries.shape
    kv_width = suffix[0].shape[1] // 2
    kv_local = kv_width // head_dim
    group_length = query_width // kv_width
    requests = lengths.shape[0]
    prefix_rows = prefix_dev * len(payloads)
    keys_total = prefix_rows + tok_dev * len(suffix)

    def body(lengths_ref, rank_ref, query_ref, *refs):
        suffix_refs, refs = refs[: len(suffix)], refs[len(suffix) :]
        payload_refs, out_ref = refs[:-1], refs[-1]
        token = rank_ref[0] * tok_dev + lax.broadcasted_iota(jnp.int32, (tok_dev, tok_dev), 0)
        start = jnp.int32(0)
        own_start = jnp.zeros((tok_dev, tok_dev), jnp.int32)
        for request in range(requests):
            own_start = jnp.where(token >= start, jnp.maximum(own_start, start), own_start)
            start = start + lengths_ref[request]
        bias = [jnp.zeros((tok_dev, prefix_rows), jnp.float32)]
        for distance in range(len(suffix)):
            key = (rank_ref[0] - distance) * tok_dev + lax.broadcasted_iota(
                jnp.int32, (tok_dev, tok_dev), 1
            )
            bias.append(jnp.where((key >= own_start) & (key <= token), 0.0, MASKED))
        bias = jnp.concatenate(bias, axis=1)
        bias = jnp.concatenate([bias] * group_length, axis=0)
        for c in range(kv_local):
            columns = pl.ds(c * head_dim, head_dim)
            keys = jnp.concatenate(
                [ref[pl.ds(0, prefix_dev), columns] for ref in payload_refs]
                + [ref[:, columns] for ref in suffix_refs],
                axis=0,
            )
            columns = pl.ds(kv_width + c * head_dim, head_dim)
            values = jnp.concatenate(
                [ref[pl.ds(0, prefix_dev), columns] for ref in payload_refs]
                + [ref[:, columns] for ref in suffix_refs],
                axis=0,
            )
            first = c * group_length
            query = jnp.concatenate(
                [
                    query_ref[:, pl.ds((first + r) * head_dim, head_dim)]
                    for r in range(group_length)
                ],
                axis=0,
            )
            scores = lax.dot_general(
                query, keys, (((1,), (1,)), ((), ())), preferred_element_type=jnp.float32
            )
            scores = scores * head_dim ** (-0.5) + bias
            probs = jnp.exp(scores - jnp.max(scores, axis=1, keepdims=True))
            total = jnp.sum(probs, axis=1, keepdims=True)
            summed = jnp.dot(
                probs.astype(jnp.bfloat16), values, preferred_element_type=jnp.float32
            )
            attended = (summed / total).astype(jnp.bfloat16)
            for r in range(group_length):
                out_ref[:, pl.ds((first + r) * head_dim, head_dim)] = attended[
                    r * tok_dev : (r + 1) * tok_dev
                ]

    in_vmem = pl.BlockSpec(memory_space=pltpu.VMEM)
    in_smem = pl.BlockSpec(memory_space=pltpu.SMEM)
    return pl.pallas_call(
        body,
        out_shape=jax.ShapeDtypeStruct((tok_dev, query_width), jnp.bfloat16),
        in_specs=[in_smem] * 2 + [in_vmem] * (1 + len(suffix) + len(payloads)),
        out_specs=in_vmem,
        compiler_params=pltpu.CompilerParams(vmem_limit_bytes=VMEM_LIMIT),
        name="attention",
    )(lengths, tok_rank[None], queries, *suffix, *payloads)


def resident(arrays):
    count = len(arrays)

    def body(*refs):
        sources, targets, arrived = refs[:count], refs[count : 2 * count], refs[-1]
        copies = [
            pltpu.make_async_copy(sources[i], targets[i], arrived.at[i]) for i in range(count)
        ]
        for copy in copies:
            copy.start()
        for copy in copies:
            copy.wait()

    return pl.pallas_call(
        body,
        out_shape=[pltpu.VMEM(array.shape, array.dtype) for array in arrays],
        in_specs=[pl.BlockSpec(memory_space=pl.ANY)] * count,
        out_specs=[pl.BlockSpec(memory_space=pltpu.VMEM)] * count,
        scratch_shapes=[pltpu.SemaphoreType.DMA((count,))],
        compiler_params=pltpu.CompilerParams(vmem_limit_bytes=SMALL_LIMIT),
        name="resident",
    )(*arrays)


def slots_of(chosen, payloads, first_row, grp_count, tok_dev, experts, capacity):
    count = len(payloads)

    def body(chosen_ref, *refs):
        payload_refs, (pick_ref, weight_ref) = refs[:count], refs[count:]
        for i in range(count):
            for g in range(grp_count):
                pick, weight = picked_by(
                    payload_refs[i], first_row, chosen_ref[g], experts, tok_dev, capacity
                )
                pick_ref[i, pl.ds(g * capacity, capacity), :] = pick
                weight_ref[i, pl.ds(g * capacity, capacity), :] = jnp.broadcast_to(
                    weight, (capacity, 128)
                )

    in_vmem = pl.BlockSpec(memory_space=pltpu.VMEM)
    slots = grp_count * capacity
    return pl.pallas_call(
        body,
        out_shape=[
            jax.ShapeDtypeStruct((count, slots, tok_dev), jnp.bfloat16),
            jax.ShapeDtypeStruct((count, slots, 128), jnp.float32),
        ],
        in_specs=[pl.BlockSpec(memory_space=pltpu.SMEM)] + [in_vmem] * count,
        out_specs=[in_vmem] * 2,
        compiler_params=pltpu.CompilerParams(vmem_limit_bytes=SMALL_LIMIT),
        name="slots",
    )(chosen, *payloads)


def hidden_units(picks, places, blocks, gates, ups, capacity):
    count, grp_count = len(blocks), len(gates)
    model_width, hidden_width = gates[0].shape
    tile = width_tile(hidden_width, (256, 384, 128))
    pieces = [len(block) for block in blocks]
    columns = sum(pieces)

    def body(pick_ref, *refs):
        token_refs, refs = refs[:columns], refs[columns:]
        gate_refs, refs = refs[:grp_count], refs[grp_count:]
        up_refs, refs = refs[:grp_count], refs[grp_count:]
        out_ref, rows_ref = refs
        at = 0
        for i in range(count):
            pick = pick_ref[places[i]]
            first = 0
            for token_ref in token_refs[at : at + pieces[i]]:
                width = token_ref.shape[1]
                picked = jnp.dot(
                    pick, token_ref[...], preferred_element_type=jnp.float32
                ).astype(jnp.bfloat16)
                for g in range(grp_count):
                    rows_ref[g, pl.ds(i * capacity, capacity), pl.ds(first, width)] = picked[
                        g * capacity : (g + 1) * capacity
                    ]
                first += width
            at += pieces[i]
        for g in range(grp_count):
            for n in range(0, hidden_width, tile):
                own = pl.ds(n, tile)
                gate = jnp.dot(
                    rows_ref[g], gate_refs[g][:, own], preferred_element_type=jnp.float32
                )
                up = jnp.dot(rows_ref[g], up_refs[g][:, own], preferred_element_type=jnp.float32)
                out_ref[g, :, own] = (gate / (1.0 + jnp.exp(-gate)) * up).astype(jnp.bfloat16)

    in_vmem = pl.BlockSpec(memory_space=pltpu.VMEM)
    flat = [part for block in blocks for part in block]
    return pl.pallas_call(
        body,
        out_shape=jax.ShapeDtypeStruct((grp_count, count * capacity, hidden_width), jnp.bfloat16),
        in_specs=[in_vmem] * (1 + columns + 2 * grp_count),
        out_specs=in_vmem,
        scratch_shapes=[pltpu.VMEM((grp_count, count * capacity, model_width), jnp.bfloat16)],
        compiler_params=pltpu.CompilerParams(vmem_limit_bytes=SMALL_LIMIT),
        name="hidden_units",
    )(picks, *flat, *gates, *ups)


def token_sums(rank, picks, weights, places, hiddens, downs, tok_dev, capacity):
    count, grp_count, head_count = len(places), len(downs), len(hiddens)
    rows_each = hiddens[0].shape[2]
    share_width = downs[0].shape[1]
    tile = width_tile(share_width, (256, 640))

    def body(rank_ref, pick_ref, weight_ref, *refs):
        hidden_refs, refs = refs[:head_count], refs[head_count:]
        down_refs, out_refs = refs[:grp_count], refs[grp_count:]
        firsts = [
            pl.multiple_of((rank_ref[0] - k + head_count) % head_count * rows_each, rows_each)
            for k in range(head_count)
        ]
        for n in range(0, share_width, tile):
            own = pl.ds(n, tile)
            results = []
            for g in range(grp_count):
                result = None
                for k in range(head_count):
                    part = jnp.dot(
                        hidden_refs[k][g],
                        down_refs[g][pl.ds(firsts[k], rows_each), own],
                        preferred_element_type=jnp.float32,
                    )
                    result = part if result is None else result + part
                results.append(result)
            for i in range(count):
                scaled = jnp.concatenate(
                    [result[i * capacity : (i + 1) * capacity] for result in results], axis=0
                )
                scaled = (scaled * weight_ref[places[i], :, 0:1]).astype(jnp.bfloat16)
                out_refs[i][:, own] = lax.dot_general(
                    pick_ref[places[i]],
                    scaled,
                    (((0,), (0,)), ((), ())),
                    preferred_element_type=jnp.float32,
                )

    in_vmem = pl.BlockSpec(memory_space=pltpu.VMEM)
    return pl.pallas_call(
        body,
        out_shape=[jax.ShapeDtypeStruct((tok_dev, share_width), jnp.float32)] * count,
        in_specs=[pl.BlockSpec(memory_space=pltpu.SMEM)]
        + [in_vmem] * (2 + head_count + grp_count),
        out_specs=[in_vmem] * count,
        compiler_params=pltpu.CompilerParams(vmem_limit_bytes=SMALL_LIMIT),
        name="token_sums",
    )(rank, picks, weights, *hiddens, *downs)


def on_device(
    hidden_in,
    attn_gain,
    w_query,
    key_projection_weight,
    value_projection_weight,
    w_out,
    prefix_keys,
    cached_prefix_values,
    request_lengths,
    moe_gain,
    expert_ids,
    route_weights,
    w_gate,
    w_up,
    w_down,
):
    tok_count = lax.axis_size("tok")
    grp_count = lax.axis_size("grp")
    head_count = lax.axis_size("head")
    tok_rank = lax.axis_index("tok")
    grp_rank = lax.axis_index("grp")
    head_rank = lax.axis_index("head")
    tok_dev = hidden_in.shape[1]
    model_width = attn_gain.shape[0]
    head_dim = prefix_keys.shape[3]
    kv_local = prefix_keys.shape[2]
    kv_width = kv_local * head_dim
    group_length = w_query.shape[1] // kv_width
    prefix_total = prefix_keys.shape[1] * tok_count
    share_width = model_width // head_count
    experts = grp_count * tok_count
    top_count = expert_ids.shape[2]
    capacity = 4 * tok_dev * top_count // (3 * experts)

    quarter = hidden_in[0]
    features = side_by_side(quarter, "head")
    query_blocks = others_over(w_query, "grp")
    key_blocks = others_over(key_projection_weight, "grp")
    value_blocks = others_over(value_projection_weight, "grp")
    full_out = lax.all_gather(w_out, "grp", axis=0, tiled=True)

    payload = payload_of(
        prefix_keys[0].reshape(-1, kv_width),
        cached_prefix_values[0].reshape(-1, kv_width),
        expert_ids[0],
        route_weights[0],
        experts,
    )
    half_ring = tok_count // 2
    payloads = {0: payload}
    for distance in range(1, half_ring):
        payloads[distance] = along_ring(payload, distance)
        payloads[-distance] = along_ring(payload, -distance)
    payloads[half_ring] = along_ring(payload, half_ring)
    prefix_dev = prefix_keys.shape[1]


    attention_input = rms_norm(features, attn_gain)
    lengths = request_lengths[0]
    request_ends = jnp.cumsum(lengths)
    starts = request_ends - lengths
    token_index = tok_rank * tok_dev + jnp.arange(tok_dev, dtype=jnp.int32)
    own_start = jnp.max(
        jnp.where(starts[None, :] <= token_index[:, None], starts[None, :], 0), axis=1
    )
    token_positions = prefix_total + token_index - own_start
    key_product = split_product(attention_input, key_blocks, "grp")
    value_product = split_product(attention_input, value_blocks, "grp")
    query_product = split_product(attention_input, query_blocks, "grp")
    queries = apply_rotary(
        query_product.reshape(tok_dev, kv_local * group_length, head_dim), token_positions
    )
    queries = queries.reshape(tok_dev, kv_local * group_length * head_dim)
    request_suffix_keys = apply_rotary(
        key_product.reshape(tok_dev, kv_local, head_dim), token_positions
    )
    suffix = jnp.concatenate(
        [request_suffix_keys.reshape(tok_dev, kv_width), value_product.astype(jnp.bfloat16)], axis=1
    )
    longest = tok_dev * tok_count // 4
    reach_devices = (longest - 1 + tok_dev - 1) // tok_dev
    reached = [suffix] + [shifted(suffix, "tok", d) for d in range(1, reach_devices + 1)]
    (payloads, reached), expert_weights = lax.optimization_barrier(
        ((payloads, reached), (w_gate, w_up, w_down))
    )
    gate_blocks, up_blocks, down_blocks = [
        others_over(weight[0], "grp") for weight in expert_weights
    ]
    attended = attention(
        queries,
        reached,
        list(payloads.values()),
        prefix_dev,
        lengths,
        tok_rank,
        head_dim,
    )
    halves = []
    for half in range(2):
        columns = slice(half * model_width // 2, (half + 1) * model_width // 2)
        own = lax.dot_general(
            attended, full_out[columns], (((1,), (1,)), ((), ())), preferred_element_type=jnp.float32
        )
        mixed = own + features[:, columns].astype(jnp.float32)
        for arrived in others_over(own.astype(jnp.bfloat16), "head")[1:]:
            mixed = mixed + arrived.astype(jnp.float32)
        halves.append(mixed.astype(jnp.bfloat16))
    mid_full = jnp.concatenate(halves, axis=1)
    mid_quarter = lax.dynamic_slice_in_dim(mid_full, head_rank * share_width, share_width, 1)
    moe_in = rms_norm(mid_full, moe_gain)
    chosen = jnp.stack(
        [((grp_rank - d) % grp_count) * tok_count + tok_rank for d in range(grp_count)]
    ).astype(jnp.int32)
    place_of = {d: i for i, d in enumerate(payloads)}
    picks, slot_weights = slots_of(
        chosen, list(payloads.values()), prefix_dev, grp_count, tok_dev, experts, capacity
    )

    def units_of(chunk, blocks):
        places = [place_of[d] for d in chunk]
        return hidden_units(picks, places, blocks, gate_blocks, up_blocks, capacity)

    def sums_of(chunk, exchanged):
        places = [place_of[d] for d in chunk]
        sums = token_sums(
            head_rank[None], picks, slot_weights, places, exchanged, down_blocks, tok_dev, capacity
        )
        return dict(zip(chunk, sums))

    (gate_blocks, up_blocks), _ = lax.optimization_barrier(((gate_blocks, up_blocks), moe_in))
    held = resident(gate_blocks + up_blocks)
    gate_blocks, up_blocks = held[:grp_count], held[grp_count:]

    middle = model_width // 2
    ahead, behind = moe_in, moe_in
    chunk, blocks = [0], [[moe_in]]
    parts, waiting = {}, []
    for step in range(1, half_ring + 1):
        last = step == half_ring
        sent = (ahead[:, :middle], behind[:, middle:]) if last else (ahead, behind)
        arriving = (along_ring(sent[0], 1), along_ring(sent[1], -1))
        hidden = units_of(chunk, blocks)
        if waiting and not last:
            parts.update(sums_of(*waiting.pop(0)))
        (ahead, behind), hidden, parts = lax.optimization_barrier((arriving, hidden, parts))
        if step == 1:
            down_blocks, _ = lax.optimization_barrier((down_blocks, ahead))
            down_blocks = resident(down_blocks)
        waiting.append((chunk, others_over(hidden, "head")))
        chunk = [half_ring] if last else [step, -step]
        blocks = [[ahead, behind]] if last else [[ahead], [behind]]
    exchanged = others_over(units_of(chunk, blocks), "head")
    parts.update(sums_of(*waiting.pop(0)))
    exchanged, parts = lax.optimization_barrier((exchanged, parts))
    parts.update(sums_of(chunk, exchanged))

    def late():
        own, arrived = waiting.pop(0)
        arrived, _ = lax.optimization_barrier((arrived, parts[half_ring]))
        return sums_of(own, arrived)

    weighted = ring_sum(parts, late)
    output = (mid_quarter.astype(jnp.float32) + weighted).astype(jnp.bfloat16)
    return output[None]


def solution(mesh):
    return jax.shard_map(
        on_device,
        mesh=mesh,
        in_specs=(
            P("grp", "tok", "head"),
            P(),
            P("grp", "head"),
            P("grp", "head"),
            P("grp", "head"),
            P("grp", "head"),
            P("grp", "tok", "head", None),
            P("grp", "tok", "head", None),
            P("grp", None),
            P(),
            P("grp", "tok", None),
            P("grp", "tok", None),
            P(("grp", "tok"), None, "head"),
            P(("grp", "tok"), None, "head"),
            P(("grp", "tok"), None, "head"),
        ),
        out_specs=P("grp", "tok", "head"),
        check_vma=False,
    )
```

```python
import math

import jax
import jax.numpy as jnp
from jax import lax
from jax.experimental import pallas as pl
from jax.experimental.pallas import tpu as pltpu
from jax.sharding import PartitionSpec as P

ROPE_BASE = 500000.0
NORM_EPS = 1e-06
MASKED = -1e30
VMEM_LIMIT = 40 * 1024 * 1024
SMALL_LIMIT = 16 * 1024 * 1024


def shifted(block, axis, distance):
    devices = range(lax.axis_size(axis))
    route = [(i - distance, i) for i in devices if i - distance in devices]
    return lax.ppermute(block, axis, route)


def rms_norm(values_in, gain_vector):
    widened = values_in.astype(jnp.float32)
    mean_sq = jnp.mean(widened * widened, axis=-1, keepdims=True)
    return (widened * lax.rsqrt(mean_sq + NORM_EPS) * gain_vector.astype(jnp.float32)).astype(
        jnp.bfloat16
    )


def apply_rotary(product, token_positions):
    half_dim = product.shape[-1] // 2
    frequency = jnp.exp(
        jnp.arange(half_dim, dtype=jnp.float32) * (-2.0 * math.log(ROPE_BASE) / product.shape[-1])
    )
    angles = token_positions.astype(jnp.float32)[:, None] * frequency[None, :]
    cosine = jnp.cos(angles)[:, None, :]
    sine_part = jnp.sin(angles)[:, None, :]
    first_half = product[..., :half_dim]
    second_half = product[..., half_dim:]
    turned = jnp.concatenate(
        [
            first_half * cosine - second_half * sine_part,
            second_half * cosine + first_half * sine_part,
        ],
        axis=-1,
    )
    return turned.astype(jnp.bfloat16)


def turned_by(block, axis, distance):
    devices = lax.axis_size(axis)
    return lax.ppermute(block, axis, [(i, (i + distance) % devices) for i in range(devices)])


def along_ring(block, distance):
    devices = lax.axis_size("tok")
    order = list(range(0, devices, 2)) + list(range(devices - 1 - devices % 2, 0, -2))
    route = [(order[i], order[(i + distance) % devices]) for i in range(devices)]
    return lax.ppermute(block, "tok", route)


def ring_sum(parts):
    half = lax.axis_size("tok") // 2

    def hop(values, distance):
        return along_ring(values.astype(jnp.bfloat16), distance).astype(jnp.float32)

    left_high = hop(parts[half - 1][1], -1)
    right_low = hop(parts[1 - half][0], 1)
    left_low = hop(parts[half][0], -1)
    right_high = hop(parts[half][1], 1)
    for step in range(half - 1, 0, -1):
        left_low = hop(parts[step][0] + left_low, -1)
        right_high = hop(parts[-step][1] + right_high, 1)
        if step < half - 1:
            left_high = hop(parts[step][1] + left_high, -1)
            right_low = hop(parts[-step][0] + right_low, 1)
    low, high = parts[0]
    return jnp.concatenate([low + left_low + right_low, high + left_high + right_high], axis=1)


def side_by_side(block, axis):
    count = lax.axis_size(axis)
    rank = lax.axis_index(axis)
    blocks = others_over(block, axis)
    columns = []
    for place in range(count):
        column = blocks[0]
        for distance in range(1, count):
            column = jnp.where((rank - place) % count == distance, blocks[distance], column)
        columns.append(column)
    return jnp.concatenate(columns, axis=1)


def others_over(block, axis):
    return [block] + [turned_by(block, axis, d) for d in range(1, lax.axis_size(axis))]


def split_product(activations, blocks, axis):
    count = len(blocks)
    rank = lax.axis_index(axis)
    rows = blocks[0].shape[0]
    total = None
    for distance, block in enumerate(blocks):
        part = lax.dynamic_slice_in_dim(
            activations, ((rank - distance) % count) * rows, rows, 1
        )
        product = jnp.dot(part, block, preferred_element_type=jnp.float32)
        total = product if total is None else total + product
    return total


def width_tile(width, sizes):
    for size in sizes:
        if width % size == 0:
            return size
    return width


def picked_by(payload_ref, first_row, expert, experts, tok_dev, capacity):
    beside = payload_ref.shape[1] // tok_dev
    own = lax.broadcasted_iota(jnp.int32, (experts, tok_dev), 0) == expert

    def piece(i):
        rows = pl.ds(first_row + i // beside * experts, experts)
        columns = pl.ds(i % beside * tok_dev, tok_dev)
        values = payload_ref[rows, columns].astype(jnp.float32)
        return jnp.sum(jnp.where(own, values, 0.0), axis=0, keepdims=True)

    weight = piece(0) + piece(1) + piece(2)
    mask = piece(3)
    upto = lax.broadcasted_iota(jnp.int32, (tok_dev, tok_dev), 0) <= lax.broadcasted_iota(
        jnp.int32, (tok_dev, tok_dev), 1
    )
    upto = jnp.where(upto, 1.0, 0.0).astype(jnp.bfloat16)
    many = jnp.broadcast_to(mask, (16, tok_dev)).astype(jnp.bfloat16)
    place = jnp.dot(many, upto, preferred_element_type=jnp.float32)[0:1]
    place = jnp.where(mask > 0.5, place - 1.0, -1.0).astype(jnp.int32)
    slots = lax.broadcasted_iota(jnp.int32, (capacity, tok_dev), 0)
    pick = jnp.where(slots == place, 1.0, 0.0)
    return pick.astype(jnp.bfloat16), jnp.sum(pick * weight, axis=1, keepdims=True)


def payload_of(keys, values, ids, weights, experts):
    prefix_dev, kv_width = keys.shape
    tok_dev, top_count = ids.shape
    beside = 2 * kv_width // tok_dev
    rows = prefix_dev + 4 // beside * experts

    def body(keys_ref, values_ref, ids_ref, weights_ref, out_ref):
        out_ref[pl.ds(0, prefix_dev), pl.ds(0, kv_width)] = keys_ref[...]
        out_ref[pl.ds(0, prefix_dev), pl.ds(kv_width, kv_width)] = values_ref[...]
        lanes = lax.broadcasted_iota(jnp.int32, (tok_dev, 128), 1)
        dense = jnp.zeros((tok_dev, 128), jnp.float32)
        mask = jnp.zeros((tok_dev, 128), jnp.float32)
        for k in range(top_count):
            named = lanes == ids_ref[:, k : k + 1]
            dense = dense + jnp.where(named, weights_ref[:, k : k + 1], 0.0)
            mask = mask + jnp.where(named, 1.0, 0.0)
        rest = jnp.transpose(dense)[:experts]
        pieces = []
        for _ in range(3):
            pieces.append(rest.astype(jnp.bfloat16))
            rest = rest - pieces[-1].astype(jnp.float32)
        pieces.append(jnp.transpose(mask)[:experts].astype(jnp.bfloat16))
        for i, piece in enumerate(pieces):
            out_ref[
                pl.ds(prefix_dev + i // beside * experts, experts),
                pl.ds(i % beside * tok_dev, tok_dev),
            ] = piece

    return pl.pallas_call(
        body,
        out_shape=jax.ShapeDtypeStruct((rows, 2 * kv_width), jnp.bfloat16),
        name="payload",
    )(keys, values, ids, weights)


def attention(queries, suffix, payloads, prefix_dev, lengths, tok_rank, head_dim):
    tok_dev, query_width = queries.shape
    kv_width = suffix[0].shape[1] // 2
    kv_local = kv_width // head_dim
    group_length = query_width // kv_width
    requests = lengths.shape[0]
    prefix_rows = prefix_dev * len(payloads)
    keys_total = prefix_rows + tok_dev * len(suffix)

    def body(lengths_ref, rank_ref, query_ref, *refs):
        suffix_refs, refs = refs[: len(suffix)], refs[len(suffix) :]
        payload_refs, out_ref = refs[:-1], refs[-1]
        token = rank_ref[0] * tok_dev + lax.broadcasted_iota(jnp.int32, (tok_dev, tok_dev), 0)
        start = jnp.int32(0)
        own_start = jnp.zeros((tok_dev, tok_dev), jnp.int32)
        for request in range(requests):
            own_start = jnp.where(token >= start, jnp.maximum(own_start, start), own_start)
            start = start + lengths_ref[request]
        bias = [jnp.zeros((tok_dev, prefix_rows), jnp.float32)]
        for distance in range(len(suffix)):
            key = (rank_ref[0] - distance) * tok_dev + lax.broadcasted_iota(
                jnp.int32, (tok_dev, tok_dev), 1
            )
            bias.append(jnp.where((key >= own_start) & (key <= token), 0.0, MASKED))
        bias = jnp.concatenate(bias, axis=1)
        bias = jnp.concatenate([bias] * group_length, axis=0)
        for c in range(kv_local):
            columns = pl.ds(c * head_dim, head_dim)
            keys = jnp.concatenate(
                [ref[pl.ds(0, prefix_dev), columns] for ref in payload_refs]
                + [ref[:, columns] for ref in suffix_refs],
                axis=0,
            )
            columns = pl.ds(kv_width + c * head_dim, head_dim)
            values = jnp.concatenate(
                [ref[pl.ds(0, prefix_dev), columns] for ref in payload_refs]
                + [ref[:, columns] for ref in suffix_refs],
                axis=0,
            )
            first = c * group_length
            query = jnp.concatenate(
                [
                    query_ref[:, pl.ds((first + r) * head_dim, head_dim)]
                    for r in range(group_length)
                ],
                axis=0,
            )
            scores = lax.dot_general(
                query, keys, (((1,), (1,)), ((), ())), preferred_element_type=jnp.float32
            )
            scores = scores * head_dim ** (-0.5) + bias
            probs = jnp.exp(scores - jnp.max(scores, axis=1, keepdims=True))
            total = jnp.sum(probs, axis=1, keepdims=True)
            summed = jnp.dot(
                probs.astype(jnp.bfloat16), values, preferred_element_type=jnp.float32
            )
            attended = (summed / total).astype(jnp.bfloat16)
            for r in range(group_length):
                out_ref[:, pl.ds((first + r) * head_dim, head_dim)] = attended[
                    r * tok_dev : (r + 1) * tok_dev
                ]

    in_vmem = pl.BlockSpec(memory_space=pltpu.VMEM)
    in_smem = pl.BlockSpec(memory_space=pltpu.SMEM)
    return pl.pallas_call(
        body,
        out_shape=jax.ShapeDtypeStruct((tok_dev, query_width), jnp.bfloat16),
        in_specs=[in_smem] * 2 + [in_vmem] * (1 + len(suffix) + len(payloads)),
        out_specs=in_vmem,
        compiler_params=pltpu.CompilerParams(vmem_limit_bytes=VMEM_LIMIT),
        name="attention",
    )(lengths, tok_rank[None], queries, *suffix, *payloads)


def resident(arrays):
    count = len(arrays)

    def body(*refs):
        sources, targets, arrived = refs[:count], refs[count : 2 * count], refs[-1]
        copies = [
            pltpu.make_async_copy(sources[i], targets[i], arrived.at[i]) for i in range(count)
        ]
        for copy in copies:
            copy.start()
        for copy in copies:
            copy.wait()

    return pl.pallas_call(
        body,
        out_shape=[pltpu.VMEM(array.shape, array.dtype) for array in arrays],
        in_specs=[pl.BlockSpec(memory_space=pl.ANY)] * count,
        out_specs=[pl.BlockSpec(memory_space=pltpu.VMEM)] * count,
        scratch_shapes=[pltpu.SemaphoreType.DMA((count,))],
        compiler_params=pltpu.CompilerParams(vmem_limit_bytes=SMALL_LIMIT),
        name="resident",
    )(*arrays)


def slots_of(chosen, payloads, first_row, grp_count, tok_dev, experts, capacity):
    count = len(payloads)

    def body(chosen_ref, *refs):
        payload_refs, (pick_ref, weight_ref) = refs[:count], refs[count:]
        for i in range(count):
            for g in range(grp_count):
                pick, weight = picked_by(
                    payload_refs[i], first_row, chosen_ref[g], experts, tok_dev, capacity
                )
                pick_ref[i, pl.ds(g * capacity, capacity), :] = pick
                weight_ref[i, pl.ds(g * capacity, capacity), :] = jnp.broadcast_to(
                    weight, (capacity, 128)
                )

    in_vmem = pl.BlockSpec(memory_space=pltpu.VMEM)
    slots = grp_count * capacity
    return pl.pallas_call(
        body,
        out_shape=[
            jax.ShapeDtypeStruct((count, slots, tok_dev), jnp.bfloat16),
            jax.ShapeDtypeStruct((count, slots, 128), jnp.float32),
        ],
        in_specs=[pl.BlockSpec(memory_space=pltpu.SMEM)] + [in_vmem] * count,
        out_specs=[in_vmem] * 2,
        compiler_params=pltpu.CompilerParams(vmem_limit_bytes=SMALL_LIMIT),
        name="slots",
    )(chosen, *payloads)


def hidden_units(picks, places, blocks, gates, ups, capacity):
    count, grp_count = len(blocks), len(gates)
    model_width, hidden_width = gates[0].shape
    tile = width_tile(hidden_width, (256, 384, 128))
    pieces = [len(block) for block in blocks]
    columns = sum(pieces)

    def body(pick_ref, *refs):
        token_refs, refs = refs[:columns], refs[columns:]
        gate_refs, refs = refs[:grp_count], refs[grp_count:]
        up_refs, refs = refs[:grp_count], refs[grp_count:]
        out_ref, rows_ref = refs
        at = 0
        for i in range(count):
            pick = pick_ref[places[i]]
            first = 0
            for token_ref in token_refs[at : at + pieces[i]]:
                width = token_ref.shape[1]
                picked = jnp.dot(
                    pick, token_ref[...], preferred_element_type=jnp.float32
                ).astype(jnp.bfloat16)
                for g in range(grp_count):
                    rows_ref[g, pl.ds(i * capacity, capacity), pl.ds(first, width)] = picked[
                        g * capacity : (g + 1) * capacity
                    ]
                first += width
            at += pieces[i]
        for g in range(grp_count):
            for n in range(0, hidden_width, tile):
                own = pl.ds(n, tile)
                gate = jnp.dot(
                    rows_ref[g], gate_refs[g][:, own], preferred_element_type=jnp.float32
                )
                up = jnp.dot(rows_ref[g], up_refs[g][:, own], preferred_element_type=jnp.float32)
                out_ref[g, :, own] = (gate / (1.0 + jnp.exp(-gate)) * up).astype(jnp.bfloat16)

    in_vmem = pl.BlockSpec(memory_space=pltpu.VMEM)
    flat = [part for block in blocks for part in block]
    return pl.pallas_call(
        body,
        out_shape=jax.ShapeDtypeStruct((grp_count, count * capacity, hidden_width), jnp.bfloat16),
        in_specs=[in_vmem] * (1 + columns + 2 * grp_count),
        out_specs=in_vmem,
        scratch_shapes=[pltpu.VMEM((grp_count, count * capacity, model_width), jnp.bfloat16)],
        compiler_params=pltpu.CompilerParams(vmem_limit_bytes=SMALL_LIMIT),
        name="hidden_units",
    )(picks, *flat, *gates, *ups)


def token_sums(rank, picks, weights, places, hiddens, downs, tok_dev, capacity):
    count, grp_count, head_count = len(places), len(downs), len(hiddens)
    rows_each = hiddens[0].shape[2]
    share_width = downs[0].shape[1]
    middle = share_width // 2
    apart = 2 if middle % 128 == 0 else 1
    tile = share_width // apart

    def body(rank_ref, pick_ref, weight_ref, *refs):
        hidden_refs, refs = refs[:head_count], refs[head_count:]
        down_refs, out_refs = refs[:grp_count], refs[grp_count:]
        firsts = [
            pl.multiple_of((rank_ref[0] - k + head_count) % head_count * rows_each, rows_each)
            for k in range(head_count)
        ]
        for n in range(0, share_width, tile):
            own = pl.ds(n, tile)
            results = []
            for g in range(grp_count):
                result = None
                for k in range(head_count):
                    part = jnp.dot(
                        hidden_refs[k][g],
                        down_refs[g][pl.ds(firsts[k], rows_each), own],
                        preferred_element_type=jnp.float32,
                    )
                    result = part if result is None else result + part
                results.append(result)
            for i in range(count):
                scaled = jnp.concatenate(
                    [result[i * capacity : (i + 1) * capacity] for result in results], axis=0
                )
                scaled = (scaled * weight_ref[places[i], :, 0:1]).astype(jnp.bfloat16)
                out_refs[i * apart + n // tile][...] = lax.dot_general(
                    pick_ref[places[i]],
                    scaled,
                    (((0,), (0,)), ((), ())),
                    preferred_element_type=jnp.float32,
                )

    in_vmem = pl.BlockSpec(memory_space=pltpu.VMEM)
    sums = pl.pallas_call(
        body,
        out_shape=[jax.ShapeDtypeStruct((tok_dev, tile), jnp.float32)] * (count * apart),
        in_specs=[pl.BlockSpec(memory_space=pltpu.SMEM)]
        + [in_vmem] * (2 + head_count + grp_count),
        out_specs=[in_vmem] * (count * apart),
        compiler_params=pltpu.CompilerParams(vmem_limit_bytes=SMALL_LIMIT),
        name="token_sums",
    )(rank, picks, weights, *hiddens, *downs)
    if apart == 2:
        return list(zip(sums[::2], sums[1::2]))
    return [(both[:, :middle], both[:, middle:]) for both in sums]


def on_device(
    hidden_in,
    attn_gain,
    w_query,
    key_projection_weight,
    value_projection_weight,
    w_out,
    prefix_keys,
    cached_prefix_values,
    request_lengths,
    moe_gain,
    expert_ids,
    route_weights,
    w_gate,
    w_up,
    w_down,
):
    tok_count = lax.axis_size("tok")
    grp_count = lax.axis_size("grp")
    head_count = lax.axis_size("head")
    tok_rank = lax.axis_index("tok")
    grp_rank = lax.axis_index("grp")
    head_rank = lax.axis_index("head")
    tok_dev = hidden_in.shape[1]
    model_width = attn_gain.shape[0]
    head_dim = prefix_keys.shape[3]
    kv_local = prefix_keys.shape[2]
    kv_width = kv_local * head_dim
    group_length = w_query.shape[1] // kv_width
    prefix_total = prefix_keys.shape[1] * tok_count
    share_width = model_width // head_count
    experts = grp_count * tok_count
    top_count = expert_ids.shape[2]
    capacity = 4 * tok_dev * top_count // (3 * experts)

    quarter = hidden_in[0]
    features = side_by_side(quarter, "head")
    query_blocks = others_over(w_query, "grp")
    key_blocks = others_over(key_projection_weight, "grp")
    value_blocks = others_over(value_projection_weight, "grp")
    full_out = lax.all_gather(w_out, "grp", axis=0, tiled=True)

    payload = payload_of(
        prefix_keys[0].reshape(-1, kv_width),
        cached_prefix_values[0].reshape(-1, kv_width),
        expert_ids[0],
        route_weights[0],
        experts,
    )
    half_ring = tok_count // 2
    payloads = {0: payload}
    for distance in range(1, half_ring):
        payloads[distance] = along_ring(payload, distance)
        payloads[-distance] = along_ring(payload, -distance)
    payloads[half_ring] = along_ring(payload, half_ring)
    prefix_dev = prefix_keys.shape[1]


    attention_input = rms_norm(features, attn_gain)
    lengths = request_lengths[0]
    request_ends = jnp.cumsum(lengths)
    starts = request_ends - lengths
    token_index = tok_rank * tok_dev + jnp.arange(tok_dev, dtype=jnp.int32)
    own_start = jnp.max(
        jnp.where(starts[None, :] <= token_index[:, None], starts[None, :], 0), axis=1
    )
    token_positions = prefix_total + token_index - own_start
    key_product = split_product(attention_input, key_blocks, "grp")
    value_product = split_product(attention_input, value_blocks, "grp")
    query_product = split_product(attention_input, query_blocks, "grp")
    queries = apply_rotary(
        query_product.reshape(tok_dev, kv_local * group_length, head_dim), token_positions
    )
    queries = queries.reshape(tok_dev, kv_local * group_length * head_dim)
    request_suffix_keys = apply_rotary(
        key_product.reshape(tok_dev, kv_local, head_dim), token_positions
    )
    suffix = jnp.concatenate(
        [request_suffix_keys.reshape(tok_dev, kv_width), value_product.astype(jnp.bfloat16)], axis=1
    )
    longest = tok_dev * tok_count // 4
    reach_devices = (longest - 1 + tok_dev - 1) // tok_dev
    reached = [suffix] + [shifted(suffix, "tok", d) for d in range(1, reach_devices + 1)]
    (payloads, reached), expert_weights = lax.optimization_barrier(
        ((payloads, reached), (w_gate, w_up, w_down))
    )
    gate_blocks, up_blocks, down_blocks = [
        others_over(weight[0], "grp") for weight in expert_weights
    ]
    attended = attention(
        queries,
        reached,
        list(payloads.values()),
        prefix_dev,
        lengths,
        tok_rank,
        head_dim,
    )
    halves = []
    for half in range(2):
        columns = slice(half * model_width // 2, (half + 1) * model_width // 2)
        own = lax.dot_general(
            attended, full_out[columns], (((1,), (1,)), ((), ())), preferred_element_type=jnp.float32
        )
        mixed = own + features[:, columns].astype(jnp.float32)
        for arrived in others_over(own.astype(jnp.bfloat16), "head")[1:]:
            mixed = mixed + arrived.astype(jnp.float32)
        halves.append(mixed.astype(jnp.bfloat16))
    mid_full = jnp.concatenate(halves, axis=1)
    mid_quarter = lax.dynamic_slice_in_dim(mid_full, head_rank * share_width, share_width, 1)
    moe_in = rms_norm(mid_full, moe_gain)
    chosen = jnp.stack(
        [((grp_rank - d) % grp_count) * tok_count + tok_rank for d in range(grp_count)]
    ).astype(jnp.int32)
    place_of = {d: i for i, d in enumerate(payloads)}
    picks, slot_weights = slots_of(
        chosen, list(payloads.values()), prefix_dev, grp_count, tok_dev, experts, capacity
    )

    def units_of(chunk, blocks):
        places = [place_of[d] for d in chunk]
        return hidden_units(picks, places, blocks, gate_blocks, up_blocks, capacity)

    def sums_of(chunk, exchanged):
        places = [place_of[d] for d in chunk]
        sums = token_sums(
            head_rank[None], picks, slot_weights, places, exchanged, down_blocks, tok_dev, capacity
        )
        return dict(zip(chunk, sums))

    (gate_blocks, up_blocks), _ = lax.optimization_barrier(((gate_blocks, up_blocks), moe_in))
    held = resident(gate_blocks + up_blocks)
    gate_blocks, up_blocks = held[:grp_count], held[grp_count:]

    middle = model_width // 2
    ahead, behind = moe_in, moe_in
    chunk, blocks = [0], [[moe_in]]
    parts, waiting = {}, []
    for step in range(1, half_ring + 1):
        last = step == half_ring
        sent = (ahead[:, :middle], behind[:, middle:]) if last else (ahead, behind)
        arriving = (along_ring(sent[0], 1), along_ring(sent[1], -1))
        hidden = units_of(chunk, blocks)
        if waiting and not last:
            parts.update(sums_of(*waiting.pop(0)))
        (ahead, behind), hidden, parts = lax.optimization_barrier((arriving, hidden, parts))
        if step == 1:
            down_blocks, _ = lax.optimization_barrier((down_blocks, ahead))
            down_blocks = resident(down_blocks)
        waiting.append((chunk, others_over(hidden, "head")))
        chunk = [half_ring] if last else [step, -step]
        blocks = [[ahead, behind]] if last else [[ahead], [behind]]
    exchanged = others_over(units_of(chunk, blocks), "head")
    early = sums_of(*waiting.pop())
    exchanged, early = lax.optimization_barrier((exchanged, early))
    parts = {**parts, **early, **sums_of(chunk, exchanged)}
    for own, arrived in waiting:
        arrived, _ = lax.optimization_barrier((arrived, parts[half_ring]))
        parts = {**parts, **sums_of(own, arrived)}
    weighted = ring_sum(parts)
    output = (mid_quarter.astype(jnp.float32) + weighted).astype(jnp.bfloat16)
    return output[None]


def solution(mesh):
    return jax.shard_map(
        on_device,
        mesh=mesh,
        in_specs=(
            P("grp", "tok", "head"),
            P(),
            P("grp", "head"),
            P("grp", "head"),
            P("grp", "head"),
            P("grp", "head"),
            P("grp", "tok", "head", None),
            P("grp", "tok", "head", None),
            P("grp", None),
            P(),
            P("grp", "tok", None),
            P("grp", "tok", None),
            P(("grp", "tok"), None, "head"),
            P(("grp", "tok"), None, "head"),
            P(("grp", "tok"), None, "head"),
        ),
        out_specs=P("grp", "tok", "head"),
        check_vma=False,
    )
```

```python
import math

import jax
import jax.numpy as jnp
from jax import lax
from jax.experimental import pallas as pl
from jax.experimental.pallas import tpu as pltpu
from jax.sharding import PartitionSpec as P

ROPE_BASE = 500000.0
NORM_EPS = 1e-06
MASKED = -1e30
PAYLOAD_ROWS = 160
VMEM_LIMIT = 40 * 1024 * 1024
SMALL_LIMIT = 16 * 1024 * 1024


def shifted(block, axis, distance):
    devices = range(lax.axis_size(axis))
    route = [(i - distance, i) for i in devices if i - distance in devices]
    return lax.ppermute(block, axis, route)


def rms_norm(values_in, gain_vector):
    widened = values_in.astype(jnp.float32)
    mean_sq = jnp.mean(widened * widened, axis=-1, keepdims=True)
    return (widened * lax.rsqrt(mean_sq + NORM_EPS) * gain_vector.astype(jnp.float32)).astype(
        jnp.bfloat16
    )


def apply_rotary(product, token_positions):
    half_dim = product.shape[-1] // 2
    frequency = jnp.exp(
        jnp.arange(half_dim, dtype=jnp.float32) * (-2.0 * math.log(ROPE_BASE) / product.shape[-1])
    )
    angles = token_positions.astype(jnp.float32)[:, None] * frequency[None, :]
    cosine = jnp.cos(angles)[:, None, :]
    sine_part = jnp.sin(angles)[:, None, :]
    first_half = product[..., :half_dim]
    second_half = product[..., half_dim:]
    turned = jnp.concatenate(
        [
            first_half * cosine - second_half * sine_part,
            second_half * cosine + first_half * sine_part,
        ],
        axis=-1,
    )
    return turned.astype(jnp.bfloat16)


def turned_by(block, axis, distance):
    devices = lax.axis_size(axis)
    return lax.ppermute(block, axis, [(i, (i + distance) % devices) for i in range(devices)])


def ring_order(devices):
    return list(range(0, devices, 2)) + list(range(devices - 1 - devices % 2, 0, -2))


def along_ring(block, distance):
    devices = lax.axis_size("tok")
    order = ring_order(devices)
    route = [(order[i], order[(i + distance) % devices]) for i in range(devices)]
    return lax.ppermute(block, "tok", route)


def ring_sum(parts, late):
    half = lax.axis_size("tok") // 2
    middle = parts[0].shape[1] // 2
    left = along_ring(parts[half][:, :middle].astype(jnp.bfloat16), -1)
    right = along_ring(parts[half][:, middle:].astype(jnp.bfloat16), 1)
    parts = {**parts, **late()}
    left, right, parts = lax.optimization_barrier((left, right, parts))
    left = parts[half - 1] + jnp.pad(
        left.astype(jnp.float32), ((0, 0), (0, parts[0].shape[1] - middle))
    )
    right = parts[1 - half] + jnp.pad(right.astype(jnp.float32), ((0, 0), (middle, 0)))
    for step in range(half - 2, -1, -1):
        left = along_ring(left.astype(jnp.bfloat16), -1).astype(jnp.float32)
        right = along_ring(right.astype(jnp.bfloat16), 1).astype(jnp.float32)
        if step:
            left = left + parts[step]
            right = right + parts[-step]
    return parts[0] + left + right


def in_order(blocks, axis):
    count = lax.axis_size(axis)
    rank = lax.axis_index(axis)
    columns = []
    for place in range(count):
        column = blocks[0]
        for distance in range(1, count):
            column = jnp.where((rank - place) % count == distance, blocks[distance], column)
        columns.append(column)
    return jnp.concatenate(columns, axis=1)


def others_over(block, axis):
    return [block] + [turned_by(block, axis, d) for d in range(1, lax.axis_size(axis))]


def split_product(activations, blocks, axis):
    count = len(blocks)
    rank = lax.axis_index(axis)
    rows = blocks[0].shape[0]
    total = None
    for distance, block in enumerate(blocks):
        part = lax.dynamic_slice_in_dim(
            activations, ((rank - distance) % count) * rows, rows, 1
        )
        product = jnp.dot(part, block, preferred_element_type=jnp.float32)
        total = product if total is None else total + product
    return total


def width_tile(width, sizes):
    for size in sizes:
        if width % size == 0:
            return size
    return width


def picked_by(payload_ref, first_row, expert, experts, tok_dev, capacity):
    beside = payload_ref.shape[1] // tok_dev
    own = lax.broadcasted_iota(jnp.int32, (experts, tok_dev), 0) == expert

    def piece(i):
        rows = pl.ds(first_row + i // beside * experts, experts)
        columns = pl.ds(i % beside * tok_dev, tok_dev)
        values = payload_ref[rows, columns].astype(jnp.float32)
        return jnp.sum(jnp.where(own, values, 0.0), axis=0, keepdims=True)

    weight = piece(0) + piece(1) + piece(2)
    mask = piece(3)
    upto = lax.broadcasted_iota(jnp.int32, (tok_dev, tok_dev), 0) <= lax.broadcasted_iota(
        jnp.int32, (tok_dev, tok_dev), 1
    )
    upto = jnp.where(upto, 1.0, 0.0).astype(jnp.bfloat16)
    many = jnp.broadcast_to(mask, (16, tok_dev)).astype(jnp.bfloat16)
    place = jnp.dot(many, upto, preferred_element_type=jnp.float32)[0:1]
    place = jnp.where(mask > 0.5, place - 1.0, -1.0).astype(jnp.int32)
    slots = lax.broadcasted_iota(jnp.int32, (capacity, tok_dev), 0)
    pick = jnp.where(slots == place, 1.0, 0.0)
    return pick.astype(jnp.bfloat16), jnp.sum(pick * weight, axis=1, keepdims=True)


def payload_of(keys, values, ids, weights, experts):
    prefix_dev, kv_width = keys.shape
    tok_dev, top_count = ids.shape
    beside = 2 * kv_width // tok_dev
    rows = max(prefix_dev + 4 // beside * experts, PAYLOAD_ROWS)

    def body(keys_ref, values_ref, ids_ref, weights_ref, out_ref):
        out_ref[pl.ds(0, prefix_dev), pl.ds(0, kv_width)] = keys_ref[...]
        out_ref[pl.ds(0, prefix_dev), pl.ds(kv_width, kv_width)] = values_ref[...]
        lanes = lax.broadcasted_iota(jnp.int32, (tok_dev, 128), 1)
        dense = jnp.zeros((tok_dev, 128), jnp.float32)
        mask = jnp.zeros((tok_dev, 128), jnp.float32)
        for k in range(top_count):
            named = lanes == ids_ref[:, k : k + 1]
            dense = dense + jnp.where(named, weights_ref[:, k : k + 1], 0.0)
            mask = mask + jnp.where(named, 1.0, 0.0)
        rest = jnp.transpose(dense)[:experts]
        pieces = []
        for _ in range(3):
            pieces.append(rest.astype(jnp.bfloat16))
            rest = rest - pieces[-1].astype(jnp.float32)
        pieces.append(jnp.transpose(mask)[:experts].astype(jnp.bfloat16))
        for i, piece in enumerate(pieces):
            out_ref[
                pl.ds(prefix_dev + i // beside * experts, experts),
                pl.ds(i % beside * tok_dev, tok_dev),
            ] = piece
        used = prefix_dev + 4 // beside * experts
        if rows > used:
            out_ref[pl.ds(used, rows - used), :] = jnp.zeros(
                (rows - used, 2 * kv_width), jnp.bfloat16
            )

    return pl.pallas_call(
        body,
        out_shape=jax.ShapeDtypeStruct((rows, 2 * kv_width), jnp.bfloat16),
        name="payload",
    )(keys, values, ids, weights)


def attention(queries, suffix, payload, prefix_dev, lengths, tok_rank, head_dim):
    tok_dev, query_width = queries.shape
    kv_width = suffix[0].shape[1] // 2
    kv_local = kv_width // head_dim
    group_length = query_width // kv_width
    requests = lengths.shape[0]
    prefix_rows = prefix_dev * payload.shape[0]
    keys_total = prefix_rows + tok_dev * len(suffix)

    def body(lengths_ref, rank_ref, query_ref, *refs):
        suffix_refs, refs = refs[: len(suffix)], refs[len(suffix) :]
        payload_ref, out_ref = refs
        token = rank_ref[0] * tok_dev + lax.broadcasted_iota(jnp.int32, (tok_dev, tok_dev), 0)
        start = jnp.int32(0)
        own_start = jnp.zeros((tok_dev, tok_dev), jnp.int32)
        for request in range(requests):
            own_start = jnp.where(token >= start, jnp.maximum(own_start, start), own_start)
            start = start + lengths_ref[request]
        bias = [jnp.zeros((tok_dev, prefix_rows), jnp.float32)]
        for distance in range(len(suffix)):
            key = (rank_ref[0] - distance) * tok_dev + lax.broadcasted_iota(
                jnp.int32, (tok_dev, tok_dev), 1
            )
            bias.append(jnp.where((key >= own_start) & (key <= token), 0.0, MASKED))
        bias = jnp.concatenate(bias, axis=1)
        bias = jnp.concatenate([bias] * group_length, axis=0)
        for c in range(kv_local):
            columns = pl.ds(c * head_dim, head_dim)
            keys = jnp.concatenate(
                [
                    payload_ref[block, pl.ds(0, prefix_dev), columns]
                    for block in range(payload.shape[0])
                ]
                + [ref[:, columns] for ref in suffix_refs],
                axis=0,
            )
            columns = pl.ds(kv_width + c * head_dim, head_dim)
            values = jnp.concatenate(
                [
                    payload_ref[block, pl.ds(0, prefix_dev), columns]
                    for block in range(payload.shape[0])
                ]
                + [ref[:, columns] for ref in suffix_refs],
                axis=0,
            )
            first = c * group_length
            query = jnp.concatenate(
                [
                    query_ref[:, pl.ds((first + r) * head_dim, head_dim)]
                    for r in range(group_length)
                ],
                axis=0,
            )
            scores = lax.dot_general(
                query, keys, (((1,), (1,)), ((), ())), preferred_element_type=jnp.float32
            )
            scores = scores * head_dim ** (-0.5) + bias
            probs = jnp.exp(scores - jnp.max(scores, axis=1, keepdims=True))
            total = jnp.sum(probs, axis=1, keepdims=True)
            summed = jnp.dot(
                probs.astype(jnp.bfloat16), values, preferred_element_type=jnp.float32
            )
            attended = (summed / total).astype(jnp.bfloat16)
            for r in range(group_length):
                out_ref[:, pl.ds((first + r) * head_dim, head_dim)] = attended[
                    r * tok_dev : (r + 1) * tok_dev
                ]

    in_vmem = pl.BlockSpec(memory_space=pltpu.VMEM)
    in_smem = pl.BlockSpec(memory_space=pltpu.SMEM)
    return pl.pallas_call(
        body,
        out_shape=jax.ShapeDtypeStruct((tok_dev, query_width), jnp.bfloat16),
        in_specs=[in_smem] * 2 + [in_vmem] * (2 + len(suffix)),
        out_specs=in_vmem,
        compiler_params=pltpu.CompilerParams(vmem_limit_bytes=VMEM_LIMIT),
        name="attention",
    )(lengths, tok_rank[None], queries, *suffix, payload)


def resident(arrays):
    count = len(arrays)

    def body(*refs):
        sources, targets, arrived = refs[:count], refs[count : 2 * count], refs[-1]
        copies = [
            pltpu.make_async_copy(sources[i], targets[i], arrived.at[i]) for i in range(count)
        ]
        for copy in copies:
            copy.start()
        for copy in copies:
            copy.wait()

    return pl.pallas_call(
        body,
        out_shape=[pltpu.VMEM(array.shape, array.dtype) for array in arrays],
        in_specs=[pl.BlockSpec(memory_space=pl.ANY)] * count,
        out_specs=[pl.BlockSpec(memory_space=pltpu.VMEM)] * count,
        scratch_shapes=[pltpu.SemaphoreType.DMA((count,))],
        compiler_params=pltpu.CompilerParams(vmem_limit_bytes=SMALL_LIMIT),
        name="resident",
    )(*arrays)


def slots_of(chosen, sources, payload, first_row, grp_count, tok_dev, experts, capacity):
    count = payload.shape[0]

    def body(chosen_ref, source_ref, payload_ref, pick_ref, weight_ref):
        for i in range(count):
            for g in range(grp_count):
                pick, weight = picked_by(
                    payload_ref.at[source_ref[i]],
                    first_row,
                    chosen_ref[g],
                    experts,
                    tok_dev,
                    capacity,
                )
                pick_ref[i, pl.ds(g * capacity, capacity), :] = pick
                weight_ref[i, pl.ds(g * capacity, capacity), :] = jnp.broadcast_to(
                    weight, (capacity, 128)
                )

    in_vmem = pl.BlockSpec(memory_space=pltpu.VMEM)
    slots = grp_count * capacity
    return pl.pallas_call(
        body,
        out_shape=[
            jax.ShapeDtypeStruct((count, slots, tok_dev), jnp.bfloat16),
            jax.ShapeDtypeStruct((count, slots, 128), jnp.float32),
        ],
        in_specs=[pl.BlockSpec(memory_space=pltpu.SMEM)] * 2 + [in_vmem],
        out_specs=[in_vmem] * 2,
        compiler_params=pltpu.CompilerParams(vmem_limit_bytes=SMALL_LIMIT),
        name="slots",
    )(chosen, sources, payload)


def hidden_units(picks, places, blocks, gates, ups, capacity):
    count, grp_count = len(blocks), len(gates)
    model_width, hidden_width = gates[0].shape
    tile = width_tile(hidden_width, (256, 384, 128))
    pieces = [len(block) for block in blocks]
    columns = sum(pieces)

    def body(pick_ref, *refs):
        token_refs, refs = refs[:columns], refs[columns:]
        gate_refs, refs = refs[:grp_count], refs[grp_count:]
        up_refs, refs = refs[:grp_count], refs[grp_count:]
        out_ref, rows_ref = refs
        at = 0
        for i in range(count):
            pick = pick_ref[places[i]]
            first = 0
            for token_ref in token_refs[at : at + pieces[i]]:
                width = token_ref.shape[1]
                picked = jnp.dot(
                    pick, token_ref[...], preferred_element_type=jnp.float32
                ).astype(jnp.bfloat16)
                for g in range(grp_count):
                    rows_ref[g, pl.ds(i * capacity, capacity), pl.ds(first, width)] = picked[
                        g * capacity : (g + 1) * capacity
                    ]
                first += width
            at += pieces[i]
        for g in range(grp_count):
            for n in range(0, hidden_width, tile):
                own = pl.ds(n, tile)
                gate = jnp.dot(
                    rows_ref[g], gate_refs[g][:, own], preferred_element_type=jnp.float32
                )
                up = jnp.dot(rows_ref[g], up_refs[g][:, own], preferred_element_type=jnp.float32)
                out_ref[g, :, own] = (gate / (1.0 + jnp.exp(-gate)) * up).astype(jnp.bfloat16)

    in_vmem = pl.BlockSpec(memory_space=pltpu.VMEM)
    flat = [part for block in blocks for part in block]
    return pl.pallas_call(
        body,
        out_shape=jax.ShapeDtypeStruct((grp_count, count * capacity, hidden_width), jnp.bfloat16),
        in_specs=[in_vmem] * (1 + columns + 2 * grp_count),
        out_specs=in_vmem,
        scratch_shapes=[pltpu.VMEM((grp_count, count * capacity, model_width), jnp.bfloat16)],
        compiler_params=pltpu.CompilerParams(vmem_limit_bytes=SMALL_LIMIT),
        name="hidden_units",
    )(picks, *flat, *gates, *ups)


def token_sums(rank, picks, weights, places, hiddens, downs, tok_dev, capacity):
    count, grp_count, head_count = len(places), len(downs), len(hiddens)
    rows_each = hiddens[0].shape[2]
    share_width = downs[0].shape[1]
    tile = width_tile(share_width, (256, 640))

    def body(rank_ref, pick_ref, weight_ref, *refs):
        hidden_refs, refs = refs[:head_count], refs[head_count:]
        down_refs, out_refs = refs[:grp_count], refs[grp_count:]
        firsts = [
            pl.multiple_of((rank_ref[0] - k + head_count) % head_count * rows_each, rows_each)
            for k in range(head_count)
        ]
        for n in range(0, share_width, tile):
            own = pl.ds(n, tile)
            results = []
            for g in range(grp_count):
                result = None
                for k in range(head_count):
                    part = jnp.dot(
                        hidden_refs[k][g],
                        down_refs[g][pl.ds(firsts[k], rows_each), own],
                        preferred_element_type=jnp.float32,
                    )
                    result = part if result is None else result + part
                results.append(result)
            for i in range(count):
                scaled = jnp.concatenate(
                    [result[i * capacity : (i + 1) * capacity] for result in results], axis=0
                )
                scaled = (scaled * weight_ref[places[i], :, 0:1]).astype(jnp.bfloat16)
                out_refs[i][:, own] = lax.dot_general(
                    pick_ref[places[i]],
                    scaled,
                    (((0,), (0,)), ((), ())),
                    preferred_element_type=jnp.float32,
                )

    in_vmem = pl.BlockSpec(memory_space=pltpu.VMEM)
    return pl.pallas_call(
        body,
        out_shape=[jax.ShapeDtypeStruct((tok_dev, share_width), jnp.float32)] * count,
        in_specs=[pl.BlockSpec(memory_space=pltpu.SMEM)]
        + [in_vmem] * (2 + head_count + grp_count),
        out_specs=[in_vmem] * count,
        compiler_params=pltpu.CompilerParams(vmem_limit_bytes=SMALL_LIMIT),
        name="token_sums",
    )(rank, picks, weights, *hiddens, *downs)


def on_device(
    hidden_in,
    attn_gain,
    w_query,
    key_projection_weight,
    value_projection_weight,
    w_out,
    prefix_keys,
    cached_prefix_values,
    request_lengths,
    moe_gain,
    expert_ids,
    route_weights,
    w_gate,
    w_up,
    w_down,
):
    tok_count = lax.axis_size("tok")
    grp_count = lax.axis_size("grp")
    head_count = lax.axis_size("head")
    tok_rank = lax.axis_index("tok")
    grp_rank = lax.axis_index("grp")
    head_rank = lax.axis_index("head")
    tok_dev = hidden_in.shape[1]
    model_width = attn_gain.shape[0]
    head_dim = prefix_keys.shape[3]
    kv_local = prefix_keys.shape[2]
    kv_width = kv_local * head_dim
    group_length = w_query.shape[1] // kv_width
    prefix_total = prefix_keys.shape[1] * tok_count
    share_width = model_width // head_count
    experts = grp_count * tok_count
    top_count = expert_ids.shape[2]
    capacity = 4 * tok_dev * top_count // (3 * experts)

    quarter = hidden_in[0]
    features = in_order(others_over(quarter, "head"), "head")
    query_blocks = others_over(w_query, "grp")
    key_blocks = others_over(key_projection_weight, "grp")
    value_blocks = others_over(value_projection_weight, "grp")
    out_blocks = others_over(w_out, "grp")

    payload = payload_of(
        prefix_keys[0].reshape(-1, kv_width),
        cached_prefix_values[0].reshape(-1, kv_width),
        expert_ids[0],
        route_weights[0],
        experts,
    )
    half_ring = tok_count // 2
    payload = lax.all_gather(payload, "tok", axis=0, tiled=True).reshape((tok_count,) + payload.shape)
    prefix_dev = prefix_keys.shape[1]


    attention_input = rms_norm(features, attn_gain)
    lengths = request_lengths[0]
    request_ends = jnp.cumsum(lengths)
    starts = request_ends - lengths
    token_index = tok_rank * tok_dev + jnp.arange(tok_dev, dtype=jnp.int32)
    own_start = jnp.max(
        jnp.where(starts[None, :] <= token_index[:, None], starts[None, :], 0), axis=1
    )
    token_positions = prefix_total + token_index - own_start
    key_product = split_product(attention_input, key_blocks, "grp")
    value_product = split_product(attention_input, value_blocks, "grp")
    query_product = split_product(attention_input, query_blocks, "grp")
    queries = apply_rotary(
        query_product.reshape(tok_dev, kv_local * group_length, head_dim), token_positions
    )
    queries = queries.reshape(tok_dev, kv_local * group_length * head_dim)
    request_suffix_keys = apply_rotary(
        key_product.reshape(tok_dev, kv_local, head_dim), token_positions
    )
    suffix = jnp.concatenate(
        [request_suffix_keys.reshape(tok_dev, kv_width), value_product.astype(jnp.bfloat16)], axis=1
    )
    longest = tok_dev * tok_count // 4
    reach_devices = (longest - 1 + tok_dev - 1) // tok_dev
    reached = [suffix] + [shifted(suffix, "tok", d) for d in range(1, reach_devices + 1)]
    (payload, reached), expert_weights = lax.optimization_barrier(
        ((payload, reached), (w_gate, w_up, w_down))
    )
    gate_blocks, up_blocks, down_blocks = [
        others_over(weight[0], "grp") for weight in expert_weights
    ]
    attended = attention(
        queries,
        reached,
        payload,
        prefix_dev,
        lengths,
        tok_rank,
        head_dim,
    )
    out_rows = w_out.shape[0]
    mixed_blocks = []
    for distance, block in enumerate(out_blocks):
        own = lax.dot_general(
            attended, block, (((1,), (1,)), ((), ())), preferred_element_type=jnp.float32
        )
        first = (grp_rank - distance) % grp_count * out_rows
        mixed = own + lax.dynamic_slice_in_dim(features, first, out_rows, 1).astype(jnp.float32)
        for arrived in others_over(own.astype(jnp.bfloat16), "head")[1:]:
            mixed = mixed + arrived.astype(jnp.float32)
        mixed_blocks.append(mixed.astype(jnp.bfloat16))
    mid_full = in_order(mixed_blocks, "grp")
    mid_quarter = lax.dynamic_slice_in_dim(mid_full, head_rank * share_width, share_width, 1)
    moe_in = rms_norm(mid_full, moe_gain)
    chosen = jnp.stack(
        [((grp_rank - d) % grp_count) * tok_count + tok_rank for d in range(grp_count)]
    ).astype(jnp.int32)
    distances = [0] + [d for step in range(1, half_ring) for d in (step, -step)] + [half_ring]
    place_of = {d: i for i, d in enumerate(distances)}
    order = ring_order(tok_count)
    sources = [
        [order[(order.index(device) - d) % tok_count] for d in distances]
        for device in range(tok_count)
    ]
    sources = lax.dynamic_index_in_dim(
        jnp.array(sources, jnp.int32), tok_rank, axis=0, keepdims=False
    )
    picks, slot_weights = slots_of(
        chosen, sources, payload, prefix_dev, grp_count, tok_dev, experts, capacity
    )

    def units_of(chunk, blocks):
        places = [place_of[d] for d in chunk]
        return hidden_units(picks, places, blocks, gate_blocks, up_blocks, capacity)

    def sums_of(chunk, exchanged):
        places = [place_of[d] for d in chunk]
        sums = token_sums(
            head_rank[None], picks, slot_weights, places, exchanged, down_blocks, tok_dev, capacity
        )
        return dict(zip(chunk, sums))

    (gate_blocks, up_blocks), _ = lax.optimization_barrier(((gate_blocks, up_blocks), moe_in))
    held = resident(gate_blocks + up_blocks)
    gate_blocks, up_blocks = held[:grp_count], held[grp_count:]

    middle = model_width // 2
    ahead, behind = moe_in, moe_in
    chunk, blocks = [0], [[moe_in]]
    parts, waiting = {}, []
    for step in range(1, half_ring + 1):
        last = step == half_ring
        sent = (ahead[:, :middle], behind[:, middle:]) if last else (ahead, behind)
        arriving = (along_ring(sent[0], 1), along_ring(sent[1], -1))
        hidden = units_of(chunk, blocks)
        if waiting and not last:
            parts.update(sums_of(*waiting.pop(0)))
        (ahead, behind), hidden, parts = lax.optimization_barrier((arriving, hidden, parts))
        if step == 1:
            down_blocks, _ = lax.optimization_barrier((down_blocks, ahead))
            down_blocks = resident(down_blocks)
        waiting.append((chunk, others_over(hidden, "head")))
        chunk = [half_ring] if last else [step, -step]
        blocks = [[ahead, behind]] if last else [[ahead], [behind]]
    exchanged = others_over(units_of(chunk, blocks), "head")
    parts.update(sums_of(*waiting.pop(0)))
    exchanged, parts = lax.optimization_barrier((exchanged, parts))
    parts.update(sums_of(chunk, exchanged))

    def late():
        own, arrived = waiting.pop(0)
        arrived, _ = lax.optimization_barrier((arrived, parts[half_ring]))
        return sums_of(own, arrived)

    weighted = ring_sum(parts, late)
    output = (mid_quarter.astype(jnp.float32) + weighted).astype(jnp.bfloat16)
    return output[None]


def solution(mesh):
    return jax.shard_map(
        on_device,
        mesh=mesh,
        in_specs=(
            P("grp", "tok", "head"),
            P(),
            P("grp", "head"),
            P("grp", "head"),
            P("grp", "head"),
            P("grp", "head"),
            P("grp", "tok", "head", None),
            P("grp", "tok", "head", None),
            P("grp", None),
            P(),
            P("grp", "tok", None),
            P("grp", "tok", None),
            P(("grp", "tok"), None, "head"),
            P(("grp", "tok"), None, "head"),
            P(("grp", "tok"), None, "head"),
        ),
        out_specs=P("grp", "tok", "head"),
        check_vma=False,
    )
```

```python
import math

import jax
import jax.numpy as jnp
from jax import lax
from jax.experimental import pallas as pl
from jax.experimental.pallas import tpu as pltpu
from jax.sharding import PartitionSpec as P

ROPE_BASE = 500000.0
NORM_EPS = 1e-06
MASKED = -1e30
VMEM_LIMIT = 40 * 1024 * 1024
SMALL_LIMIT = 16 * 1024 * 1024


def shifted(block, axis, distance):
    devices = range(lax.axis_size(axis))
    route = [(i - distance, i) for i in devices if i - distance in devices]
    return lax.ppermute(block, axis, route)


def rms_norm(values_in, gain_vector):
    widened = values_in.astype(jnp.float32)
    mean_sq = jnp.mean(widened * widened, axis=-1, keepdims=True)
    return (widened * lax.rsqrt(mean_sq + NORM_EPS) * gain_vector.astype(jnp.float32)).astype(
        jnp.bfloat16
    )


def apply_rotary(product, token_positions):
    half_dim = product.shape[-1] // 2
    frequency = jnp.exp(
        jnp.arange(half_dim, dtype=jnp.float32) * (-2.0 * math.log(ROPE_BASE) / product.shape[-1])
    )
    angles = token_positions.astype(jnp.float32)[:, None] * frequency[None, :]
    cosine = jnp.cos(angles)[:, None, :]
    sine_part = jnp.sin(angles)[:, None, :]
    first_half = product[..., :half_dim]
    second_half = product[..., half_dim:]
    turned = jnp.concatenate(
        [
            first_half * cosine - second_half * sine_part,
            second_half * cosine + first_half * sine_part,
        ],
        axis=-1,
    )
    return turned.astype(jnp.bfloat16)


def turned_by(block, axis, distance):
    devices = lax.axis_size(axis)
    return lax.ppermute(block, axis, [(i, (i + distance) % devices) for i in range(devices)])


def ring_order(devices):
    return list(range(0, devices, 2)) + list(range(devices - 1 - devices % 2, 0, -2))


def along_ring(block, distance):
    devices = lax.axis_size("tok")
    order = ring_order(devices)
    route = [(order[i], order[(i + distance) % devices]) for i in range(devices)]
    return lax.ppermute(block, "tok", route)


def ring_sum(parts, late):
    half = lax.axis_size("tok") // 2
    middle = parts[0].shape[1] // 2
    left = along_ring(parts[half][:, :middle].astype(jnp.bfloat16), -1)
    right = along_ring(parts[half][:, middle:].astype(jnp.bfloat16), 1)
    parts = {**parts, **late()}
    left, right, parts = lax.optimization_barrier((left, right, parts))
    left = parts[half - 1] + jnp.pad(
        left.astype(jnp.float32), ((0, 0), (0, parts[0].shape[1] - middle))
    )
    right = parts[1 - half] + jnp.pad(right.astype(jnp.float32), ((0, 0), (middle, 0)))
    for step in range(half - 2, -1, -1):
        left = along_ring(left.astype(jnp.bfloat16), -1).astype(jnp.float32)
        right = along_ring(right.astype(jnp.bfloat16), 1).astype(jnp.float32)
        if step:
            left = left + parts[step]
            right = right + parts[-step]
    return parts[0] + left + right


def side_by_side(block, axis):
    count = lax.axis_size(axis)
    rank = lax.axis_index(axis)
    blocks = others_over(block, axis)
    columns = []
    for place in range(count):
        column = blocks[0]
        for distance in range(1, count):
            column = jnp.where((rank - place) % count == distance, blocks[distance], column)
        columns.append(column)
    return jnp.concatenate(columns, axis=1)


def others_over(block, axis):
    return [block] + [turned_by(block, axis, d) for d in range(1, lax.axis_size(axis))]


def split_product(activations, blocks, axis):
    count = len(blocks)
    rank = lax.axis_index(axis)
    rows = blocks[0].shape[0]
    total = None
    for distance, block in enumerate(blocks):
        part = lax.dynamic_slice_in_dim(
            activations, ((rank - distance) % count) * rows, rows, 1
        )
        product = jnp.dot(part, block, preferred_element_type=jnp.float32)
        total = product if total is None else total + product
    return total


def width_tile(width, sizes):
    for size in sizes:
        if width % size == 0:
            return size
    return width


def picked_by(payload_ref, first_row, expert, experts, tok_dev, capacity):
    beside = payload_ref.shape[1] // tok_dev
    own = lax.broadcasted_iota(jnp.int32, (experts, tok_dev), 0) == expert

    def piece(i):
        rows = pl.ds(first_row + i // beside * experts, experts)
        columns = pl.ds(i % beside * tok_dev, tok_dev)
        values = payload_ref[rows, columns].astype(jnp.float32)
        return jnp.sum(jnp.where(own, values, 0.0), axis=0, keepdims=True)

    weight = piece(0) + piece(1) + piece(2)
    mask = piece(3)
    upto = lax.broadcasted_iota(jnp.int32, (tok_dev, tok_dev), 0) <= lax.broadcasted_iota(
        jnp.int32, (tok_dev, tok_dev), 1
    )
    upto = jnp.where(upto, 1.0, 0.0).astype(jnp.bfloat16)
    many = jnp.broadcast_to(mask, (16, tok_dev)).astype(jnp.bfloat16)
    place = jnp.dot(many, upto, preferred_element_type=jnp.float32)[0:1]
    place = jnp.where(mask > 0.5, place - 1.0, -1.0).astype(jnp.int32)
    slots = lax.broadcasted_iota(jnp.int32, (capacity, tok_dev), 0)
    pick = jnp.where(slots == place, 1.0, 0.0)
    return pick.astype(jnp.bfloat16), jnp.sum(pick * weight, axis=1, keepdims=True)


def payload_of(keys, values, ids, weights, experts):
    prefix_dev, kv_width = keys.shape
    tok_dev, top_count = ids.shape
    beside = 2 * kv_width // tok_dev
    rows = prefix_dev + 4 // beside * experts

    def body(keys_ref, values_ref, ids_ref, weights_ref, out_ref):
        out_ref[pl.ds(0, prefix_dev), pl.ds(0, kv_width)] = keys_ref[...]
        out_ref[pl.ds(0, prefix_dev), pl.ds(kv_width, kv_width)] = values_ref[...]
        lanes = lax.broadcasted_iota(jnp.int32, (tok_dev, 128), 1)
        dense = jnp.zeros((tok_dev, 128), jnp.float32)
        mask = jnp.zeros((tok_dev, 128), jnp.float32)
        for k in range(top_count):
            named = lanes == ids_ref[:, k : k + 1]
            dense = dense + jnp.where(named, weights_ref[:, k : k + 1], 0.0)
            mask = mask + jnp.where(named, 1.0, 0.0)
        rest = jnp.transpose(dense)[:experts]
        pieces = []
        for _ in range(3):
            pieces.append(rest.astype(jnp.bfloat16))
            rest = rest - pieces[-1].astype(jnp.float32)
        pieces.append(jnp.transpose(mask)[:experts].astype(jnp.bfloat16))
        for i, piece in enumerate(pieces):
            out_ref[
                pl.ds(prefix_dev + i // beside * experts, experts),
                pl.ds(i % beside * tok_dev, tok_dev),
            ] = piece

    return pl.pallas_call(
        body,
        out_shape=jax.ShapeDtypeStruct((rows, 2 * kv_width), jnp.bfloat16),
        name="payload",
    )(keys, values, ids, weights)


def attention(queries, suffix, payloads, prefix_dev, lengths, tok_rank, head_dim):
    tok_dev, query_width = queries.shape
    kv_width = suffix[0].shape[1] // 2
    kv_local = kv_width // head_dim
    group_length = query_width // kv_width
    requests = lengths.shape[0]
    payload_rows = payloads[0].shape[0] // 2
    prefix_rows = 2 * prefix_dev * len(payloads)
    keys_total = prefix_rows + tok_dev * len(suffix)

    def body(lengths_ref, rank_ref, query_ref, *refs):
        suffix_refs, refs = refs[: len(suffix)], refs[len(suffix) :]
        payload_refs, out_ref = refs[:-1], refs[-1]
        token = rank_ref[0] * tok_dev + lax.broadcasted_iota(jnp.int32, (tok_dev, tok_dev), 0)
        start = jnp.int32(0)
        own_start = jnp.zeros((tok_dev, tok_dev), jnp.int32)
        for request in range(requests):
            own_start = jnp.where(token >= start, jnp.maximum(own_start, start), own_start)
            start = start + lengths_ref[request]
        bias = [jnp.zeros((tok_dev, prefix_rows), jnp.float32)]
        for distance in range(len(suffix)):
            key = (rank_ref[0] - distance) * tok_dev + lax.broadcasted_iota(
                jnp.int32, (tok_dev, tok_dev), 1
            )
            bias.append(jnp.where((key >= own_start) & (key <= token), 0.0, MASKED))
        bias = jnp.concatenate(bias, axis=1)
        bias = jnp.concatenate([bias] * group_length, axis=0)
        for c in range(kv_local):
            columns = pl.ds(c * head_dim, head_dim)
            keys = jnp.concatenate(
                [
                    ref[pl.ds(first_row, prefix_dev), columns]
                    for ref in payload_refs
                    for first_row in (0, payload_rows)
                ]
                + [ref[:, columns] for ref in suffix_refs],
                axis=0,
            )
            columns = pl.ds(kv_width + c * head_dim, head_dim)
            values = jnp.concatenate(
                [
                    ref[pl.ds(first_row, prefix_dev), columns]
                    for ref in payload_refs
                    for first_row in (0, payload_rows)
                ]
                + [ref[:, columns] for ref in suffix_refs],
                axis=0,
            )
            first = c * group_length
            query = jnp.concatenate(
                [
                    query_ref[:, pl.ds((first + r) * head_dim, head_dim)]
                    for r in range(group_length)
                ],
                axis=0,
            )
            scores = lax.dot_general(
                query, keys, (((1,), (1,)), ((), ())), preferred_element_type=jnp.float32
            )
            scores = scores * head_dim ** (-0.5) + bias
            probs = jnp.exp(scores - jnp.max(scores, axis=1, keepdims=True))
            total = jnp.sum(probs, axis=1, keepdims=True)
            summed = jnp.dot(
                probs.astype(jnp.bfloat16), values, preferred_element_type=jnp.float32
            )
            attended = (summed / total).astype(jnp.bfloat16)
            for r in range(group_length):
                out_ref[:, pl.ds((first + r) * head_dim, head_dim)] = attended[
                    r * tok_dev : (r + 1) * tok_dev
                ]

    in_vmem = pl.BlockSpec(memory_space=pltpu.VMEM)
    in_smem = pl.BlockSpec(memory_space=pltpu.SMEM)
    return pl.pallas_call(
        body,
        out_shape=jax.ShapeDtypeStruct((tok_dev, query_width), jnp.bfloat16),
        in_specs=[in_smem] * 2 + [in_vmem] * (1 + len(suffix) + len(payloads)),
        out_specs=in_vmem,
        compiler_params=pltpu.CompilerParams(vmem_limit_bytes=VMEM_LIMIT),
        name="attention",
    )(lengths, tok_rank[None], queries, *suffix, *payloads)


def resident(arrays):
    count = len(arrays)

    def body(*refs):
        sources, targets, arrived = refs[:count], refs[count : 2 * count], refs[-1]
        copies = [
            pltpu.make_async_copy(sources[i], targets[i], arrived.at[i]) for i in range(count)
        ]
        for copy in copies:
            copy.start()
        for copy in copies:
            copy.wait()

    return pl.pallas_call(
        body,
        out_shape=[pltpu.VMEM(array.shape, array.dtype) for array in arrays],
        in_specs=[pl.BlockSpec(memory_space=pl.ANY)] * count,
        out_specs=[pl.BlockSpec(memory_space=pltpu.VMEM)] * count,
        scratch_shapes=[pltpu.SemaphoreType.DMA((count,))],
        compiler_params=pltpu.CompilerParams(vmem_limit_bytes=SMALL_LIMIT),
        name="resident",
    )(*arrays)


def slots_of(chosen, sources, payload, first_row, grp_count, tok_dev, experts, capacity):
    count = payload.shape[0]

    def body(chosen_ref, source_ref, payload_ref, pick_ref, weight_ref):
        for i in range(count):
            for g in range(grp_count):
                pick, weight = picked_by(
                    payload_ref.at[source_ref[i]],
                    first_row,
                    chosen_ref[g],
                    experts,
                    tok_dev,
                    capacity,
                )
                pick_ref[i, pl.ds(g * capacity, capacity), :] = pick
                weight_ref[i, pl.ds(g * capacity, capacity), :] = jnp.broadcast_to(
                    weight, (capacity, 128)
                )

    in_vmem = pl.BlockSpec(memory_space=pltpu.VMEM)
    slots = grp_count * capacity
    return pl.pallas_call(
        body,
        out_shape=[
            jax.ShapeDtypeStruct((count, slots, tok_dev), jnp.bfloat16),
            jax.ShapeDtypeStruct((count, slots, 128), jnp.float32),
        ],
        in_specs=[pl.BlockSpec(memory_space=pltpu.SMEM)] * 2 + [in_vmem],
        out_specs=[in_vmem] * 2,
        compiler_params=pltpu.CompilerParams(vmem_limit_bytes=SMALL_LIMIT),
        name="slots",
    )(chosen, sources, payload)


def hidden_units(picks, places, blocks, gates, ups, capacity):
    count, grp_count = len(blocks), len(gates)
    model_width, hidden_width = gates[0].shape
    tile = width_tile(hidden_width, (256, 384, 128))
    pieces = [len(block) for block in blocks]
    columns = sum(pieces)

    def body(pick_ref, *refs):
        token_refs, refs = refs[:columns], refs[columns:]
        gate_refs, refs = refs[:grp_count], refs[grp_count:]
        up_refs, refs = refs[:grp_count], refs[grp_count:]
        out_ref, rows_ref = refs
        at = 0
        for i in range(count):
            pick = pick_ref[places[i]]
            first = 0
            for token_ref in token_refs[at : at + pieces[i]]:
                width = token_ref.shape[1]
                picked = jnp.dot(
                    pick, token_ref[...], preferred_element_type=jnp.float32
                ).astype(jnp.bfloat16)
                for g in range(grp_count):
                    rows_ref[g, pl.ds(i * capacity, capacity), pl.ds(first, width)] = picked[
                        g * capacity : (g + 1) * capacity
                    ]
                first += width
            at += pieces[i]
        for g in range(grp_count):
            for n in range(0, hidden_width, tile):
                own = pl.ds(n, tile)
                gate = jnp.dot(
                    rows_ref[g], gate_refs[g][:, own], preferred_element_type=jnp.float32
                )
                up = jnp.dot(rows_ref[g], up_refs[g][:, own], preferred_element_type=jnp.float32)
                out_ref[g, :, own] = (gate / (1.0 + jnp.exp(-gate)) * up).astype(jnp.bfloat16)

    in_vmem = pl.BlockSpec(memory_space=pltpu.VMEM)
    flat = [part for block in blocks for part in block]
    return pl.pallas_call(
        body,
        out_shape=jax.ShapeDtypeStruct((grp_count, count * capacity, hidden_width), jnp.bfloat16),
        in_specs=[in_vmem] * (1 + columns + 2 * grp_count),
        out_specs=in_vmem,
        scratch_shapes=[pltpu.VMEM((grp_count, count * capacity, model_width), jnp.bfloat16)],
        compiler_params=pltpu.CompilerParams(vmem_limit_bytes=SMALL_LIMIT),
        name="hidden_units",
    )(picks, *flat, *gates, *ups)


def token_sums(rank, picks, weights, places, hiddens, downs, tok_dev, capacity):
    count, grp_count, head_count = len(places), len(downs), len(hiddens)
    rows_each = hiddens[0].shape[2]
    share_width = downs[0].shape[1]
    tile = width_tile(share_width, (256, 640))

    def body(rank_ref, pick_ref, weight_ref, *refs):
        hidden_refs, refs = refs[:head_count], refs[head_count:]
        down_refs, out_refs = refs[:grp_count], refs[grp_count:]
        firsts = [
            pl.multiple_of((rank_ref[0] - k + head_count) % head_count * rows_each, rows_each)
            for k in range(head_count)
        ]
        for n in range(0, share_width, tile):
            own = pl.ds(n, tile)
            results = []
            for g in range(grp_count):
                result = None
                for k in range(head_count):
                    part = jnp.dot(
                        hidden_refs[k][g],
                        down_refs[g][pl.ds(firsts[k], rows_each), own],
                        preferred_element_type=jnp.float32,
                    )
                    result = part if result is None else result + part
                results.append(result)
            for i in range(count):
                scaled = jnp.concatenate(
                    [result[i * capacity : (i + 1) * capacity] for result in results], axis=0
                )
                scaled = (scaled * weight_ref[places[i], :, 0:1]).astype(jnp.bfloat16)
                out_refs[i][:, own] = lax.dot_general(
                    pick_ref[places[i]],
                    scaled,
                    (((0,), (0,)), ((), ())),
                    preferred_element_type=jnp.float32,
                )

    in_vmem = pl.BlockSpec(memory_space=pltpu.VMEM)
    return pl.pallas_call(
        body,
        out_shape=[jax.ShapeDtypeStruct((tok_dev, share_width), jnp.float32)] * count,
        in_specs=[pl.BlockSpec(memory_space=pltpu.SMEM)]
        + [in_vmem] * (2 + head_count + grp_count),
        out_specs=[in_vmem] * count,
        compiler_params=pltpu.CompilerParams(vmem_limit_bytes=SMALL_LIMIT),
        name="token_sums",
    )(rank, picks, weights, *hiddens, *downs)


def on_device(
    hidden_in,
    attn_gain,
    w_query,
    key_projection_weight,
    value_projection_weight,
    w_out,
    prefix_keys,
    cached_prefix_values,
    request_lengths,
    moe_gain,
    expert_ids,
    route_weights,
    w_gate,
    w_up,
    w_down,
):
    tok_count = lax.axis_size("tok")
    grp_count = lax.axis_size("grp")
    head_count = lax.axis_size("head")
    tok_rank = lax.axis_index("tok")
    grp_rank = lax.axis_index("grp")
    head_rank = lax.axis_index("head")
    tok_dev = hidden_in.shape[1]
    model_width = attn_gain.shape[0]
    head_dim = prefix_keys.shape[3]
    kv_local = prefix_keys.shape[2]
    kv_width = kv_local * head_dim
    group_length = w_query.shape[1] // kv_width
    prefix_total = prefix_keys.shape[1] * tok_count
    share_width = model_width // head_count
    experts = grp_count * tok_count
    top_count = expert_ids.shape[2]
    capacity = 4 * tok_dev * top_count // (3 * experts)

    quarter = hidden_in[0]
    features = side_by_side(quarter, "head")
    query_blocks = others_over(w_query, "grp")
    key_blocks = others_over(key_projection_weight, "grp")
    value_blocks = others_over(value_projection_weight, "grp")
    full_out = lax.all_gather(w_out, "grp", axis=0, tiled=True)

    payload = payload_of(
        prefix_keys[0].reshape(-1, kv_width),
        cached_prefix_values[0].reshape(-1, kv_width),
        expert_ids[0],
        route_weights[0],
        experts,
    )
    half_ring = tok_count // 2
    beside = lax.ppermute(payload, "tok", [(i, i ^ 1) for i in range(tok_count)])
    pair = jnp.where(
        tok_rank % 2 == 0,
        jnp.concatenate([payload, beside], axis=0),
        jnp.concatenate([beside, payload], axis=0),
    )
    payloads = [pair] + [turned_by(pair, "tok", 2 * d) for d in range(1, half_ring)]
    prefix_dev = prefix_keys.shape[1]


    attention_input = rms_norm(features, attn_gain)
    lengths = request_lengths[0]
    request_ends = jnp.cumsum(lengths)
    starts = request_ends - lengths
    token_index = tok_rank * tok_dev + jnp.arange(tok_dev, dtype=jnp.int32)
    own_start = jnp.max(
        jnp.where(starts[None, :] <= token_index[:, None], starts[None, :], 0), axis=1
    )
    token_positions = prefix_total + token_index - own_start
    key_product = split_product(attention_input, key_blocks, "grp")
    value_product = split_product(attention_input, value_blocks, "grp")
    query_product = split_product(attention_input, query_blocks, "grp")
    queries = apply_rotary(
        query_product.reshape(tok_dev, kv_local * group_length, head_dim), token_positions
    )
    queries = queries.reshape(tok_dev, kv_local * group_length * head_dim)
    request_suffix_keys = apply_rotary(
        key_product.reshape(tok_dev, kv_local, head_dim), token_positions
    )
    suffix = jnp.concatenate(
        [request_suffix_keys.reshape(tok_dev, kv_width), value_product.astype(jnp.bfloat16)], axis=1
    )
    longest = tok_dev * tok_count // 4
    reach_devices = (longest - 1 + tok_dev - 1) // tok_dev
    reached = [suffix] + [shifted(suffix, "tok", d) for d in range(1, reach_devices + 1)]
    (payloads, reached), expert_weights = lax.optimization_barrier(
        ((payloads, reached), (w_gate, w_up, w_down))
    )
    gate_blocks, up_blocks, down_blocks = [
        others_over(weight[0], "grp") for weight in expert_weights
    ]
    attended = attention(
        queries,
        reached,
        payloads,
        prefix_dev,
        lengths,
        tok_rank,
        head_dim,
    )
    halves = []
    for half in range(2):
        columns = slice(half * model_width // 2, (half + 1) * model_width // 2)
        own = lax.dot_general(
            attended, full_out[columns], (((1,), (1,)), ((), ())), preferred_element_type=jnp.float32
        )
        mixed = own + features[:, columns].astype(jnp.float32)
        for arrived in others_over(own.astype(jnp.bfloat16), "head")[1:]:
            mixed = mixed + arrived.astype(jnp.float32)
        halves.append(mixed.astype(jnp.bfloat16))
    mid_full = jnp.concatenate(halves, axis=1)
    mid_quarter = lax.dynamic_slice_in_dim(mid_full, head_rank * share_width, share_width, 1)
    moe_in = rms_norm(mid_full, moe_gain)
    chosen = jnp.stack(
        [((grp_rank - d) % grp_count) * tok_count + tok_rank for d in range(grp_count)]
    ).astype(jnp.int32)
    distances = [0] + [d for step in range(1, half_ring) for d in (step, -step)] + [half_ring]
    place_of = {d: i for i, d in enumerate(distances)}
    order = ring_order(tok_count)
    sources = []
    for device in range(tok_count):
        blocks = [order[(order.index(device) - d) % tok_count] for d in distances]
        sources.append([(device // 2 - b // 2) % half_ring * 2 + b % 2 for b in blocks])
    sources = lax.dynamic_index_in_dim(
        jnp.array(sources, jnp.int32), tok_rank, axis=0, keepdims=False
    )
    together = jnp.concatenate(payloads, axis=0).reshape((tok_count,) + payload.shape)
    picks, slot_weights = slots_of(
        chosen, sources, together, prefix_dev, grp_count, tok_dev, experts, capacity
    )

    def units_of(chunk, blocks):
        places = [place_of[d] for d in chunk]
        return hidden_units(picks, places, blocks, gate_blocks, up_blocks, capacity)

    def sums_of(chunk, exchanged):
        places = [place_of[d] for d in chunk]
        sums = token_sums(
            head_rank[None], picks, slot_weights, places, exchanged, down_blocks, tok_dev, capacity
        )
        return dict(zip(chunk, sums))

    (gate_blocks, up_blocks), _ = lax.optimization_barrier(((gate_blocks, up_blocks), moe_in))
    held = resident(gate_blocks + up_blocks)
    gate_blocks, up_blocks = held[:grp_count], held[grp_count:]

    middle = model_width // 2
    ahead, behind = moe_in, moe_in
    chunk, blocks = [0], [[moe_in]]
    parts, waiting = {}, []
    for step in range(1, half_ring + 1):
        last = step == half_ring
        sent = (ahead[:, :middle], behind[:, middle:]) if last else (ahead, behind)
        arriving = (along_ring(sent[0], 1), along_ring(sent[1], -1))
        hidden = units_of(chunk, blocks)
        if waiting and not last:
            parts.update(sums_of(*waiting.pop(0)))
        (ahead, behind), hidden, parts = lax.optimization_barrier((arriving, hidden, parts))
        if step == 1:
            down_blocks, _ = lax.optimization_barrier((down_blocks, ahead))
            down_blocks = resident(down_blocks)
        waiting.append((chunk, others_over(hidden, "head")))
        chunk = [half_ring] if last else [step, -step]
        blocks = [[ahead, behind]] if last else [[ahead], [behind]]
    exchanged = others_over(units_of(chunk, blocks), "head")
    parts.update(sums_of(*waiting.pop(0)))
    exchanged, parts = lax.optimization_barrier((exchanged, parts))
    parts.update(sums_of(chunk, exchanged))

    def late():
        own, arrived = waiting.pop(0)
        arrived, _ = lax.optimization_barrier((arrived, parts[half_ring]))
        return sums_of(own, arrived)

    weighted = ring_sum(parts, late)
    output = (mid_quarter.astype(jnp.float32) + weighted).astype(jnp.bfloat16)
    return output[None]


def solution(mesh):
    return jax.shard_map(
        on_device,
        mesh=mesh,
        in_specs=(
            P("grp", "tok", "head"),
            P(),
            P("grp", "head"),
            P("grp", "head"),
            P("grp", "head"),
            P("grp", "head"),
            P("grp", "tok", "head", None),
            P("grp", "tok", "head", None),
            P("grp", None),
            P(),
            P("grp", "tok", None),
            P("grp", "tok", None),
            P(("grp", "tok"), None, "head"),
            P(("grp", "tok"), None, "head"),
            P(("grp", "tok"), None, "head"),
        ),
        out_specs=P("grp", "tok", "head"),
        check_vma=False,
    )
```

```python
import math

import jax
import jax.numpy as jnp
from jax import lax
from jax.experimental import pallas as pl
from jax.experimental.pallas import tpu as pltpu
from jax.sharding import PartitionSpec as P

ROPE_BASE = 500000.0
NORM_EPS = 1e-06
MASKED = -1e30
VMEM_LIMIT = 40 * 1024 * 1024
SMALL_LIMIT = 16 * 1024 * 1024


def shifted(block, axis, distance):
    devices = range(lax.axis_size(axis))
    route = [(i - distance, i) for i in devices if i - distance in devices]
    return lax.ppermute(block, axis, route)


def rms_norm(values_in, gain_vector):
    widened = values_in.astype(jnp.float32)
    mean_sq = jnp.mean(widened * widened, axis=-1, keepdims=True)
    return (widened * lax.rsqrt(mean_sq + NORM_EPS) * gain_vector.astype(jnp.float32)).astype(
        jnp.bfloat16
    )


def apply_rotary(product, token_positions):
    half_dim = product.shape[-1] // 2
    frequency = jnp.exp(
        jnp.arange(half_dim, dtype=jnp.float32) * (-2.0 * math.log(ROPE_BASE) / product.shape[-1])
    )
    angles = token_positions.astype(jnp.float32)[:, None] * frequency[None, :]
    cosine = jnp.cos(angles)[:, None, :]
    sine_part = jnp.sin(angles)[:, None, :]
    first_half = product[..., :half_dim]
    second_half = product[..., half_dim:]
    turned = jnp.concatenate(
        [
            first_half * cosine - second_half * sine_part,
            second_half * cosine + first_half * sine_part,
        ],
        axis=-1,
    )
    return turned.astype(jnp.bfloat16)


def turned_by(block, axis, distance):
    devices = lax.axis_size(axis)
    return lax.ppermute(block, axis, [(i, (i + distance) % devices) for i in range(devices)])


def ring_order(devices):
    return list(range(0, devices, 2)) + list(range(devices - 1 - devices % 2, 0, -2))


def along_ring(block, distance):
    devices = lax.axis_size("tok")
    order = ring_order(devices)
    route = [(order[i], order[(i + distance) % devices]) for i in range(devices)]
    return lax.ppermute(block, "tok", route)


def ring_sum(parts, late):
    half = lax.axis_size("tok") // 2
    middle = parts[0].shape[1] // 2
    left = along_ring(parts[half][:, :middle].astype(jnp.bfloat16), -1)
    right = along_ring(parts[half][:, middle:].astype(jnp.bfloat16), 1)
    parts = {**parts, **late()}
    left, right, parts = lax.optimization_barrier((left, right, parts))
    left = parts[half - 1] + jnp.pad(
        left.astype(jnp.float32), ((0, 0), (0, parts[0].shape[1] - middle))
    )
    right = parts[1 - half] + jnp.pad(right.astype(jnp.float32), ((0, 0), (middle, 0)))
    for step in range(half - 2, -1, -1):
        left = along_ring(left.astype(jnp.bfloat16), -1).astype(jnp.float32)
        right = along_ring(right.astype(jnp.bfloat16), 1).astype(jnp.float32)
        if step:
            left = left + parts[step]
            right = right + parts[-step]
    return parts[0] + left + right


def side_by_side(block, axis):
    count = lax.axis_size(axis)
    rank = lax.axis_index(axis)
    blocks = others_over(block, axis)
    columns = []
    for place in range(count):
        column = blocks[0]
        for distance in range(1, count):
            column = jnp.where((rank - place) % count == distance, blocks[distance], column)
        columns.append(column)
    return jnp.concatenate(columns, axis=1)


def others_over(block, axis):
    return [block] + [turned_by(block, axis, d) for d in range(1, lax.axis_size(axis))]


def split_product(activations, blocks, axis):
    count = len(blocks)
    rank = lax.axis_index(axis)
    rows = blocks[0].shape[0]
    total = None
    for distance, block in enumerate(blocks):
        part = lax.dynamic_slice_in_dim(
            activations, ((rank - distance) % count) * rows, rows, 1
        )
        product = jnp.dot(part, block, preferred_element_type=jnp.float32)
        total = product if total is None else total + product
    return total


def width_tile(width, sizes):
    for size in sizes:
        if width % size == 0:
            return size
    return width


def picked_by(payload_ref, first_row, expert, experts, tok_dev, capacity):
    beside = payload_ref.shape[1] // tok_dev
    own = lax.broadcasted_iota(jnp.int32, (experts, tok_dev), 0) == expert

    def piece(i):
        rows = pl.ds(first_row + i // beside * experts, experts)
        columns = pl.ds(i % beside * tok_dev, tok_dev)
        values = payload_ref[rows, columns].astype(jnp.float32)
        return jnp.sum(jnp.where(own, values, 0.0), axis=0, keepdims=True)

    weight = piece(0) + piece(1) + piece(2)
    mask = piece(3)
    upto = lax.broadcasted_iota(jnp.int32, (tok_dev, tok_dev), 0) <= lax.broadcasted_iota(
        jnp.int32, (tok_dev, tok_dev), 1
    )
    upto = jnp.where(upto, 1.0, 0.0).astype(jnp.bfloat16)
    many = jnp.broadcast_to(mask, (16, tok_dev)).astype(jnp.bfloat16)
    place = jnp.dot(many, upto, preferred_element_type=jnp.float32)[0:1]
    place = jnp.where(mask > 0.5, place - 1.0, -1.0).astype(jnp.int32)
    slots = lax.broadcasted_iota(jnp.int32, (capacity, tok_dev), 0)
    pick = jnp.where(slots == place, 1.0, 0.0)
    return pick.astype(jnp.bfloat16), jnp.sum(pick * weight, axis=1, keepdims=True)


def payload_of(keys, values, ids, weights, experts):
    prefix_dev, kv_width = keys.shape
    tok_dev, top_count = ids.shape
    beside = 2 * kv_width // tok_dev
    rows = prefix_dev + 4 // beside * experts

    def body(keys_ref, values_ref, ids_ref, weights_ref, out_ref):
        out_ref[pl.ds(0, prefix_dev), pl.ds(0, kv_width)] = keys_ref[...]
        out_ref[pl.ds(0, prefix_dev), pl.ds(kv_width, kv_width)] = values_ref[...]
        lanes = lax.broadcasted_iota(jnp.int32, (tok_dev, 128), 1)
        dense = jnp.zeros((tok_dev, 128), jnp.float32)
        mask = jnp.zeros((tok_dev, 128), jnp.float32)
        for k in range(top_count):
            named = lanes == ids_ref[:, k : k + 1]
            dense = dense + jnp.where(named, weights_ref[:, k : k + 1], 0.0)
            mask = mask + jnp.where(named, 1.0, 0.0)
        rest = jnp.transpose(dense)[:experts]
        pieces = []
        for _ in range(3):
            pieces.append(rest.astype(jnp.bfloat16))
            rest = rest - pieces[-1].astype(jnp.float32)
        pieces.append(jnp.transpose(mask)[:experts].astype(jnp.bfloat16))
        for i, piece in enumerate(pieces):
            out_ref[
                pl.ds(prefix_dev + i // beside * experts, experts),
                pl.ds(i % beside * tok_dev, tok_dev),
            ] = piece

    return pl.pallas_call(
        body,
        out_shape=jax.ShapeDtypeStruct((rows, 2 * kv_width), jnp.bfloat16),
        name="payload",
    )(keys, values, ids, weights)


def attention(queries, suffix, payloads, prefix_dev, lengths, tok_rank, head_dim):
    tok_dev, query_width = queries.shape
    kv_width = suffix[0].shape[1] // 2
    kv_local = kv_width // head_dim
    group_length = query_width // kv_width
    requests = lengths.shape[0]
    payload_rows = payloads[0].shape[0] // 2
    prefix_rows = 2 * prefix_dev * len(payloads)
    keys_total = prefix_rows + tok_dev * len(suffix)

    def body(lengths_ref, rank_ref, query_ref, *refs):
        suffix_refs, refs = refs[: len(suffix)], refs[len(suffix) :]
        payload_refs, out_ref = refs[:-1], refs[-1]
        token = rank_ref[0] * tok_dev + lax.broadcasted_iota(jnp.int32, (tok_dev, tok_dev), 0)
        start = jnp.int32(0)
        own_start = jnp.zeros((tok_dev, tok_dev), jnp.int32)
        for request in range(requests):
            own_start = jnp.where(token >= start, jnp.maximum(own_start, start), own_start)
            start = start + lengths_ref[request]
        bias = [jnp.zeros((tok_dev, prefix_rows), jnp.float32)]
        for distance in range(len(suffix)):
            key = (rank_ref[0] - distance) * tok_dev + lax.broadcasted_iota(
                jnp.int32, (tok_dev, tok_dev), 1
            )
            bias.append(jnp.where((key >= own_start) & (key <= token), 0.0, MASKED))
        bias = jnp.concatenate(bias, axis=1)
        bias = jnp.concatenate([bias] * group_length, axis=0)
        for c in range(kv_local):
            columns = pl.ds(c * head_dim, head_dim)
            keys = jnp.concatenate(
                [
                    ref[pl.ds(first_row, prefix_dev), columns]
                    for ref in payload_refs
                    for first_row in (0, payload_rows)
                ]
                + [ref[:, columns] for ref in suffix_refs],
                axis=0,
            )
            columns = pl.ds(kv_width + c * head_dim, head_dim)
            values = jnp.concatenate(
                [
                    ref[pl.ds(first_row, prefix_dev), columns]
                    for ref in payload_refs
                    for first_row in (0, payload_rows)
                ]
                + [ref[:, columns] for ref in suffix_refs],
                axis=0,
            )
            first = c * group_length
            query = jnp.concatenate(
                [
                    query_ref[:, pl.ds((first + r) * head_dim, head_dim)]
                    for r in range(group_length)
                ],
                axis=0,
            )
            scores = lax.dot_general(
                query, keys, (((1,), (1,)), ((), ())), preferred_element_type=jnp.float32
            )
            scores = scores * head_dim ** (-0.5) + bias
            probs = jnp.exp(scores - jnp.max(scores, axis=1, keepdims=True))
            total = jnp.sum(probs, axis=1, keepdims=True)
            summed = jnp.dot(
                probs.astype(jnp.bfloat16), values, preferred_element_type=jnp.float32
            )
            attended = (summed / total).astype(jnp.bfloat16)
            for r in range(group_length):
                out_ref[:, pl.ds((first + r) * head_dim, head_dim)] = attended[
                    r * tok_dev : (r + 1) * tok_dev
                ]

    in_vmem = pl.BlockSpec(memory_space=pltpu.VMEM)
    in_smem = pl.BlockSpec(memory_space=pltpu.SMEM)
    return pl.pallas_call(
        body,
        out_shape=jax.ShapeDtypeStruct((tok_dev, query_width), jnp.bfloat16),
        in_specs=[in_smem] * 2 + [in_vmem] * (1 + len(suffix) + len(payloads)),
        out_specs=in_vmem,
        compiler_params=pltpu.CompilerParams(vmem_limit_bytes=VMEM_LIMIT),
        name="attention",
    )(lengths, tok_rank[None], queries, *suffix, *payloads)


def resident(arrays):
    count = len(arrays)

    def body(*refs):
        sources, targets, arrived = refs[:count], refs[count : 2 * count], refs[-1]
        copies = [
            pltpu.make_async_copy(sources[i], targets[i], arrived.at[i]) for i in range(count)
        ]
        for copy in copies:
            copy.start()
        for copy in copies:
            copy.wait()

    return pl.pallas_call(
        body,
        out_shape=[pltpu.VMEM(array.shape, array.dtype) for array in arrays],
        in_specs=[pl.BlockSpec(memory_space=pl.ANY)] * count,
        out_specs=[pl.BlockSpec(memory_space=pltpu.VMEM)] * count,
        scratch_shapes=[pltpu.SemaphoreType.DMA((count,))],
        compiler_params=pltpu.CompilerParams(vmem_limit_bytes=SMALL_LIMIT),
        name="resident",
    )(*arrays)


def slots_of(chosen, sources, payload, first_row, grp_count, tok_dev, experts, capacity):
    count = payload.shape[0]

    def body(chosen_ref, source_ref, payload_ref, pick_ref, weight_ref):
        for i in range(count):
            for g in range(grp_count):
                pick, weight = picked_by(
                    payload_ref.at[source_ref[i]],
                    first_row,
                    chosen_ref[g],
                    experts,
                    tok_dev,
                    capacity,
                )
                pick_ref[i, pl.ds(g * capacity, capacity), :] = pick
                weight_ref[i, pl.ds(g * capacity, capacity), :] = jnp.broadcast_to(
                    weight, (capacity, 128)
                )

    in_vmem = pl.BlockSpec(memory_space=pltpu.VMEM)
    slots = grp_count * capacity
    return pl.pallas_call(
        body,
        out_shape=[
            jax.ShapeDtypeStruct((count, slots, tok_dev), jnp.bfloat16),
            jax.ShapeDtypeStruct((count, slots, 128), jnp.float32),
        ],
        in_specs=[pl.BlockSpec(memory_space=pltpu.SMEM)] * 2 + [in_vmem],
        out_specs=[in_vmem] * 2,
        compiler_params=pltpu.CompilerParams(vmem_limit_bytes=SMALL_LIMIT),
        name="slots",
    )(chosen, sources, payload)


def hidden_units(picks, places, blocks, gates, ups, capacity):
    count, grp_count = len(blocks), len(gates)
    model_width, hidden_width = gates[0].shape
    tile = width_tile(hidden_width, (256, 384, 128))
    pieces = [len(block) for block in blocks]
    columns = sum(pieces)

    def body(pick_ref, *refs):
        token_refs, refs = refs[:columns], refs[columns:]
        gate_refs, refs = refs[:grp_count], refs[grp_count:]
        up_refs, refs = refs[:grp_count], refs[grp_count:]
        out_ref, rows_ref = refs
        at = 0
        for i in range(count):
            pick = pick_ref[places[i]]
            first = 0
            for token_ref in token_refs[at : at + pieces[i]]:
                width = token_ref.shape[1]
                picked = jnp.dot(
                    pick, token_ref[...], preferred_element_type=jnp.float32
                ).astype(jnp.bfloat16)
                for g in range(grp_count):
                    rows_ref[g, pl.ds(i * capacity, capacity), pl.ds(first, width)] = picked[
                        g * capacity : (g + 1) * capacity
                    ]
                first += width
            at += pieces[i]
        for g in range(grp_count):
            for n in range(0, hidden_width, tile):
                own = pl.ds(n, tile)
                gate = jnp.dot(
                    rows_ref[g], gate_refs[g][:, own], preferred_element_type=jnp.float32
                )
                up = jnp.dot(rows_ref[g], up_refs[g][:, own], preferred_element_type=jnp.float32)
                out_ref[g, :, own] = (gate / (1.0 + jnp.exp(-gate)) * up).astype(jnp.bfloat16)

    in_vmem = pl.BlockSpec(memory_space=pltpu.VMEM)
    flat = [part for block in blocks for part in block]
    return pl.pallas_call(
        body,
        out_shape=jax.ShapeDtypeStruct((grp_count, count * capacity, hidden_width), jnp.bfloat16),
        in_specs=[in_vmem] * (1 + columns + 2 * grp_count),
        out_specs=in_vmem,
        scratch_shapes=[pltpu.VMEM((grp_count, count * capacity, model_width), jnp.bfloat16)],
        compiler_params=pltpu.CompilerParams(vmem_limit_bytes=SMALL_LIMIT),
        name="hidden_units",
    )(picks, *flat, *gates, *ups)


def token_sums(rank, picks, weights, places, hiddens, downs, tok_dev, capacity):
    count, grp_count, head_count = len(places), len(downs), len(hiddens)
    rows_each = hiddens[0].shape[2]
    share_width = downs[0].shape[1]
    tile = width_tile(share_width, (640,))

    def body(rank_ref, pick_ref, weight_ref, *refs):
        hidden_refs, refs = refs[:head_count], refs[head_count:]
        down_refs, out_refs = refs[:grp_count], refs[grp_count:]
        firsts = [
            pl.multiple_of((rank_ref[0] - k + head_count) % head_count * rows_each, rows_each)
            for k in range(head_count)
        ]
        for n in range(0, share_width, tile):
            own = pl.ds(n, tile)
            results = []
            for g in range(grp_count):
                result = None
                for k in range(head_count):
                    part = jnp.dot(
                        hidden_refs[k][g],
                        down_refs[g][pl.ds(firsts[k], rows_each), own],
                        preferred_element_type=jnp.float32,
                    )
                    result = part if result is None else result + part
                results.append(result)
            for i in range(count):
                scaled = jnp.concatenate(
                    [result[i * capacity : (i + 1) * capacity] for result in results], axis=0
                )
                scaled = (scaled * weight_ref[places[i], :, 0:1]).astype(jnp.bfloat16)
                out_refs[i][:, own] = lax.dot_general(
                    pick_ref[places[i]],
                    scaled,
                    (((0,), (0,)), ((), ())),
                    preferred_element_type=jnp.float32,
                )

    in_vmem = pl.BlockSpec(memory_space=pltpu.VMEM)
    return pl.pallas_call(
        body,
        out_shape=[jax.ShapeDtypeStruct((tok_dev, share_width), jnp.float32)] * count,
        in_specs=[pl.BlockSpec(memory_space=pltpu.SMEM)]
        + [in_vmem] * (2 + head_count + grp_count),
        out_specs=[in_vmem] * count,
        compiler_params=pltpu.CompilerParams(vmem_limit_bytes=SMALL_LIMIT),
        name="token_sums",
    )(rank, picks, weights, *hiddens, *downs)


def on_device(
    hidden_in,
    attn_gain,
    w_query,
    key_projection_weight,
    value_projection_weight,
    w_out,
    prefix_keys,
    cached_prefix_values,
    request_lengths,
    moe_gain,
    expert_ids,
    route_weights,
    w_gate,
    w_up,
    w_down,
):
    tok_count = lax.axis_size("tok")
    grp_count = lax.axis_size("grp")
    head_count = lax.axis_size("head")
    tok_rank = lax.axis_index("tok")
    grp_rank = lax.axis_index("grp")
    head_rank = lax.axis_index("head")
    tok_dev = hidden_in.shape[1]
    model_width = attn_gain.shape[0]
    head_dim = prefix_keys.shape[3]
    kv_local = prefix_keys.shape[2]
    kv_width = kv_local * head_dim
    group_length = w_query.shape[1] // kv_width
    prefix_total = prefix_keys.shape[1] * tok_count
    share_width = model_width // head_count
    experts = grp_count * tok_count
    top_count = expert_ids.shape[2]
    capacity = 4 * tok_dev * top_count // (3 * experts)

    quarter = hidden_in[0]
    features = side_by_side(quarter, "head")
    query_blocks = others_over(w_query, "grp")
    key_blocks = others_over(key_projection_weight, "grp")
    value_blocks = others_over(value_projection_weight, "grp")
    full_out = lax.all_gather(w_out, "grp", axis=0, tiled=True)

    payload = payload_of(
        prefix_keys[0].reshape(-1, kv_width),
        cached_prefix_values[0].reshape(-1, kv_width),
        expert_ids[0],
        route_weights[0],
        experts,
    )
    half_ring = tok_count // 2
    beside = lax.ppermute(payload, "tok", [(i, i ^ 1) for i in range(tok_count)])
    pair = jnp.where(
        tok_rank % 2 == 0,
        jnp.concatenate([payload, beside], axis=0),
        jnp.concatenate([beside, payload], axis=0),
    )
    payloads = [pair] + [turned_by(pair, "tok", 2 * d) for d in range(1, half_ring)]
    prefix_dev = prefix_keys.shape[1]


    attention_input = rms_norm(features, attn_gain)
    lengths = request_lengths[0]
    request_ends = jnp.cumsum(lengths)
    starts = request_ends - lengths
    token_index = tok_rank * tok_dev + jnp.arange(tok_dev, dtype=jnp.int32)
    own_start = jnp.max(
        jnp.where(starts[None, :] <= token_index[:, None], starts[None, :], 0), axis=1
    )
    token_positions = prefix_total + token_index - own_start
    key_product = split_product(attention_input, key_blocks, "grp")
    value_product = split_product(attention_input, value_blocks, "grp")
    query_product = split_product(attention_input, query_blocks, "grp")
    queries = apply_rotary(
        query_product.reshape(tok_dev, kv_local * group_length, head_dim), token_positions
    )
    queries = queries.reshape(tok_dev, kv_local * group_length * head_dim)
    request_suffix_keys = apply_rotary(
        key_product.reshape(tok_dev, kv_local, head_dim), token_positions
    )
    suffix = jnp.concatenate(
        [request_suffix_keys.reshape(tok_dev, kv_width), value_product.astype(jnp.bfloat16)], axis=1
    )
    longest = tok_dev * tok_count // 4
    reach_devices = (longest - 1 + tok_dev - 1) // tok_dev
    reached = [suffix] + [shifted(suffix, "tok", d) for d in range(1, reach_devices + 1)]
    (payloads, reached), expert_weights = lax.optimization_barrier(
        ((payloads, reached), (w_gate, w_up, w_down))
    )
    gate_blocks, up_blocks, down_blocks = [
        others_over(weight[0], "grp") for weight in expert_weights
    ]
    attended = attention(
        queries,
        reached,
        payloads,
        prefix_dev,
        lengths,
        tok_rank,
        head_dim,
    )
    halves = []
    for half in range(2):
        columns = slice(half * model_width // 2, (half + 1) * model_width // 2)
        own = lax.dot_general(
            attended, full_out[columns], (((1,), (1,)), ((), ())), preferred_element_type=jnp.float32
        )
        mixed = own + features[:, columns].astype(jnp.float32)
        for arrived in others_over(own.astype(jnp.bfloat16), "head")[1:]:
            mixed = mixed + arrived.astype(jnp.float32)
        halves.append(mixed.astype(jnp.bfloat16))
    mid_full = jnp.concatenate(halves, axis=1)
    mid_quarter = lax.dynamic_slice_in_dim(mid_full, head_rank * share_width, share_width, 1)
    moe_in = rms_norm(mid_full, moe_gain)
    chosen = jnp.stack(
        [((grp_rank - d) % grp_count) * tok_count + tok_rank for d in range(grp_count)]
    ).astype(jnp.int32)
    distances = [0] + [d for step in range(1, half_ring) for d in (step, -step)] + [half_ring]
    place_of = {d: i for i, d in enumerate(distances)}
    order = ring_order(tok_count)
    sources = []
    for device in range(tok_count):
        blocks = [order[(order.index(device) - d) % tok_count] for d in distances]
        sources.append([(device // 2 - b // 2) % half_ring * 2 + b % 2 for b in blocks])
    sources = lax.dynamic_index_in_dim(
        jnp.array(sources, jnp.int32), tok_rank, axis=0, keepdims=False
    )
    together = jnp.concatenate(payloads, axis=0).reshape((tok_count,) + payload.shape)
    picks, slot_weights = slots_of(
        chosen, sources, together, prefix_dev, grp_count, tok_dev, experts, capacity
    )

    def units_of(chunk, blocks):
        places = [place_of[d] for d in chunk]
        return hidden_units(picks, places, blocks, gate_blocks, up_blocks, capacity)

    def sums_of(chunk, exchanged):
        places = [place_of[d] for d in chunk]
        sums = token_sums(
            head_rank[None], picks, slot_weights, places, exchanged, down_blocks, tok_dev, capacity
        )
        return dict(zip(chunk, sums))

    (gate_blocks, up_blocks), _ = lax.optimization_barrier(((gate_blocks, up_blocks), moe_in))
    held = resident(gate_blocks + up_blocks)
    gate_blocks, up_blocks = held[:grp_count], held[grp_count:]

    middle = model_width // 2
    ahead, behind = moe_in, moe_in
    chunk, blocks = [0], [[moe_in]]
    parts, waiting = {}, []
    for step in range(1, half_ring + 1):
        last = step == half_ring
        sent = (ahead[:, :middle], behind[:, middle:]) if last else (ahead, behind)
        arriving = (along_ring(sent[0], 1), along_ring(sent[1], -1))
        hidden = units_of(chunk, blocks)
        if waiting and not last:
            parts.update(sums_of(*waiting.pop(0)))
        (ahead, behind), hidden, parts = lax.optimization_barrier((arriving, hidden, parts))
        if step == 1:
            down_blocks, _ = lax.optimization_barrier((down_blocks, ahead))
            down_blocks = resident(down_blocks)
        waiting.append((chunk, others_over(hidden, "head")))
        chunk = [half_ring] if last else [step, -step]
        blocks = [[ahead, behind]] if last else [[ahead], [behind]]
    exchanged = others_over(units_of(chunk, blocks), "head")
    parts.update(sums_of(*waiting.pop(0)))
    exchanged, parts = lax.optimization_barrier((exchanged, parts))
    parts.update(sums_of(chunk, exchanged))

    def late():
        own, arrived = waiting.pop(0)
        arrived, _ = lax.optimization_barrier((arrived, parts[half_ring]))
        return sums_of(own, arrived)

    weighted = ring_sum(parts, late)
    output = (mid_quarter.astype(jnp.float32) + weighted).astype(jnp.bfloat16)
    return output[None]


def solution(mesh):
    return jax.shard_map(
        on_device,
        mesh=mesh,
        in_specs=(
            P("grp", "tok", "head"),
            P(),
            P("grp", "head"),
            P("grp", "head"),
            P("grp", "head"),
            P("grp", "head"),
            P("grp", "tok", "head", None),
            P("grp", "tok", "head", None),
            P("grp", None),
            P(),
            P("grp", "tok", None),
            P("grp", "tok", None),
            P(("grp", "tok"), None, "head"),
            P(("grp", "tok"), None, "head"),
            P(("grp", "tok"), None, "head"),
        ),
        out_specs=P("grp", "tok", "head"),
        check_vma=False,
    )
```
